512 devices in a mesh: seq: 128 (over z, y, core), chan: 4 (over x).
Axes of the slice: x: 4, y: 8, z: 8, core: 2. Of those that a mesh axis runs over, the one named last changes fastest.
Arguments:
- tokens: bfloat16 [65536, 4096], P('seq', 'chan'), may hold values from -24 to 24
- grad_out: bfloat16 [65536, 4096], P('seq', 'chan'), may hold values from -0.09375 to 0.09375
- in_weight: bfloat16 [4096, 3, 256], P('seq', None, 'chan'), may hold values from -0.09375 to 0.09375
- out_weight: bfloat16 [4096, 256], P('seq', 'chan'), may hold values from -0.09375 to 0.09375
- conv_out: bfloat16 [65536, 256], P('seq', 'chan'), may hold values from -6 to 6
- residues: float32 [16, 128], P(None, 'chan'), may hold values from -1.5 to 1.5
- decay_length: float32 [16, 128], P(None, 'chan'), may hold values from 8 to 4194304
Outputs:
- grad_in_weight: float32 [4096, 3, 256], P('seq', None, 'chan')
- grad_out_weight: float32 [4096, 256], P('seq', 'chan')
The draws below stay inside these ranges and needn't reach their ends.
All inputs are finite; a program needn't handle non-finite values.
Results may differ from the reference program's by a relative error of at most 0.0041.
Values may be sent and summed in bfloat16 or wider, within the bound.
No kernel may reach another device: no remote copies, remote signals or barrier semaphores. Data moves between devices by JAX's collectives and lax.ppermute only.
A program may use at most 64 MiB of HBM per device.

```python
import math
import jax
import jax.numpy as jnp
from jax import lax

D = 4096
C = 256
MODES = 16
SEQ = 65536
FILTERS = 128


def strengthened(array, rng, source, target, blocks, factor):
    def block_of(position):
        return (jnp.arange(array.shape[position]) // (array.shape[position] // blocks)).reshape((-1,) + (1,) * (array.ndim - 1 - position))

    first = jax.random.permutation(rng, blocks)[block_of(target)]
    other_side = (block_of(target) + blocks // 2) % blocks
    return jnp.where((block_of(source) == first) | (block_of(source) == other_side), factor * array, array)


def steps_of(own_key, shape, split, smallest, top_value):
    loudness, own = 1.0, jax.random.fold_in(own_key, 6)
    for axis_at, blocks in split:
        draws = jnp.exp(jax.random.uniform(jax.random.fold_in(own, axis_at), (blocks,), jnp.float32, smallest / len(split), top_value / len(split)))
        loudness = loudness * jnp.repeat(draws, shape[axis_at] // blocks).reshape([-1 if axis == axis_at else 1 for axis in range(len(shape))])
    return loudness


def bell_draw(stream_key, dims, scale, bound, split=(), held_as=jnp.bfloat16):
    entries = scale * jax.random.normal(stream_key, dims, jnp.float32)
    if split:
        entries = entries * steps_of(stream_key, dims, split, -0.22, 0.18)
    return jnp.clip(entries, -bound, bound).astype(held_as)


def gaussian_with(rng, shape, deviation, most, split, heavy, dtype=jnp.bfloat16):
    array = deviation * jax.random.normal(rng, shape, jnp.float32)
    if split:
        array = array * steps_of(rng, shape, split, -0.22, 0.18)
    return jnp.clip(strengthened(array, jax.random.fold_in(rng, 3), *heavy), -most, most).astype(dtype)


def setup_inputs(seed: int = 0) -> dict:
    keys = jax.random.split(jax.random.key(seed), 8)
    return {
        "tokens": gaussian_with(keys[0], (SEQ, D), 1.0, 24.0, ((0, 128), (1, 4)), (0, 1, 128, 5.5)),
        "grad_out": gaussian_with(keys[1], (SEQ, D), SEQ ** -0.5, 0.09375, ((0, 128), (1, 4)), (0, 1, 128, 5.5)),
        "in_weight": bell_draw(keys[2], (D, 3, C), D ** -0.5, 0.09375, ((0, 128), (2, 4))),
        "out_weight": bell_draw(keys[3], (D, C), D ** -0.5, 0.09375, ((0, 128), (1, 4))),
        "conv_out": bell_draw(keys[4], (SEQ, C), 1.0, 6.0, ((0, 128), (1, 4))),
        "residues": bell_draw(keys[5], (MODES, FILTERS), MODES ** -0.5, 1.5, ((1, 4),), jnp.float32),
        "decay_length": jnp.clip(jnp.exp(math.log(4194304) - 13.169796 * jax.random.uniform(keys[6], (MODES, FILTERS), jnp.float32) ** steps_of(keys[6], (MODES, FILTERS), ((1, 4),), -0.2, 0.2)), 8.0, 4194304),
    }


def filter_taps(residues, decay_length):
    inverse_len = 1.0 / decay_length
    weight = residues * jnp.sqrt(-jnp.expm1(-2.0 * inverse_len))
    moments = jnp.arange(SEQ).astype(jnp.float32)

    def add_mode(running, inputs):
        mode_weight, mode_rate = inputs
        return (running + mode_weight[None, :] * jnp.exp(-moments[:, None] * mode_rate[None, :]), None)
    impulse, _ = lax.scan(add_mode, jnp.zeros((SEQ, FILTERS), jnp.float32), (weight, inverse_len))
    return impulse

def correlate(impulse, signal):
    paired = signal[:, 0::2] + 1j * signal[:, 1::2]
    spectrum = jnp.fft.fft(paired, n=2 * SEQ, axis=0)
    response = jnp.conj(jnp.fft.fft(impulse, n=2 * SEQ, axis=0))
    result = jnp.fft.ifft(spectrum * response, axis=0)[:SEQ]
    return jnp.stack([jnp.real(result), jnp.imag(result)], axis=2).reshape(SEQ, C)

def reference(tokens, grad_out, in_weight, out_weight, conv_out, residues, decay_length):
    projected = jnp.dot(tokens, in_weight.reshape(D, 3 * C), preferred_element_type=jnp.float32)
    streams = projected.astype(jnp.bfloat16).reshape(SEQ, 3, C)
    gate_first = streams[:, 0].astype(jnp.float32)
    gate_second = streams[:, 1].astype(jnp.float32)
    value_stream = streams[:, 2].astype(jnp.float32)
    conv_value = conv_out.astype(jnp.float32)
    gated = (gate_second * conv_value).astype(jnp.bfloat16)
    upstream = jnp.dot(grad_out, out_weight, preferred_element_type=jnp.float32)
    grad_second = (upstream * conv_value).astype(jnp.bfloat16)
    grad_conv = upstream * gate_second
    grad_source = correlate(filter_taps(residues, decay_length), grad_conv)
    grad_first = (grad_source * value_stream).astype(jnp.bfloat16)
    grad_value = (grad_source * gate_first).astype(jnp.bfloat16)
    grad_streams = jnp.stack([grad_first, grad_second, grad_value], axis=1).reshape(SEQ, 3 * C)
    grad_in = lax.dot_general(tokens, grad_streams, (((0,), (0,)), ((), ())), preferred_element_type=jnp.float32)
    grad_proj = lax.dot_general(grad_out, gated, (((0,), (0,)), ((), ())), preferred_element_type=jnp.float32)
    return (grad_in.reshape(D, 3, C), grad_proj)
```

```python
import jax
import jax.numpy as jnp
from jax import lax
from jax.experimental import pallas as pl
from jax.experimental.pallas import tpu as pltpu
from jax.sharding import Mesh
from jax.sharding import PartitionSpec as P

SEQ = ("seq_0", "seq_1", "seq_2")
CHIPS = ("seq_0", "seq_1")
STEPS = 64
MODE_ROWS = 4
GROUPS = 4
F32 = jnp.float32
BF16 = jnp.bfloat16
VMEM = 48 * 1024 * 1024


def call(body, out_shape, scratch=(), flops=0, moved=0):
    return pl.pallas_call(
        body,
        out_shape=out_shape,
        scratch_shapes=list(scratch),
        compiler_params=pltpu.CompilerParams(vmem_limit_bytes=VMEM),
        cost_estimate=pl.CostEstimate(flops=flops, bytes_accessed=moved, transcendentals=0),
    )


def lane_group(shape):
    lane = lax.broadcasted_iota(jnp.int32, shape, len(shape) - 1)
    return lane // 32


def turn(x, by):
    return pltpu.roll(x, by, x.ndim - 1)


def transpose_body(a_ref, b_ref, out_ref):
    half = a_ref.shape[0]
    out_ref[:, :half] = a_ref[...].T
    out_ref[:, half:] = b_ref[...].T


def project_body(own_t, other_t, own_g, other_g, w_ref, out_ref):
    half = own_t.shape[0]
    for at, (t_ref, g_ref) in enumerate(((own_t, own_g), (other_t, other_g))):
        for c in range(0, w_ref.shape[0], 2):
            w = jnp.concatenate([w_ref[c], w_ref[c + 1]], axis=1)
            from_t = jnp.dot(t_ref[...], w, preferred_element_type=F32)
            from_g = jnp.dot(g_ref[...], w, preferred_element_type=F32)
            both = jnp.where(lane_group(from_t.shape) % GROUPS < 3, from_t, from_g)
            out_ref[c, at * half : (at + 1) * half] = both[:, :128]
            out_ref[c + 1, at * half : (at + 1) * half] = both[:, 128:]


def signal_of(x):
    product = x * turn(x, 64)
    return jnp.where(lane_group(x.shape) % 2 == 1, product, turn(product, 32))


def chunk_rows(core, q_half, step, rows):
    half = rows // 2
    start = half * core if q_half == 0 else half * (1 - core)
    return pl.ds(start + step, half // STEPS, stride=STEPS)


def first_body(core_ref, part_ref, decay_ref, far_ref, x_ref, left_ref, state_ref, sig, st):
    core = core_ref[0]
    rows = x_ref.shape[0]
    total = part_ref[0]
    for k in range(1, part_ref.shape[0]):
        total = total + part_ref[k]
    rounded = total.astype(BF16).astype(F32)
    x = jnp.where(lane_group(total.shape) < 3, rounded, total)
    x_ref[...] = x
    sig[...] = signal_of(x)
    decay = [decay_ref[m : m + 1, :] for m in range(MODE_ROWS)]
    chunks = rows // STEPS
    per = chunks // 2

    def step(i, held):
        t = STEPS - 1 - i
        g = [sig[chunk_rows(core, h, t, rows), :] for h in range(2)]
        return tuple(
            decay[m] * held[2 * m + h] + g[h] for m in range(MODE_ROWS) for h in range(2)
        )

    zero = jnp.zeros((per, 128), F32)
    held = lax.fori_loop(0, STEPS, step, (zero,) * (2 * MODE_ROWS), unroll=8)
    for m in range(MODE_ROWS):
        for h in range(2):
            st[m * chunks + h * per : m * chunks + (h + 1) * per, :] = held[2 * m + h]
    far = far_ref[...]
    acc = jnp.zeros((MODE_ROWS, 128), F32)
    for q in reversed(range(chunks)):
        where = pl.ds(q, MODE_ROWS, stride=chunks)
        left_ref[where, :] = acc
        acc = st[where, :] + far * acc
    state_ref[...] = jnp.broadcast_to(acc[None], state_ref.shape)


def second_body(
    core_ref, x_ref, left_ref, states_ref, reach_ref, power_ref, decay_ref, weight_ref, conv_ref,
    out_ref, sig, ys,
):
    core = core_ref[0]
    rows = x_ref.shape[0]
    chunks = rows // STEPS
    per = chunks // 2
    sig[...] = signal_of(x_ref[...])
    carry = jnp.sum(states_ref[...] * reach_ref[...], axis=0)
    decay = [decay_ref[m : m + 1, :] for m in range(MODE_ROWS)]
    weight = [weight_ref[m : m + 1, :] for m in range(MODE_ROWS)]
    begin = []
    for m in range(MODE_ROWS):
        here = slice(m * chunks, (m + 1) * chunks)
        c = left_ref[here, :] + power_ref[here, :] * carry[m : m + 1, :]
        begin += [c[:per], c[per:]]

    def step(i, held):
        t = STEPS - 1 - i
        new = []
        for h in range(2):
            g = sig[chunk_rows(core, h, t, rows), :]
            states = [decay[m] * held[2 * m + h] + g for m in range(MODE_ROWS)]
            y = weight[0] * states[0]
            for m in range(1, MODE_ROWS):
                y = y + weight[m] * states[m]
            ys[chunk_rows(core, h, t, rows), :] = y
            new.append(states)
        return tuple(new[h][m] for m in range(MODE_ROWS) for h in range(2))

    lax.fori_loop(0, STEPS, step, tuple(begin), unroll=8)
    y = ys[...]
    y = y + turn(y, 64)
    y = y + turn(y, 32)
    factor = jnp.where(lane_group(y.shape) % 2 == 0, y, conv_ref[...].astype(F32))
    out = (turn(x_ref[...], 64) * factor).astype(BF16)
    for k in range(out_ref.shape[0]):
        out_ref[k] = out


def weigh_body(tt_ref, gt_ref, grads_ref, out_ref):
    depth = tt_ref.shape[0]
    block = 512
    for r in range(0, depth, block):
        for c in range(0, grads_ref.shape[0], 2):
            g = jnp.concatenate([grads_ref[c], grads_ref[c + 1]], axis=1)
            from_t = jnp.dot(tt_ref[r : r + block, :], g, preferred_element_type=F32)
            from_g = jnp.dot(gt_ref[r : r + block, :], g, preferred_element_type=F32)
            both = jnp.where(lane_group(from_t.shape) % GROUPS < 3, from_t, from_g).astype(BF16)
            out_ref[c, r : r + block] = both[:, :128]
            out_ref[c + 1, r : r + block] = both[:, 128:]


def by_lanes(table):
    wide = jnp.repeat(table, 2, axis=1)
    channels = wide.shape[1]
    return wide.reshape(GROUPS, MODE_ROWS, channels).transpose(1, 0, 2).reshape(MODE_ROWS, -1)


def local(tokens, grad_out, in_weight, out_weight, conv_out, residues, decay_length):
    half = tokens.shape[0]
    depth = tokens.shape[1]
    rows = 2 * half
    owned = in_weight.shape[0]
    channels = out_weight.shape[1]
    mine = channels // 2
    size_z, size_y, size_x = (lax.axis_size(a) for a in ("seq_0", "seq_1", "chan"))
    chips = size_z * size_y
    fold = size_z // size_x
    core = lax.axis_index("seq_2")
    place = lax.axis_index(CHIPS)

    def transposed(value, swap):
        pairs = []
        for z in range(size_z):
            for k in range(2):
                for x in range(size_x):
                    c, l = z // fold, z % fold
                    source = (z * 2 + k) * size_x + x
                    target = ((fold * x + l) * 2 + (1 - k if swap else k)) * size_x + c
                    pairs.append((source, target))
        return lax.ppermute(value, ("seq_0", "seq_2", "chan"), pairs)

    def swapped(value):
        return lax.ppermute(value, "seq_2", [(0, 1), (1, 0)])

    packed = jnp.concatenate([in_weight, out_weight[:, None, :]], axis=1)
    packed = packed.reshape(owned, GROUPS, 2, mine).transpose(2, 0, 1, 3).reshape(2, owned, 128)
    kept, given = (
        jnp.where(core == 0, packed[0], packed[1]),
        jnp.where(core == 0, packed[1], packed[0]),
    )
    kept = transposed(kept, False)
    given = transposed(given, True)
    low = jnp.where(core == 0, kept, given)
    high = jnp.where(core == 0, given, kept)
    piece = jnp.concatenate([low, high], axis=0)
    piece = jnp.broadcast_to(piece[None], (chips, 2 * owned, 128))
    weights = lax.all_to_all(piece, CHIPS, 0, 0, tiled=True).reshape(size_x, depth, 128)

    tokens_too = swapped(tokens)
    grads_too = swapped(grad_out)
    conv_own = jnp.where(core == 0, conv_out[:, :mine], conv_out[:, mine:])
    conv_sent = jnp.where(core == 0, conv_out[:, mine:], conv_out[:, :mine])
    conv = jnp.concatenate([conv_own, swapped(conv_sent)], axis=0)
    conv = jnp.tile(conv, (1, GROUPS))
    flip = call(
        transpose_body, jax.ShapeDtypeStruct((depth, rows), BF16), moved=4 * depth * rows
    )
    tokens_t = flip(tokens, tokens_too)
    grads_t = flip(grad_out, grads_too)

    pick = residues.shape[1] // 2
    res = jnp.where(core == 0, residues[:, :pick], residues[:, pick:])
    length = jnp.where(core == 0, decay_length[:, :pick], decay_length[:, pick:])
    rate_raw = 1.0 / length
    weight = by_lanes(res * jnp.sqrt(-jnp.expm1(-2.0 * rate_raw)))
    rate = by_lanes(rate_raw)
    decay = jnp.exp(-rate)
    far = jnp.exp(-float(STEPS) * rate)
    chunks = rows // STEPS
    left_of = (chunks - 1 - jnp.arange(chunks)).astype(F32) * float(STEPS)
    power = jnp.exp(-left_of[None, :, None] * rate[:, None, :]).reshape(-1, 128)
    ahead = jnp.arange(chips) - place - 1
    reach = jnp.where(
        (ahead >= 0)[:, None, None],
        jnp.exp(-(jnp.maximum(ahead, 0) * rows).astype(F32)[:, None, None] * rate[None]),
        0.0,
    )
    core_at = core.astype(jnp.int32).reshape(1)

    project = call(
        project_body,
        jax.ShapeDtypeStruct((size_x, rows, 128), F32),
        flops=4 * rows * depth * size_x * 128,
        moved=8 * rows * depth,
    )
    parts = project(tokens, tokens_too, grad_out, grads_too, weights)
    parts = lax.all_to_all(parts, "chan", 0, 0, tiled=True)

    smem = pl.BlockSpec(memory_space=pltpu.SMEM)
    full = pl.BlockSpec(memory_space=pltpu.VMEM)
    x, left, state = pl.pallas_call(
        first_body,
        out_shape=(
            jax.ShapeDtypeStruct((rows, 128), F32),
            jax.ShapeDtypeStruct((MODE_ROWS * chunks, 128), F32),
            jax.ShapeDtypeStruct((chips, MODE_ROWS, 128), F32),
        ),
        in_specs=[smem, full, full, full],
        out_specs=(full, full, full),
        scratch_shapes=[pltpu.VMEM((rows, 128), F32), pltpu.VMEM((MODE_ROWS * chunks, 128), F32)],
        compiler_params=pltpu.CompilerParams(vmem_limit_bytes=VMEM),
    )(core_at, parts, decay, far)
    states = lax.all_to_all(state, CHIPS, 0, 0, tiled=True)
    grads = pl.pallas_call(
        second_body,
        out_shape=jax.ShapeDtypeStruct((size_x, rows, 128), BF16),
        in_specs=[smem] + [full] * 8,
        out_specs=full,
        scratch_shapes=[pltpu.VMEM((rows, 128), F32), pltpu.VMEM((rows, 128), F32)],
        compiler_params=pltpu.CompilerParams(vmem_limit_bytes=VMEM),
    )(core_at, x, left, states, reach, power, decay, weight, conv)
    grads = lax.all_to_all(grads, "chan", 0, 0, tiled=True)

    weigh = call(
        weigh_body,
        jax.ShapeDtypeStruct((size_x, depth, 128), BF16),
        flops=4 * rows * depth * size_x * 128,
        moved=8 * rows * depth,
    )
    partial = weigh(tokens_t, grads_t, grads).reshape(chips, 2 * owned, 128)
    partial = lax.all_to_all(partial, CHIPS, 0, 0, tiled=True)
    total = jnp.sum(partial.astype(F32), axis=0)
    kept = transposed(jnp.where(core == 0, total[:owned], total[owned:]), False)
    given = transposed(jnp.where(core == 0, total[owned:], total[:owned]), True)
    low = jnp.where(core == 0, kept, given)
    high = jnp.where(core == 0, given, kept)
    result = jnp.stack([low, high]).reshape(2, owned, GROUPS, mine)
    result = result.transpose(1, 2, 0, 3).reshape(owned, GROUPS, channels)
    return (result[:, :3], result[:, 3])


def solution(mesh):
    finer = Mesh(
        mesh.devices.reshape(8, 8, 2, mesh.shape["chan"]), ("seq_0", "seq_1", "seq_2", "chan")
    )
    in_specs = (
        P(SEQ, "chan"),
        P(SEQ, "chan"),
        P(SEQ, None, "chan"),
        P(SEQ, "chan"),
        P(SEQ, "chan"),
        P(None, "chan"),
        P(None, "chan"),
    )
    out_specs = (P(SEQ, None, "chan"), P(SEQ, "chan"))
    return jax.shard_map(local, mesh=finer, in_specs=in_specs, out_specs=out_specs, check_vma=False)
```

```python
import jax
import jax.numpy as jnp
from jax import lax
from jax.experimental import pallas as pl
from jax.experimental.pallas import tpu as pltpu
from jax.sharding import Mesh
from jax.sharding import PartitionSpec as P

SEQ = ("seq_0", "seq_1", "seq_2")
CHIPS = ("seq_0", "seq_1")
STEPS = 64
MODE_ROWS = 4
GROUPS = 4
F32 = jnp.float32
BF16 = jnp.bfloat16
MIB = 1024 * 1024

OFFSETS = ((5, 4), (2, 3), (0, 1), (6, 7))


def call(body, out_shape, mib, scratch=(), flops=0, moved=0, inputs=None):
    specs = {}
    if inputs is not None:
        specs["in_specs"] = [pl.BlockSpec(memory_space=pltpu.SMEM)] + [
            pl.BlockSpec(memory_space=pltpu.VMEM)
        ] * (inputs - 1)
    return pl.pallas_call(
        body,
        out_shape=out_shape,
        scratch_shapes=list(scratch),
        compiler_params=pltpu.CompilerParams(vmem_limit_bytes=mib * MIB),
        cost_estimate=pl.CostEstimate(flops=flops, bytes_accessed=moved, transcendentals=0),
        **specs,
    )


def holder(plane, c, l):
    e = lax.rem(c + len(OFFSETS) - plane, len(OFFSETS))
    o = OFFSETS[0][l]
    for k in range(1, len(OFFSETS)):
        o = jnp.where(e == k, OFFSETS[k][l], o)
    return lax.rem(2 * plane + o, 2 * len(OFFSETS))


def lane_group(shape):
    lane = lax.broadcasted_iota(jnp.int32, shape, len(shape) - 1)
    return lane // 32


def turn(x, by):
    return pltpu.roll(x, by, x.ndim - 1)


def transpose_body(a_ref, b_ref, out_ref):
    half = a_ref.shape[0]
    out_ref[:, :half] = a_ref[...].T
    out_ref[:, half:] = b_ref[...].T


def pack_body(at_ref, in_ref, out_w_ref, kept_ref, given_ref):
    core = at_ref[0]
    width = out_w_ref.shape[1]
    row = lax.broadcasted_iota(jnp.int32, (width, 128), 0)
    lane = lax.broadcasted_iota(jnp.int32, (width, 128), 1)
    streams = [in_ref[0], in_ref[1], in_ref[2], out_w_ref[...]]
    for half, ref in ((core, kept_ref), (1 - core, given_ref)):
        total = jnp.zeros(ref.shape, F32)
        for s, w in enumerate(streams):
            chosen = (lane // 32 == s) & (row == half * 32 + lane % 32)
            total = total + jnp.dot(w, chosen.astype(F32).astype(BF16), preferred_element_type=F32)
        ref[...] = total.astype(BF16)


def spread_body(at_ref, kept_ref, given_ref, out_ref):
    first = at_ref[0] == 0
    kept = kept_ref[...].astype(F32)
    given = given_ref[...].astype(F32)
    low = jnp.where(first, kept, given)
    high = jnp.where(first, given, kept)
    piece = jnp.concatenate([low, high], axis=0).astype(BF16)
    for k in range(out_ref.shape[0]):
        out_ref[k] = piece


def total_body(at_ref, part_ref, kept_ref, given_ref):
    first = at_ref[0] == 0
    owned = kept_ref.shape[0]
    total = part_ref[0].astype(F32)
    for k in range(1, part_ref.shape[0]):
        total = total + part_ref[k].astype(F32)
    kept_ref[...] = jnp.where(first, total[:owned], total[owned:])
    given_ref[...] = jnp.where(first, total[owned:], total[:owned])


def unpack_body(at_ref, kept_ref, given_ref, in_ref, out_w_ref):
    first = at_ref[0] == 0
    low = jnp.where(first, kept_ref[...], given_ref[...])
    high = jnp.where(first, given_ref[...], kept_ref[...])
    for s in range(GROUPS):
        left = low if s == 0 else turn(low, 128 - 32 * s)
        right = high if s == 1 else turn(high, (160 - 32 * s) % 128)
        both = jnp.where(lane_group(low.shape) == 0, left, right)[:, : out_w_ref.shape[1]]
        if s < 3:
            in_ref[s] = both
        else:
            out_w_ref[...] = both


def project_body(at_ref, own_t, other_t, own_g, other_g, w_ref, out_ref):
    half = own_t.shape[0]
    plane = at_ref[1]

    def columns(c):
        return jnp.concatenate([w_ref[holder(plane, c, l)] for l in range(2)], axis=0)

    for c in range(0, out_ref.shape[0], 2):
        w = jnp.concatenate([columns(c), columns(c + 1)], axis=1)
        for at, (t_ref, g_ref) in enumerate(((own_t, own_g), (other_t, other_g))):
            from_t = jnp.dot(t_ref[...], w, preferred_element_type=F32)
            from_g = jnp.dot(g_ref[...], w, preferred_element_type=F32)
            both = jnp.where(lane_group(from_t.shape) % GROUPS < 3, from_t, from_g)
            out_ref[c, at * half : (at + 1) * half] = both[:, :128]
            out_ref[c + 1, at * half : (at + 1) * half] = both[:, 128:]


def signal_of(x):
    product = x * turn(x, 64)
    return jnp.where(lane_group(x.shape) % 2 == 1, product, turn(product, 32))


def chunk_rows(core, q_half, step, rows):
    half = rows // 2
    start = half * core if q_half == 0 else half * (1 - core)
    return pl.ds(start + step, half // STEPS, stride=STEPS)


def first_body(at_ref, part_ref, decay_ref, far_ref, x_ref, left_ref, state_ref, sig, st):
    core = at_ref[0]
    rows = x_ref.shape[0]
    total = part_ref[0]
    for k in range(1, part_ref.shape[0]):
        total = total + part_ref[k]
    rounded = total.astype(BF16).astype(F32)
    x = jnp.where(lane_group(total.shape) < 3, rounded, total)
    x_ref[...] = x
    sig[...] = signal_of(x)
    decay = [decay_ref[m : m + 1, :] for m in range(MODE_ROWS)]
    chunks = rows // STEPS
    per = chunks // 2

    def step(i, held):
        t = STEPS - 1 - i
        g = [sig[chunk_rows(core, h, t, rows), :] for h in range(2)]
        return tuple(
            decay[m] * held[2 * m + h] + g[h] for m in range(MODE_ROWS) for h in range(2)
        )

    zero = jnp.zeros((per, 128), F32)
    held = lax.fori_loop(0, STEPS, step, (zero,) * (2 * MODE_ROWS), unroll=8)
    for m in range(MODE_ROWS):
        for h in range(2):
            st[m * chunks + h * per : m * chunks + (h + 1) * per, :] = held[2 * m + h]
    far = far_ref[...]
    acc = jnp.zeros((MODE_ROWS, 128), F32)
    for q in reversed(range(chunks)):
        where = pl.ds(q, MODE_ROWS, stride=chunks)
        left_ref[where, :] = acc
        acc = st[where, :] + far * acc
    state_ref[...] = jnp.broadcast_to(acc[None], state_ref.shape)


def second_body(
    at_ref, x_ref, left_ref, states_ref, reach_ref, power_ref, decay_ref, weight_ref, conv_ref,
    out_ref, sig, ys,
):
    core = at_ref[0]
    rows = x_ref.shape[0]
    chunks = rows // STEPS
    per = chunks // 2
    sig[...] = signal_of(x_ref[...])
    carry = jnp.sum(states_ref[...] * reach_ref[...], axis=0)
    decay = [decay_ref[m : m + 1, :] for m in range(MODE_ROWS)]
    weight = [weight_ref[m : m + 1, :] for m in range(MODE_ROWS)]
    begin = []
    for m in range(MODE_ROWS):
        here = slice(m * chunks, (m + 1) * chunks)
        c = left_ref[here, :] + power_ref[here, :] * carry[m : m + 1, :]
        begin += [c[:per], c[per:]]

    def step(i, held):
        t = STEPS - 1 - i
        new = []
        for h in range(2):
            g = sig[chunk_rows(core, h, t, rows), :]
            states = [decay[m] * held[2 * m + h] + g for m in range(MODE_ROWS)]
            y = weight[0] * states[0]
            for m in range(1, MODE_ROWS):
                y = y + weight[m] * states[m]
            ys[chunk_rows(core, h, t, rows), :] = y
            new.append(states)
        return tuple(new[h][m] for m in range(MODE_ROWS) for h in range(2))

    lax.fori_loop(0, STEPS, step, tuple(begin), unroll=8)
    y = ys[...]
    y = y + turn(y, 64)
    y = y + turn(y, 32)
    factor = jnp.where(lane_group(y.shape) % 2 == 0, y, conv_ref[...].astype(F32))
    out = (turn(x_ref[...], 64) * factor).astype(BF16)
    for k in range(out_ref.shape[0]):
        out_ref[k] = out


def weigh_body(at_ref, tt_ref, gt_ref, grads_ref, out_ref):
    plane = at_ref[1]
    block = out_ref.shape[1]
    for l in range(2):
        r = l * block
        for c in range(0, grads_ref.shape[0], 2):
            g = jnp.concatenate([grads_ref[c], grads_ref[c + 1]], axis=1)
            from_t = jnp.dot(tt_ref[r : r + block, :], g, preferred_element_type=F32)
            from_g = jnp.dot(gt_ref[r : r + block, :], g, preferred_element_type=F32)
            both = jnp.where(lane_group(from_t.shape) % GROUPS < 3, from_t, from_g).astype(BF16)
            out_ref[holder(plane, c, l)] = both[:, :128]
            out_ref[holder(plane, c + 1, l)] = both[:, 128:]


def by_lanes(table):
    wide = jnp.repeat(table, 2, axis=1)
    channels = wide.shape[1]
    return wide.reshape(GROUPS, MODE_ROWS, channels).transpose(1, 0, 2).reshape(MODE_ROWS, -1)


def local(tokens, grad_out, in_weight, out_weight, conv_out, residues, decay_length):
    half = tokens.shape[0]
    depth = tokens.shape[1]
    rows = 2 * half
    owned = in_weight.shape[0]
    channels = out_weight.shape[1]
    mine = channels // 2
    size_z, size_y, size_x = (lax.axis_size(a) for a in ("seq_0", "seq_1", "chan"))
    chips = size_z * size_y
    core = lax.axis_index("seq_2")
    place = lax.axis_index(CHIPS)

    at = jnp.stack([core, lax.axis_index("chan")]).astype(jnp.int32)

    def transposed(value, swap, to_owner):
        pairs = []
        for z in range(size_z):
            for k in range(2):
                for x in range(size_x):
                    j, l = z // 2, z % 2
                    held_z = (2 * j + OFFSETS[(x - j) % size_x][l]) % size_z
                    owner = (z * 2 + k) * size_x + x
                    held = (held_z * 2 + (1 - k if swap else k)) * size_x + j
                    pairs.append((held, owner) if to_owner else (owner, held))
        return lax.ppermute(value, ("seq_0", "seq_2", "chan"), pairs)

    def swapped(value):
        return lax.ppermute(value, "seq_2", [(0, 1), (1, 0)])

    piece = jax.ShapeDtypeStruct((owned, 128), BF16)
    kept, given = call(pack_body, (piece, piece), 4, inputs=3)(
        at, in_weight.transpose(1, 0, 2), out_weight
    )
    kept = transposed(kept, False, False)
    given = transposed(given, True, False)
    spread = call(
        spread_body, jax.ShapeDtypeStruct((chips, 2 * owned, 128), BF16), 4, inputs=3
    )(at, kept, given)
    weights = lax.all_to_all(spread, CHIPS, 0, 0, tiled=True).reshape(size_z, -1, 128)

    tokens_too = swapped(tokens)
    grads_too = swapped(grad_out)
    conv_own = jnp.where(core == 0, conv_out[:, :mine], conv_out[:, mine:])
    conv_sent = jnp.where(core == 0, conv_out[:, mine:], conv_out[:, :mine])
    conv = jnp.concatenate([conv_own, swapped(conv_sent)], axis=0)
    conv = jnp.tile(conv, (1, GROUPS))
    flip = call(
        transpose_body, jax.ShapeDtypeStruct((depth, rows), BF16), 8, moved=4 * depth * rows
    )
    tokens_t = flip(tokens, tokens_too)
    grads_t = flip(grad_out, grads_too)

    pick = residues.shape[1] // 2
    res = jnp.where(core == 0, residues[:, :pick], residues[:, pick:])
    length = jnp.where(core == 0, decay_length[:, :pick], decay_length[:, pick:])
    rate_raw = 1.0 / length
    weight = by_lanes(res * jnp.sqrt(-jnp.expm1(-2.0 * rate_raw)))
    rate = by_lanes(rate_raw)
    decay = jnp.exp(-rate)
    far = jnp.exp(-float(STEPS) * rate)
    chunks = rows // STEPS
    left_of = (chunks - 1 - jnp.arange(chunks)).astype(F32) * float(STEPS)
    power = jnp.exp(-left_of[None, :, None] * rate[:, None, :]).reshape(-1, 128)
    ahead = jnp.arange(chips) - place - 1
    reach = jnp.where(
        (ahead >= 0)[:, None, None],
        jnp.exp(-(jnp.maximum(ahead, 0) * rows).astype(F32)[:, None, None] * rate[None]),
        0.0,
    )

    project = call(
        project_body,
        jax.ShapeDtypeStruct((size_x, rows, 128), F32),
        48,
        inputs=6,
        flops=4 * rows * depth * size_x * 128,
        moved=8 * rows * depth,
    )
    weights, tokens_t, grads_t = lax.optimization_barrier((weights, tokens_t, grads_t))
    parts = project(at, tokens, tokens_too, grad_out, grads_too, weights)
    parts = lax.all_to_all(parts, "chan", 0, 0, tiled=True)

    first = call(
        first_body,
        (
            jax.ShapeDtypeStruct((rows, 128), F32),
            jax.ShapeDtypeStruct((MODE_ROWS * chunks, 128), F32),
            jax.ShapeDtypeStruct((chips, MODE_ROWS, 128), F32),
        ),
        10,
        scratch=[pltpu.VMEM((rows, 128), F32), pltpu.VMEM((MODE_ROWS * chunks, 128), F32)],
        inputs=4,
    )
    x, left, state = first(at, parts, decay, far)
    states = lax.all_to_all(state, CHIPS, 0, 0, tiled=True)
    second = call(
        second_body,
        jax.ShapeDtypeStruct((size_x, rows, 128), BF16),
        10,
        scratch=[pltpu.VMEM((rows, 128), F32), pltpu.VMEM((rows, 128), F32)],
        inputs=9,
    )
    grads = second(at, x, left, states, reach, power, decay, weight, conv)
    grads = lax.all_to_all(grads, "chan", 0, 0, tiled=True)

    weigh = call(
        weigh_body,
        jax.ShapeDtypeStruct((size_z, depth // 2, 128), BF16),
        16,
        inputs=4,
        flops=4 * rows * depth * size_x * 128,
        moved=8 * rows * depth,
    )
    partial = weigh(at, tokens_t, grads_t, grads).reshape(chips, 2 * owned, 128)
    partial = lax.all_to_all(partial, CHIPS, 0, 0, tiled=True)
    piece = jax.ShapeDtypeStruct((owned, 128), F32)
    kept, given = call(total_body, (piece, piece), 6, inputs=2)(at, partial)
    kept = transposed(kept, False, True)
    given = transposed(given, True, True)
    grad_in, grad_proj = call(
        unpack_body,
        (
            jax.ShapeDtypeStruct((3, owned, channels), F32),
            jax.ShapeDtypeStruct((owned, channels), F32),
        ),
        4,
        inputs=3,
    )(at, kept, given)
    return (grad_in.transpose(1, 0, 2), grad_proj)


def solution(mesh):
    finer = Mesh(
        mesh.devices.reshape(8, 8, 2, mesh.shape["chan"]), ("seq_0", "seq_1", "seq_2", "chan")
    )
    in_specs = (
        P(SEQ, "chan"),
        P(SEQ, "chan"),
        P(SEQ, None, "chan"),
        P(SEQ, "chan"),
        P(SEQ, "chan"),
        P(None, "chan"),
        P(None, "chan"),
    )
    out_specs = (P(SEQ, None, "chan"), P(SEQ, "chan"))
    return jax.shard_map(local, mesh=finer, in_specs=in_specs, out_specs=out_specs, check_vma=False)
```

```python
import jax
import jax.numpy as jnp
from jax import lax
from jax.experimental import pallas as pl
from jax.experimental.pallas import tpu as pltpu
from jax.sharding import Mesh
from jax.sharding import PartitionSpec as P

SEQ = ("seq_0", "seq_1", "seq_2")
CHIPS = ("seq_0", "seq_1")
STEPS = 64
MODE_ROWS = 4
GROUPS = 4
F32 = jnp.float32
BF16 = jnp.bfloat16
MIB = 1024 * 1024

OFFSETS = ((5, 4), (2, 3), (0, 1), (6, 7))


def call(body, out_shape, mib, scratch=(), flops=0, moved=0, inputs=None):
    specs = {}
    if inputs is not None:
        specs["in_specs"] = [pl.BlockSpec(memory_space=pltpu.SMEM)] + [
            pl.BlockSpec(memory_space=pltpu.VMEM)
        ] * (inputs - 1)
    return pl.pallas_call(
        body,
        out_shape=out_shape,
        scratch_shapes=list(scratch),
        compiler_params=pltpu.CompilerParams(vmem_limit_bytes=mib * MIB),
        cost_estimate=pl.CostEstimate(flops=flops, bytes_accessed=moved, transcendentals=0),
        **specs,
    )


def holder(plane, e, l):
    return lax.rem(2 * plane + OFFSETS[e][l], 2 * len(OFFSETS))


def chunk_of(plane, e):
    return lax.rem(plane + e, len(OFFSETS))


def in_hbm(x):
    return pltpu.with_memory_space_constraint(x, pltpu.HBM)


def lane_group(shape):
    lane = lax.broadcasted_iota(jnp.int32, shape, len(shape) - 1)
    return lane // 32


def turn(x, by):
    return pltpu.roll(x, by, x.ndim - 1)


def transpose_body(a_ref, b_ref, out_ref):
    half = a_ref.shape[0]
    out_ref[:, :half] = a_ref[...].T
    out_ref[:, half:] = b_ref[...].T


def pack_body(at_ref, in_ref, out_w_ref, kept_ref, given_ref):
    core = at_ref[0]
    width = out_w_ref.shape[1]
    row = lax.broadcasted_iota(jnp.int32, (width, 128), 0)
    lane = lax.broadcasted_iota(jnp.int32, (width, 128), 1)
    streams = [in_ref[0], in_ref[1], in_ref[2], out_w_ref[...]]
    for half, ref in ((core, kept_ref), (1 - core, given_ref)):
        total = jnp.zeros(ref.shape, F32)
        for s, w in enumerate(streams):
            chosen = (lane // 32 == s) & (row == half * 32 + lane % 32)
            total = total + jnp.dot(w, chosen.astype(F32).astype(BF16), preferred_element_type=F32)
        ref[...] = total.astype(BF16)


def spread_body(at_ref, kept_ref, given_ref, out_ref):
    first = at_ref[0] == 0
    kept = kept_ref[...].astype(F32)
    given = given_ref[...].astype(F32)
    low = jnp.where(first, kept, given)
    high = jnp.where(first, given, kept)
    piece = jnp.concatenate([low, high], axis=0).astype(BF16)
    for k in range(out_ref.shape[0]):
        out_ref[k] = piece


def total_body(at_ref, part_ref, kept_ref, given_ref):
    first = at_ref[0] == 0
    owned = kept_ref.shape[0]
    total = part_ref[0].astype(F32)
    for k in range(1, part_ref.shape[0]):
        total = total + part_ref[k].astype(F32)
    kept_ref[...] = jnp.where(first, total[:owned], total[owned:])
    given_ref[...] = jnp.where(first, total[owned:], total[:owned])


def unpack_body(at_ref, kept_ref, given_ref, in_ref, out_w_ref):
    first = at_ref[0] == 0
    low = jnp.where(first, kept_ref[...], given_ref[...])
    high = jnp.where(first, given_ref[...], kept_ref[...])
    for s, group in enumerate((0, 3, 2, 1)):
        left = low if group == 0 else turn(low, 128 - 32 * group)
        right = high if group == 1 else turn(high, (160 - 32 * group) % 128)
        both = jnp.where(lane_group(low.shape) == 0, left, right)[:, : out_w_ref.shape[1]]
        if s < 3:
            in_ref[s] = both
        else:
            out_w_ref[...] = both


def project_body(at_ref, own_t, other_t, own_g, other_g, w_ref, out_ref, late_ref):
    plane = at_ref[1]
    half = own_t.shape[0]

    def columns(e):
        return jnp.concatenate([w_ref[holder(plane, e, l)] for l in range(2)], axis=0)

    for e in range(0, out_ref.shape[0], 2):
        w = jnp.concatenate([columns(e), columns(e + 1)], axis=1)
        both = []
        for t_ref, g_ref in ((own_t, own_g), (other_t, other_g)):
            from_t = jnp.dot(t_ref[...], w, preferred_element_type=F32)
            from_g = jnp.dot(g_ref[...], w, preferred_element_type=F32)
            both.append(jnp.where(lane_group(from_t.shape) % GROUPS < 3, from_t, from_g))
        for k in range(2):
            own, other = (b[:, 128 * k : 128 * (k + 1)] for b in both)
            odd = lane_group(own.shape) % 2 == 1
            chunk = chunk_of(plane, e + k)
            early = jnp.where(odd, own, turn(other, 96))
            high = early.astype(BF16)
            late = jnp.where(odd, turn(other, 32), own)
            out_ref[chunk, :half] = high
            out_ref[chunk, half : 2 * half] = (early - high.astype(F32)).astype(BF16)
            out_ref[chunk, 2 * half :] = late.astype(BF16)
            if e + k == 0:
                late_ref[...] = late


def store_signal(x, sig):
    half = x.shape[0]
    product = x * turn(x, 64)
    turned = turn(product, 32)
    odd = lane_group(x.shape) % 2 == 1
    sig[:half] = jnp.where(odd, product, turned)
    sig[half:] = jnp.where(odd, turned, product)


def chunk_rows(core, q_half, step, rows):
    half = rows // 2
    start = half * core if q_half == 0 else half * (1 - core)
    return pl.ds(start + step, half // STEPS, stride=STEPS)


def first_body(
    at_ref, part_ref, own_late_ref, decay_ref, far_ref, x_ref, late_ref, left_ref, state_ref, sig, st
):
    core = at_ref[0]
    rows = sig.shape[0]
    half = rows // 2
    total = jnp.zeros(x_ref.shape, F32)
    late = own_late_ref[...]
    for k in range(part_ref.shape[0]):
        total = total + (part_ref[k, :half].astype(F32) + part_ref[k, half : 2 * half].astype(F32))
        late = late + jnp.where(at_ref[1] == k, 0.0, part_ref[k, 2 * half :].astype(F32))
    late_ref[...] = late.astype(BF16).astype(F32)
    rounded = total.astype(BF16).astype(F32)
    x = jnp.where(lane_group(total.shape) < 2, rounded, total)
    x_ref[...] = x
    store_signal(x, sig)
    decay = [decay_ref[m : m + 1, :] for m in range(MODE_ROWS)]
    chunks = rows // STEPS
    per = chunks // 2

    def step(i, held):
        t = STEPS - 1 - i
        g = [sig[chunk_rows(core, h, t, rows), :] for h in range(2)]
        return tuple(
            decay[m] * held[2 * m + h] + g[h] for m in range(MODE_ROWS) for h in range(2)
        )

    zero = jnp.zeros((per, 128), F32)
    held = lax.fori_loop(0, STEPS, step, (zero,) * (2 * MODE_ROWS), unroll=8)
    for m in range(MODE_ROWS):
        for h in range(2):
            st[m * chunks + h * per : m * chunks + (h + 1) * per, :] = held[2 * m + h]
    far = far_ref[...]
    acc = jnp.zeros((MODE_ROWS, 128), F32)
    for q in reversed(range(chunks)):
        where = pl.ds(q, MODE_ROWS, stride=chunks)
        left_ref[where, :] = acc
        acc = st[where, :] + far * acc
    state_ref[...] = jnp.broadcast_to(acc[None], state_ref.shape)


def second_body(
    at_ref, x_ref, late_ref, left_ref, states_ref, reach_ref, power_ref, decay_ref, weight_ref,
    conv_ref, out_ref, sig, ys,
):
    core = at_ref[0]
    rows = sig.shape[0]
    half = rows // 2
    chunks = rows // STEPS
    per = chunks // 2
    store_signal(x_ref[...], sig)
    carry = jnp.sum(states_ref[...] * reach_ref[...], axis=0)
    decay = [decay_ref[m : m + 1, :] for m in range(MODE_ROWS)]
    weight = [weight_ref[m : m + 1, :] for m in range(MODE_ROWS)]
    begin = []
    for m in range(MODE_ROWS):
        here = slice(m * chunks, (m + 1) * chunks)
        c = left_ref[here, :] + power_ref[here, :] * carry[m : m + 1, :]
        begin += [c[:per], c[per:]]

    def step(i, held):
        t = STEPS - 1 - i
        new = []
        for h in range(2):
            g = sig[chunk_rows(core, h, t, rows), :]
            states = [decay[m] * held[2 * m + h] + g for m in range(MODE_ROWS)]
            y = weight[0] * states[0]
            for m in range(1, MODE_ROWS):
                y = y + weight[m] * states[m]
            ys[chunk_rows(core, h, t, rows), :] = y
            new.append(states)
        return tuple(new[h][m] for m in range(MODE_ROWS) for h in range(2))

    lax.fori_loop(0, STEPS, step, tuple(begin), unroll=8)
    y = ys[...]
    y = y + turn(y, 64)
    y = y + turn(y, 32)
    odd = lane_group((half, 128)) % 2 == 1
    late = turn(late_ref[...], 64) * jnp.where(odd, y[half:], y[:half])
    early = x_ref[...] * conv_ref[...].astype(F32)
    own = jnp.where(odd, early, late)
    other = turn(jnp.where(odd, late, turn(early, 64)), 96)
    out = jnp.concatenate([own, other], axis=0).astype(BF16)
    for k in range(out_ref.shape[0]):
        out_ref[k] = out


def weigh_body(at_ref, tt_ref, gt_ref, grads_ref, out_ref):
    plane = at_ref[1]
    block = out_ref.shape[1]
    for l in range(2):
        r = l * block
        for c in range(0, grads_ref.shape[0], 2):
            g = jnp.concatenate([grads_ref[chunk_of(plane, c + k)] for k in range(2)], axis=1)
            from_t = jnp.dot(tt_ref[r : r + block, :], g, preferred_element_type=F32)
            from_g = jnp.dot(gt_ref[r : r + block, :], g, preferred_element_type=F32)
            both = jnp.where(lane_group(from_t.shape) % GROUPS != 1, from_t, from_g).astype(BF16)
            out_ref[holder(plane, c, l)] = both[:, :128]
            out_ref[holder(plane, c + 1, l)] = both[:, 128:]


def by_lanes(table):
    wide = jnp.repeat(table, 2, axis=1)
    channels = wide.shape[1]
    return wide.reshape(GROUPS, MODE_ROWS, channels).transpose(1, 0, 2).reshape(MODE_ROWS, -1)


def local(tokens, grad_out, in_weight, out_weight, conv_out, residues, decay_length):
    half = tokens.shape[0]
    depth = tokens.shape[1]
    rows = 2 * half
    owned = in_weight.shape[0]
    channels = out_weight.shape[1]
    mine = channels // 2
    size_z, size_y, size_x = (lax.axis_size(a) for a in ("seq_0", "seq_1", "chan"))
    chips = size_z * size_y
    core = lax.axis_index("seq_2")
    place = lax.axis_index(CHIPS)

    at = jnp.stack([core, lax.axis_index("chan")]).astype(jnp.int32)

    def transposed(value, swap, to_owner):
        pairs = []
        for z in range(size_z):
            for k in range(2):
                for x in range(size_x):
                    j, l = z // 2, z % 2
                    held_z = (2 * j + OFFSETS[(x - j) % size_x][l]) % size_z
                    owner = (z * 2 + k) * size_x + x
                    held = (held_z * 2 + (1 - k if swap else k)) * size_x + j
                    pairs.append((held, owner) if to_owner else (owner, held))
        return lax.ppermute(value, ("seq_0", "seq_2", "chan"), pairs)

    def swapped(value):
        return lax.ppermute(value, "seq_2", [(0, 1), (1, 0)])

    piece = jax.ShapeDtypeStruct((owned, 128), BF16)
    kept, given = call(pack_body, (piece, piece), 4, inputs=3)(
        at, in_hbm(in_weight.transpose(1, 0, 2)), in_hbm(out_weight)
    )
    kept = transposed(kept, False, False)
    given = transposed(given, True, False)
    tokens_too = swapped(tokens)
    grads_too = swapped(grad_out)
    kept, given, tokens_too, grads_too = lax.optimization_barrier(
        (kept, given, tokens_too, grads_too)
    )
    spread = call(
        spread_body, jax.ShapeDtypeStruct((chips, 2 * owned, 128), BF16), 4, inputs=3
    )(at, kept, given)
    weights = lax.all_to_all(spread, CHIPS, 0, 0, tiled=True).reshape(size_z, -1, 128)


    conv_own = jnp.where(core == 0, conv_out[:, :mine], conv_out[:, mine:])
    conv_sent = jnp.where(core == 0, conv_out[:, mine:], conv_out[:, :mine])
    conv = jnp.concatenate([swapped(conv_sent), conv_own], axis=1)
    conv = jnp.tile(conv, (1, 2))
    flip = call(
        transpose_body, jax.ShapeDtypeStruct((depth, rows), BF16), 8, moved=4 * depth * rows
    )
    tokens_t = flip(tokens, tokens_too)
    grads_t = flip(grad_out, grads_too)

    pick = residues.shape[1] // 2
    res = jnp.where(core == 0, residues[:, :pick], residues[:, pick:])
    length = jnp.where(core == 0, decay_length[:, :pick], decay_length[:, pick:])
    rate_raw = 1.0 / length
    weight = by_lanes(res * jnp.sqrt(-jnp.expm1(-2.0 * rate_raw)))
    rate = by_lanes(rate_raw)
    decay = jnp.exp(-rate)
    far = jnp.exp(-float(STEPS) * rate)
    chunks = rows // STEPS
    left_of = (chunks - 1 - jnp.arange(chunks)).astype(F32) * float(STEPS)
    power = jnp.exp(-left_of[None, :, None] * rate[:, None, :]).reshape(-1, 128)
    ahead = jnp.arange(chips) - place - 1
    reach = jnp.where(
        (ahead >= 0)[:, None, None],
        jnp.exp(-(jnp.maximum(ahead, 0) * rows).astype(F32)[:, None, None] * rate[None]),
        0.0,
    )

    project = call(
        project_body,
        (pltpu.HBM((size_x, 3 * half, 128), BF16), jax.ShapeDtypeStruct((half, 128), F32)),
        48,
        inputs=6,
        flops=4 * rows * depth * size_x * 128,
        moved=8 * rows * depth,
    )
    weights, tokens_t, grads_t = lax.optimization_barrier((weights, tokens_t, grads_t))
    parts, own_late = project(
        at, in_hbm(tokens), in_hbm(tokens_too), in_hbm(grad_out), in_hbm(grads_too), weights
    )
    parts = lax.all_to_all(parts, "chan", 0, 0, tiled=True)

    first = call(
        first_body,
        (
            jax.ShapeDtypeStruct((half, 128), F32),
            jax.ShapeDtypeStruct((half, 128), F32),
            jax.ShapeDtypeStruct((MODE_ROWS * chunks, 128), F32),
            jax.ShapeDtypeStruct((chips, MODE_ROWS, 128), F32),
        ),
        10,
        scratch=[pltpu.VMEM((rows, 128), F32), pltpu.VMEM((MODE_ROWS * chunks, 128), F32)],
        inputs=5,
    )
    x, late, left, state = first(at, parts, own_late, decay, far)
    states = lax.all_to_all(state, CHIPS, 0, 0, tiled=True)
    second = call(
        second_body,
        jax.ShapeDtypeStruct((size_x, rows, 128), BF16),
        10,
        scratch=[pltpu.VMEM((rows, 128), F32), pltpu.VMEM((rows, 128), F32)],
        inputs=10,
    )
    grads = second(at, x, late, left, states, reach, power, decay, weight, conv)
    grads = lax.all_to_all(grads, "chan", 0, 0, tiled=True)

    weigh = call(
        weigh_body,
        jax.ShapeDtypeStruct((size_z, depth // 2, 128), BF16),
        16,
        inputs=4,
        flops=4 * rows * depth * size_x * 128,
        moved=8 * rows * depth,
    )
    partial = weigh(at, tokens_t, grads_t, grads).reshape(chips, 2 * owned, 128)
    partial = lax.all_to_all(partial, CHIPS, 0, 0, tiled=True)
    piece = jax.ShapeDtypeStruct((owned, 128), F32)
    kept, given = call(total_body, (piece, piece), 6, inputs=2)(at, partial)
    kept = transposed(kept, False, True)
    given = transposed(given, True, True)
    grad_in, grad_proj = call(
        unpack_body,
        (
            jax.ShapeDtypeStruct((3, owned, channels), F32),
            jax.ShapeDtypeStruct((owned, channels), F32),
        ),
        4,
        inputs=3,
    )(at, kept, given)
    return (grad_in.transpose(1, 0, 2), grad_proj)


def solution(mesh):
    finer = Mesh(
        mesh.devices.reshape(8, 8, 2, mesh.shape["chan"]), ("seq_0", "seq_1", "seq_2", "chan")
    )
    in_specs = (
        P(SEQ, "chan"),
        P(SEQ, "chan"),
        P(SEQ, None, "chan"),
        P(SEQ, "chan"),
        P(SEQ, "chan"),
        P(None, "chan"),
        P(None, "chan"),
    )
    out_specs = (P(SEQ, None, "chan"), P(SEQ, "chan"))
    return jax.shard_map(local, mesh=finer, in_specs=in_specs, out_specs=out_specs, check_vma=False)
```

```python
import jax
import jax.numpy as jnp
from jax import lax
from jax.experimental import pallas as pl
from jax.experimental.pallas import tpu as pltpu
from jax.sharding import Mesh
from jax.sharding import PartitionSpec as P

SEQ = ("seq_0", "seq_1", "seq_2")
CHIPS = ("seq_0", "seq_1")
STEPS = 64
MODE_ROWS = 4
GROUPS = 4
F32 = jnp.float32
BF16 = jnp.bfloat16
MIB = 1024 * 1024

OFFSETS = ((5, 4), (2, 3), (0, 1), (6, 7))


def call(body, out_shape, mib, scratch=(), flops=0, moved=0, inputs=None):
    specs = {}
    if inputs is not None:
        specs["in_specs"] = [pl.BlockSpec(memory_space=pltpu.SMEM)] + [
            pl.BlockSpec(memory_space=pltpu.VMEM)
        ] * (inputs - 1)
    return pl.pallas_call(
        body,
        out_shape=out_shape,
        scratch_shapes=list(scratch),
        compiler_params=pltpu.CompilerParams(vmem_limit_bytes=mib * MIB),
        cost_estimate=pl.CostEstimate(flops=flops, bytes_accessed=moved, transcendentals=0),
        **specs,
    )


def holder(plane, e, l):
    return lax.rem(2 * plane + OFFSETS[e][l], 2 * len(OFFSETS))


def chunk_of(plane, e):
    return lax.rem(plane + e, len(OFFSETS))


def in_hbm(x):
    return pltpu.with_memory_space_constraint(x, pltpu.HBM)


def lane_group(shape):
    lane = lax.broadcasted_iota(jnp.int32, shape, len(shape) - 1)
    return lane // 32


def turn(x, by):
    return pltpu.roll(x, by, x.ndim - 1)


def transpose_body(a_ref, b_ref, out_ref):
    half = a_ref.shape[0]
    out_ref[:, :half] = a_ref[...].T
    out_ref[:, half:] = b_ref[...].T


def pack_body(at_ref, in_ref, out_w_ref, kept_ref, given_ref):
    core = at_ref[0]
    width = out_w_ref.shape[1]
    row = lax.broadcasted_iota(jnp.int32, (width, 128), 0)
    lane = lax.broadcasted_iota(jnp.int32, (width, 128), 1)
    streams = [in_ref[0], in_ref[1], in_ref[2], out_w_ref[...]]
    for half, ref in ((core, kept_ref), (1 - core, given_ref)):
        total = jnp.zeros(ref.shape, F32)
        for s, w in enumerate(streams):
            chosen = (lane // 32 == s) & (row == half * 32 + lane % 32)
            total = total + jnp.dot(w, chosen.astype(F32).astype(BF16), preferred_element_type=F32)
        ref[...] = total.astype(BF16)


def spread_body(at_ref, kept_ref, given_ref, out_ref):
    first = at_ref[0] == 0
    kept = kept_ref[...].astype(F32)
    given = given_ref[...].astype(F32)
    low = jnp.where(first, kept, given)
    high = jnp.where(first, given, kept)
    piece = jnp.concatenate([low, high], axis=0).astype(BF16)
    for k in range(out_ref.shape[0]):
        out_ref[k] = piece


def total_body(at_ref, part_ref, kept_ref, given_ref):
    first = at_ref[0] == 0
    owned = kept_ref.shape[0]
    total = part_ref[0].astype(F32)
    for k in range(1, part_ref.shape[0]):
        total = total + part_ref[k].astype(F32)
    kept_ref[...] = jnp.where(first, total[:owned], total[owned:])
    given_ref[...] = jnp.where(first, total[owned:], total[:owned])


def unpack_body(at_ref, kept_ref, given_ref, in_ref, out_w_ref):
    first = at_ref[0] == 0
    low = jnp.where(first, kept_ref[...], given_ref[...])
    high = jnp.where(first, given_ref[...], kept_ref[...])
    for s, group in enumerate((0, 3, 2, 1)):
        left = low if group == 0 else turn(low, 128 - 32 * group)
        right = high if group == 1 else turn(high, (160 - 32 * group) % 128)
        both = jnp.where(lane_group(low.shape) == 0, left, right)[:, : out_w_ref.shape[1]]
        if s < 3:
            in_ref[s] = both
        else:
            out_w_ref[...] = both


def project_body(at_ref, own_t, other_t, own_g, other_g, w_ref, out_ref, own_ref):
    plane = at_ref[1]
    half = own_t.shape[0]

    def columns(e):
        return jnp.concatenate([w_ref[holder(plane, e, l)] for l in range(2)], axis=0)

    for e in range(0, out_ref.shape[0], 2):
        w = jnp.concatenate([columns(e), columns(e + 1)], axis=1)
        both = []
        for t_ref, g_ref in ((own_t, own_g), (other_t, other_g)):
            from_t = jnp.dot(t_ref[...], w, preferred_element_type=F32)
            from_g = jnp.dot(g_ref[...], w, preferred_element_type=F32)
            both.append(jnp.where(lane_group(from_t.shape) % GROUPS < 3, from_t, from_g))
        for k in range(2):
            own, other = (b[:, 128 * k : 128 * (k + 1)] for b in both)
            odd = lane_group(own.shape) % 2 == 1
            chunk = chunk_of(plane, e + k)
            early = jnp.where(odd, own, turn(other, 96))
            late = jnp.where(odd, turn(other, 32), own)
            out_ref[chunk, :half] = early.astype(BF16)
            out_ref[chunk, half:] = late.astype(BF16)
            if e + k == 0:
                own_ref[:half] = early
                own_ref[half:] = late


def store_signal(x, sig):
    half = x.shape[0]
    product = x * turn(x, 64)
    turned = turn(product, 32)
    odd = lane_group(x.shape) % 2 == 1
    sig[:half] = jnp.where(odd, product, turned)
    sig[half:] = jnp.where(odd, turned, product)


def chunk_rows(core, q_half, step, rows):
    half = rows // 2
    start = half * core if q_half == 0 else half * (1 - core)
    return pl.ds(start + step, half // STEPS, stride=STEPS)


def first_body(
    at_ref, part_ref, own_ref, decay_ref, far_ref, x_ref, late_ref, left_ref, state_ref, sig, st
):
    core = at_ref[0]
    rows = sig.shape[0]
    half = rows // 2
    total = own_ref[...]
    for k in range(part_ref.shape[0]):
        total = total + jnp.where(at_ref[1] == k, 0.0, part_ref[k].astype(F32))
    x = total[:half]
    x_ref[...] = x
    late_ref[...] = total[half:]
    store_signal(x, sig)
    decay = [decay_ref[m : m + 1, :] for m in range(MODE_ROWS)]
    chunks = rows // STEPS
    per = chunks // 2

    def step(i, held):
        t = STEPS - 1 - i
        g = [sig[chunk_rows(core, h, t, rows), :] for h in range(2)]
        return tuple(
            decay[m] * held[2 * m + h] + g[h] for m in range(MODE_ROWS) for h in range(2)
        )

    zero = jnp.zeros((per, 128), F32)
    held = lax.fori_loop(0, STEPS, step, (zero,) * (2 * MODE_ROWS), unroll=8)
    for m in range(MODE_ROWS):
        for h in range(2):
            st[m * chunks + h * per : m * chunks + (h + 1) * per, :] = held[2 * m + h]
    far = far_ref[...]
    acc = jnp.zeros((MODE_ROWS, 128), F32)
    for q in reversed(range(chunks)):
        where = pl.ds(q, MODE_ROWS, stride=chunks)
        left_ref[where, :] = acc
        acc = st[where, :] + far * acc
    state_ref[...] = jnp.broadcast_to(acc[None], state_ref.shape)


def second_body(
    at_ref, x_ref, late_ref, left_ref, states_ref, reach_ref, power_ref, decay_ref, weight_ref,
    conv_ref, out_ref, sig, ys,
):
    core = at_ref[0]
    rows = sig.shape[0]
    half = rows // 2
    chunks = rows // STEPS
    per = chunks // 2
    store_signal(x_ref[...], sig)
    carry = jnp.sum(states_ref[...] * reach_ref[...], axis=0)
    decay = [decay_ref[m : m + 1, :] for m in range(MODE_ROWS)]
    weight = [weight_ref[m : m + 1, :] for m in range(MODE_ROWS)]
    begin = []
    for m in range(MODE_ROWS):
        here = slice(m * chunks, (m + 1) * chunks)
        c = left_ref[here, :] + power_ref[here, :] * carry[m : m + 1, :]
        begin += [c[:per], c[per:]]

    def step(i, held):
        t = STEPS - 1 - i
        new = []
        for h in range(2):
            g = sig[chunk_rows(core, h, t, rows), :]
            states = [decay[m] * held[2 * m + h] + g for m in range(MODE_ROWS)]
            y = weight[0] * states[0]
            for m in range(1, MODE_ROWS):
                y = y + weight[m] * states[m]
            ys[chunk_rows(core, h, t, rows), :] = y
            new.append(states)
        return tuple(new[h][m] for m in range(MODE_ROWS) for h in range(2))

    lax.fori_loop(0, STEPS, step, tuple(begin), unroll=8)
    y = ys[...]
    y = y + turn(y, 64)
    y = y + turn(y, 32)
    odd = lane_group((half, 128)) % 2 == 1
    late = turn(late_ref[...], 64) * jnp.where(odd, y[half:], y[:half])
    early = x_ref[...] * conv_ref[...].astype(F32)
    own = jnp.where(odd, early, late)
    other = turn(jnp.where(odd, late, turn(early, 64)), 96)
    out = jnp.concatenate([own, other], axis=0).astype(BF16)
    for k in range(out_ref.shape[0]):
        out_ref[k] = out


def weigh_body(at_ref, tt_ref, gt_ref, grads_ref, out_ref):
    plane = at_ref[1]
    block = out_ref.shape[1]
    for l in range(2):
        r = l * block
        for c in range(0, grads_ref.shape[0], 2):
            g = jnp.concatenate([grads_ref[chunk_of(plane, c + k)] for k in range(2)], axis=1)
            from_t = jnp.dot(tt_ref[r : r + block, :], g, preferred_element_type=F32)
            from_g = jnp.dot(gt_ref[r : r + block, :], g, preferred_element_type=F32)
            both = jnp.where(lane_group(from_t.shape) % GROUPS != 1, from_t, from_g).astype(BF16)
            out_ref[holder(plane, c, l)] = both[:, :128]
            out_ref[holder(plane, c + 1, l)] = both[:, 128:]


def by_lanes(table):
    wide = jnp.repeat(table, 2, axis=1)
    channels = wide.shape[1]
    return wide.reshape(GROUPS, MODE_ROWS, channels).transpose(1, 0, 2).reshape(MODE_ROWS, -1)


def local(tokens, grad_out, in_weight, out_weight, conv_out, residues, decay_length):
    half = tokens.shape[0]
    depth = tokens.shape[1]
    rows = 2 * half
    owned = in_weight.shape[0]
    channels = out_weight.shape[1]
    mine = channels // 2
    size_z, size_y, size_x = (lax.axis_size(a) for a in ("seq_0", "seq_1", "chan"))
    chips = size_z * size_y
    core = lax.axis_index("seq_2")
    place = lax.axis_index(CHIPS)

    at = jnp.stack([core, lax.axis_index("chan")]).astype(jnp.int32)

    def transposed(value, swap, to_owner):
        pairs = []
        for z in range(size_z):
            for k in range(2):
                for x in range(size_x):
                    j, l = z // 2, z % 2
                    held_z = (2 * j + OFFSETS[(x - j) % size_x][l]) % size_z
                    owner = (z * 2 + k) * size_x + x
                    held = (held_z * 2 + (1 - k if swap else k)) * size_x + j
                    pairs.append((held, owner) if to_owner else (owner, held))
        return lax.ppermute(value, ("seq_0", "seq_2", "chan"), pairs)

    def swapped(value):
        return lax.ppermute(value, "seq_2", [(0, 1), (1, 0)])

    piece = jax.ShapeDtypeStruct((owned, 128), BF16)
    kept, given = call(pack_body, (piece, piece), 4, inputs=3)(
        at, in_hbm(in_weight.transpose(1, 0, 2)), in_hbm(out_weight)
    )
    kept = transposed(kept, False, False)
    given = transposed(given, True, False)
    spread = call(
        spread_body, jax.ShapeDtypeStruct((chips, 2 * owned, 128), BF16), 4, inputs=3
    )(at, kept, given)
    weights = lax.all_to_all(spread, CHIPS, 0, 0, tiled=True).reshape(size_z, -1, 128)


    tokens_too = swapped(tokens)
    grads_too = swapped(grad_out)
    conv_own = jnp.where(core == 0, conv_out[:, :mine], conv_out[:, mine:])
    conv_sent = jnp.where(core == 0, conv_out[:, mine:], conv_out[:, :mine])
    conv = jnp.concatenate([swapped(conv_sent), conv_own], axis=1)
    conv = jnp.tile(conv, (1, 2))
    pick = residues.shape[1] // 2
    res = jnp.where(core == 0, residues[:, :pick], residues[:, pick:])
    length = jnp.where(core == 0, decay_length[:, :pick], decay_length[:, pick:])
    rate_raw = 1.0 / length
    weight = by_lanes(res * jnp.sqrt(-jnp.expm1(-2.0 * rate_raw)))
    rate = by_lanes(rate_raw)
    decay = jnp.exp(-rate)
    far = jnp.exp(-float(STEPS) * rate)
    chunks = rows // STEPS
    left_of = (chunks - 1 - jnp.arange(chunks)).astype(F32) * float(STEPS)
    power = jnp.exp(-left_of[None, :, None] * rate[:, None, :]).reshape(-1, 128)
    ahead = jnp.arange(chips) - place - 1
    reach = jnp.where(
        (ahead >= 0)[:, None, None],
        jnp.exp(-(jnp.maximum(ahead, 0) * rows).astype(F32)[:, None, None] * rate[None]),
        0.0,
    )

    project = call(
        project_body,
        (pltpu.HBM((size_x, rows, 128), BF16), jax.ShapeDtypeStruct((rows, 128), F32)),
        20,
        inputs=6,
        flops=4 * rows * depth * size_x * 128,
        moved=8 * rows * depth,
    )
    parts, own = project(
        at, in_hbm(tokens), in_hbm(tokens_too), in_hbm(grad_out), in_hbm(grads_too), weights
    )
    parts = lax.all_to_all(parts, "chan", 0, 0, tiled=True)

    first = call(
        first_body,
        (
            jax.ShapeDtypeStruct((half, 128), F32),
            jax.ShapeDtypeStruct((half, 128), F32),
            jax.ShapeDtypeStruct((MODE_ROWS * chunks, 128), F32),
            jax.ShapeDtypeStruct((chips, MODE_ROWS, 128), F32),
        ),
        10,
        scratch=[pltpu.VMEM((rows, 128), F32), pltpu.VMEM((MODE_ROWS * chunks, 128), F32)],
        inputs=5,
    )
    x, late, left, state = first(at, parts, own, decay, far)
    _, *turned = lax.optimization_barrier((left, tokens, tokens_too, grad_out, grads_too))
    turned = [in_hbm(t) for t in turned]
    flip = call(
        transpose_body, jax.ShapeDtypeStruct((depth, rows), BF16), 8, moved=4 * depth * rows
    )
    tokens_t = flip(*turned[:2])
    grads_t = flip(*turned[2:])
    states = lax.all_to_all(state, CHIPS, 0, 0, tiled=True)
    states, tokens_t, grads_t = lax.optimization_barrier((states, tokens_t, grads_t))
    second = call(
        second_body,
        jax.ShapeDtypeStruct((size_x, rows, 128), BF16),
        10,
        scratch=[pltpu.VMEM((rows, 128), F32), pltpu.VMEM((rows, 128), F32)],
        inputs=10,
    )
    grads = second(at, x, late, left, states, reach, power, decay, weight, conv)
    grads = lax.all_to_all(grads, "chan", 0, 0, tiled=True)

    weigh = call(
        weigh_body,
        jax.ShapeDtypeStruct((size_z, depth // 2, 128), BF16),
        16,
        inputs=4,
        flops=4 * rows * depth * size_x * 128,
        moved=8 * rows * depth,
    )
    partial = weigh(at, tokens_t, grads_t, grads).reshape(chips, 2 * owned, 128)
    partial = lax.all_to_all(partial, CHIPS, 0, 0, tiled=True)
    piece = jax.ShapeDtypeStruct((owned, 128), F32)
    kept, given = call(total_body, (piece, piece), 6, inputs=2)(at, partial)
    kept = transposed(kept, False, True)
    given = transposed(given, True, True)
    grad_in, grad_proj = call(
        unpack_body,
        (
            jax.ShapeDtypeStruct((3, owned, channels), F32),
            jax.ShapeDtypeStruct((owned, channels), F32),
        ),
        4,
        inputs=3,
    )(at, kept, given)
    return (grad_in.transpose(1, 0, 2), grad_proj)


def solution(mesh):
    finer = Mesh(
        mesh.devices.reshape(8, 8, 2, mesh.shape["chan"]), ("seq_0", "seq_1", "seq_2", "chan")
    )
    in_specs = (
        P(SEQ, "chan"),
        P(SEQ, "chan"),
        P(SEQ, None, "chan"),
        P(SEQ, "chan"),
        P(SEQ, "chan"),
        P(None, "chan"),
        P(None, "chan"),
    )
    out_specs = (P(SEQ, None, "chan"), P(SEQ, "chan"))
    return jax.shard_map(local, mesh=finer, in_specs=in_specs, out_specs=out_specs, check_vma=False)
```

```python
import jax
import jax.numpy as jnp
from jax import lax
from jax.experimental import pallas as pl
from jax.experimental.pallas import tpu as pltpu
from jax.sharding import Mesh
from jax.sharding import PartitionSpec as P

SEQ = ("seq_0", "seq_1", "seq_2")
CHIPS = ("seq_0", "seq_1")
STEPS = 64
MODE_ROWS = 4
GROUPS = 4
F32 = jnp.float32
BF16 = jnp.bfloat16
MIB = 1024 * 1024

OFFSETS = ((5, 4), (2, 3), (0, 1), (6, 7))


def call(body, out_shape, mib, scratch=(), flops=0, moved=0, inputs=None):
    specs = {}
    if inputs is not None:
        specs["in_specs"] = [pl.BlockSpec(memory_space=pltpu.SMEM)] + [
            pl.BlockSpec(memory_space=pltpu.VMEM)
        ] * (inputs - 1)
    return pl.pallas_call(
        body,
        out_shape=out_shape,
        scratch_shapes=list(scratch),
        compiler_params=pltpu.CompilerParams(vmem_limit_bytes=mib * MIB),
        cost_estimate=pl.CostEstimate(flops=flops, bytes_accessed=moved, transcendentals=0),
        **specs,
    )


def holder(plane, e, l):
    return lax.rem(2 * plane + OFFSETS[e][l], 2 * len(OFFSETS))


def chunk_of(plane, e):
    return lax.rem(plane + e, len(OFFSETS))


def in_hbm(x):
    return pltpu.with_memory_space_constraint(x, pltpu.HBM)


def lane_group(shape):
    lane = lax.broadcasted_iota(jnp.int32, shape, len(shape) - 1)
    return lane // 32


def turn(x, by):
    return pltpu.roll(x, by, x.ndim - 1)


def transpose_body(a_ref, b_ref, out_ref):
    half = a_ref.shape[0]
    out_ref[:, :half] = a_ref[...].T
    out_ref[:, half:] = b_ref[...].T


def pack_body(in_ref, out_w_ref, out_ref):
    width = out_w_ref.shape[1]
    row = lax.broadcasted_iota(jnp.int32, (width, 128), 0)
    lane = lax.broadcasted_iota(jnp.int32, (width, 128), 1)
    streams = [in_ref[0], in_ref[1], in_ref[2], out_w_ref[...]]
    for half in range(2):
        total = jnp.zeros(out_ref.shape[1:], F32)
        for s, w in enumerate(streams):
            chosen = (lane // 32 == s) & (row == half * 32 + lane % 32)
            total = total + jnp.dot(w, chosen.astype(F32).astype(BF16), preferred_element_type=F32)
        out_ref[half] = total.astype(BF16)


def spread_body(piece_ref, out_ref):
    for k in range(out_ref.shape[0]):
        out_ref[k] = piece_ref[k % 2]


def total_body(part_ref, out_ref):
    for core in range(2):
        total = part_ref[core].astype(F32)
        for k in range(core + 2, part_ref.shape[0], 2):
            total = total + part_ref[k].astype(F32)
        out_ref[core] = total


def unpack_body(part_ref, in_ref, out_w_ref):
    low = part_ref[0]
    high = part_ref[1]
    for s, group in enumerate((0, 3, 2, 1)):
        left = low if group == 0 else turn(low, 128 - 32 * group)
        right = high if group == 1 else turn(high, (160 - 32 * group) % 128)
        both = jnp.where(lane_group(low.shape) == 0, left, right)[:, : out_w_ref.shape[1]]
        if s < 3:
            in_ref[s] = both
        else:
            out_w_ref[...] = both


def project_body(at_ref, own_t, other_t, own_g, other_g, w_ref, out_ref, own_ref):
    plane = at_ref[1]
    half = own_t.shape[0]

    def columns(e):
        return jnp.concatenate([w_ref[holder(plane, e, l)] for l in range(2)], axis=0)

    for e in range(0, out_ref.shape[0], 2):
        w = jnp.concatenate([columns(e), columns(e + 1)], axis=1)
        both = []
        for t_ref, g_ref in ((own_t, own_g), (other_t, other_g)):
            from_t = jnp.dot(t_ref[...], w, preferred_element_type=F32)
            from_g = jnp.dot(g_ref[...], w, preferred_element_type=F32)
            both.append(jnp.where(lane_group(from_t.shape) % GROUPS < 3, from_t, from_g))
        for k in range(2):
            own, other = (b[:, 128 * k : 128 * (k + 1)] for b in both)
            odd = lane_group(own.shape) % 2 == 1
            chunk = chunk_of(plane, e + k)
            early = jnp.where(odd, own, turn(other, 96))
            late = jnp.where(odd, turn(other, 32), own)
            out_ref[chunk, :half] = early.astype(BF16)
            out_ref[chunk, half:] = late.astype(BF16)
            if e + k == 0:
                own_ref[:half] = early
                own_ref[half:] = late


def store_signal(x, sig):
    half = x.shape[0]
    product = x * turn(x, 64)
    turned = turn(product, 32)
    odd = lane_group(x.shape) % 2 == 1
    sig[:half] = jnp.where(odd, product, turned)
    sig[half:] = jnp.where(odd, turned, product)


def chunk_rows(core, q_half, step, rows):
    half = rows // 2
    start = half * core if q_half == 0 else half * (1 - core)
    return pl.ds(start + step, half // STEPS, stride=STEPS)


def first_body(
    at_ref, part_ref, own_ref, decay_ref, far_ref, x_ref, late_ref, left_ref, state_ref, sig, st
):
    core = at_ref[0]
    rows = sig.shape[0]
    half = rows // 2
    total = own_ref[...]
    for k in range(part_ref.shape[0]):
        total = total + jnp.where(at_ref[1] == k, 0.0, part_ref[k].astype(F32))
    rounded = total.astype(BF16).astype(F32)
    x = jnp.where(lane_group((half, 128)) < 2, rounded[:half], total[:half])
    x_ref[...] = x
    late_ref[...] = rounded[half:]
    store_signal(x, sig)
    decay = [decay_ref[m : m + 1, :] for m in range(MODE_ROWS)]
    chunks = rows // STEPS
    per = chunks // 2

    def step(i, held):
        t = STEPS - 1 - i
        g = [sig[chunk_rows(core, h, t, rows), :] for h in range(2)]
        return tuple(
            decay[m] * held[2 * m + h] + g[h] for m in range(MODE_ROWS) for h in range(2)
        )

    zero = jnp.zeros((per, 128), F32)
    held = lax.fori_loop(0, STEPS, step, (zero,) * (2 * MODE_ROWS), unroll=8)
    for m in range(MODE_ROWS):
        for h in range(2):
            st[m * chunks + h * per : m * chunks + (h + 1) * per, :] = held[2 * m + h]
    far = far_ref[...]
    acc = jnp.zeros((MODE_ROWS, 128), F32)
    for q in reversed(range(chunks)):
        where = pl.ds(q, MODE_ROWS, stride=chunks)
        left_ref[where, :] = acc
        acc = st[where, :] + far * acc
    state_ref[...] = jnp.broadcast_to(acc[None], state_ref.shape)


def second_body(
    at_ref, x_ref, late_ref, left_ref, states_ref, reach_ref, power_ref, decay_ref, weight_ref,
    conv_ref, out_ref, sig, ys,
):
    core = at_ref[0]
    rows = sig.shape[0]
    half = rows // 2
    chunks = rows // STEPS
    per = chunks // 2
    store_signal(x_ref[...], sig)
    carry = jnp.sum(states_ref[...] * reach_ref[...], axis=0)
    decay = [decay_ref[m : m + 1, :] for m in range(MODE_ROWS)]
    weight = [weight_ref[m : m + 1, :] for m in range(MODE_ROWS)]
    begin = []
    for m in range(MODE_ROWS):
        here = slice(m * chunks, (m + 1) * chunks)
        c = left_ref[here, :] + power_ref[here, :] * carry[m : m + 1, :]
        begin += [c[:per], c[per:]]

    def step(i, held):
        t = STEPS - 1 - i
        new = []
        for h in range(2):
            g = sig[chunk_rows(core, h, t, rows), :]
            states = [decay[m] * held[2 * m + h] + g for m in range(MODE_ROWS)]
            y = weight[0] * states[0]
            for m in range(1, MODE_ROWS):
                y = y + weight[m] * states[m]
            ys[chunk_rows(core, h, t, rows), :] = y
            new.append(states)
        return tuple(new[h][m] for m in range(MODE_ROWS) for h in range(2))

    lax.fori_loop(0, STEPS, step, tuple(begin), unroll=8)
    y = ys[...]
    y = y + turn(y, 64)
    y = y + turn(y, 32)
    odd = lane_group((half, 128)) % 2 == 1
    late = turn(late_ref[...], 64) * jnp.where(odd, y[half:], y[:half])
    early = x_ref[...] * conv_ref[...].astype(F32)
    own = jnp.where(odd, early, late)
    other = turn(jnp.where(odd, late, turn(early, 64)), 96)
    out = jnp.concatenate([own, other], axis=0).astype(BF16)
    for k in range(out_ref.shape[0]):
        out_ref[k] = out


def weigh_body(at_ref, tt_ref, gt_ref, grads_ref, out_ref):
    plane = at_ref[1]
    block = out_ref.shape[1]
    for l in range(2):
        r = l * block
        for c in range(0, grads_ref.shape[0], 2):
            g = jnp.concatenate([grads_ref[chunk_of(plane, c + k)] for k in range(2)], axis=1)
            from_t = jnp.dot(tt_ref[r : r + block, :], g, preferred_element_type=F32)
            from_g = jnp.dot(gt_ref[r : r + block, :], g, preferred_element_type=F32)
            both = jnp.where(lane_group(from_t.shape) % GROUPS != 1, from_t, from_g).astype(BF16)
            out_ref[holder(plane, c, l)] = both[:, :128]
            out_ref[holder(plane, c + 1, l)] = both[:, 128:]


def by_lanes(table):
    wide = jnp.repeat(table, 2, axis=1)
    channels = wide.shape[1]
    return wide.reshape(GROUPS, MODE_ROWS, channels).transpose(1, 0, 2).reshape(MODE_ROWS, -1)


def local(tokens, grad_out, in_weight, out_weight, conv_out, residues, decay_length):
    half = tokens.shape[0]
    depth = tokens.shape[1]
    rows = 2 * half
    owned = in_weight.shape[0]
    channels = out_weight.shape[1]
    mine = channels // 2
    size_z, size_y, size_x = (lax.axis_size(a) for a in ("seq_0", "seq_1", "chan"))
    chips = size_z * size_y
    core = lax.axis_index("seq_2")
    place = lax.axis_index(CHIPS)

    at = jnp.stack([core, lax.axis_index("chan")]).astype(jnp.int32)

    def transposed(value, to_owner):
        pairs = []
        for z in range(size_z):
            for x in range(size_x):
                j, l = z // 2, z % 2
                held = ((2 * j + OFFSETS[(x - j) % size_x][l]) % size_z) * size_x + j
                owner = z * size_x + x
                pairs.append((held, owner) if to_owner else (owner, held))
        return lax.ppermute(value, ("seq_0", "chan"), pairs)

    def swapped(value):
        return lax.ppermute(value, "seq_2", [(0, 1), (1, 0)])

    piece = call(pack_body, jax.ShapeDtypeStruct((2, owned, 128), BF16), 4)(
        in_hbm(in_weight.transpose(1, 0, 2)), in_hbm(out_weight)
    )
    piece = transposed(piece, False)
    spread = call(spread_body, jax.ShapeDtypeStruct((2 * chips, owned, 128), BF16), 4)(piece)
    weights = lax.all_to_all(spread, SEQ, 0, 0, tiled=True).reshape(size_z, -1, 128)

    tokens_too = swapped(tokens)
    grads_too = swapped(grad_out)
    conv_own = jnp.where(core == 0, conv_out[:, :mine], conv_out[:, mine:])
    conv_sent = jnp.where(core == 0, conv_out[:, mine:], conv_out[:, :mine])
    conv = jnp.concatenate([swapped(conv_sent), conv_own], axis=1)
    conv = jnp.tile(conv, (1, 2))
    pick = residues.shape[1] // 2
    res = jnp.where(core == 0, residues[:, :pick], residues[:, pick:])
    length = jnp.where(core == 0, decay_length[:, :pick], decay_length[:, pick:])
    rate_raw = 1.0 / length
    weight = by_lanes(res * jnp.sqrt(-jnp.expm1(-2.0 * rate_raw)))
    rate = by_lanes(rate_raw)
    decay = jnp.exp(-rate)
    far = jnp.exp(-float(STEPS) * rate)
    chunks = rows // STEPS
    left_of = (chunks - 1 - jnp.arange(chunks)).astype(F32) * float(STEPS)
    power = jnp.exp(-left_of[None, :, None] * rate[:, None, :]).reshape(-1, 128)
    ahead = jnp.arange(chips) - place - 1
    reach = jnp.where(
        (ahead >= 0)[:, None, None],
        jnp.exp(-(jnp.maximum(ahead, 0) * rows).astype(F32)[:, None, None] * rate[None]),
        0.0,
    )

    project = call(
        project_body,
        (pltpu.HBM((size_x, rows, 128), BF16), jax.ShapeDtypeStruct((rows, 128), F32)),
        20,
        inputs=6,
        flops=4 * rows * depth * size_x * 128,
        moved=8 * rows * depth,
    )
    parts, own = project(
        at, in_hbm(tokens), in_hbm(tokens_too), in_hbm(grad_out), in_hbm(grads_too), weights
    )
    parts = lax.all_to_all(parts, "chan", 0, 0, tiled=True)

    first = call(
        first_body,
        (
            jax.ShapeDtypeStruct((half, 128), F32),
            jax.ShapeDtypeStruct((half, 128), F32),
            jax.ShapeDtypeStruct((MODE_ROWS * chunks, 128), F32),
            jax.ShapeDtypeStruct((chips, MODE_ROWS, 128), F32),
        ),
        10,
        scratch=[pltpu.VMEM((rows, 128), F32), pltpu.VMEM((MODE_ROWS * chunks, 128), F32)],
        inputs=5,
    )
    x, late, left, state = first(at, parts, own, decay, far)
    _, *turned = lax.optimization_barrier((left, tokens, tokens_too, grad_out, grads_too))
    turned = [in_hbm(t) for t in turned]
    flip = call(
        transpose_body, jax.ShapeDtypeStruct((depth, rows), BF16), 8, moved=4 * depth * rows
    )
    tokens_t = flip(*turned[:2])
    grads_t = flip(*turned[2:])
    states = lax.all_to_all(state, CHIPS, 0, 0, tiled=True)
    states, tokens_t, grads_t = lax.optimization_barrier((states, tokens_t, grads_t))
    second = call(
        second_body,
        jax.ShapeDtypeStruct((size_x, rows, 128), BF16),
        10,
        scratch=[pltpu.VMEM((rows, 128), F32), pltpu.VMEM((rows, 128), F32)],
        inputs=10,
    )
    grads = second(at, x, late, left, states, reach, power, decay, weight, conv)
    grads = lax.all_to_all(grads, "chan", 0, 0, tiled=True)

    weigh = call(
        weigh_body,
        jax.ShapeDtypeStruct((size_z, depth // 2, 128), BF16),
        16,
        inputs=4,
        flops=4 * rows * depth * size_x * 128,
        moved=8 * rows * depth,
    )
    partial = weigh(at, tokens_t, grads_t, grads).reshape(2 * chips, owned, 128)
    partial = lax.all_to_all(partial, SEQ, 0, 0, tiled=True)
    total = call(total_body, jax.ShapeDtypeStruct((2, owned, 128), F32), 6)(partial)
    total = transposed(total, True)
    grad_in, grad_proj = call(
        unpack_body,
        (
            jax.ShapeDtypeStruct((3, owned, channels), F32),
            jax.ShapeDtypeStruct((owned, channels), F32),
        ),
        4,
    )(total)
    return (grad_in.transpose(1, 0, 2), grad_proj)


def solution(mesh):
    finer = Mesh(
        mesh.devices.reshape(8, 8, 2, mesh.shape["chan"]), ("seq_0", "seq_1", "seq_2", "chan")
    )
    in_specs = (
        P(SEQ, "chan"),
        P(SEQ, "chan"),
        P(SEQ, None, "chan"),
        P(SEQ, "chan"),
        P(SEQ, "chan"),
        P(None, "chan"),
        P(None, "chan"),
    )
    out_specs = (P(SEQ, None, "chan"), P(SEQ, "chan"))
    return jax.shard_map(local, mesh=finer, in_specs=in_specs, out_specs=out_specs, check_vma=False)
```

```python
import jax
import jax.numpy as jnp
from jax import lax
from jax.experimental import pallas as pl
from jax.experimental.pallas import tpu as pltpu
from jax.sharding import Mesh
from jax.sharding import PartitionSpec as P

SEQ = ("seq_0", "seq_1", "seq_2")
CHIPS = ("seq_0", "seq_1")
STEPS = 64
MODE_ROWS = 4
GROUPS = 4
F32 = jnp.float32
BF16 = jnp.bfloat16
MIB = 1024 * 1024

OFFSETS = ((5, 4), (2, 3), (0, 1), (6, 7))


def call(body, out_shape, mib, scratch=(), flops=0, moved=0, inputs=None):
    specs = {}
    if inputs is not None:
        specs["in_specs"] = [pl.BlockSpec(memory_space=pltpu.SMEM)] + [
            pl.BlockSpec(memory_space=pltpu.VMEM)
        ] * (inputs - 1)
    return pl.pallas_call(
        body,
        out_shape=out_shape,
        scratch_shapes=list(scratch),
        compiler_params=pltpu.CompilerParams(vmem_limit_bytes=mib * MIB),
        cost_estimate=pl.CostEstimate(flops=flops, bytes_accessed=moved, transcendentals=0),
        **specs,
    )


def holder(plane, e, l):
    return lax.rem(2 * plane + OFFSETS[e][l], 2 * len(OFFSETS))


def chunk_of(plane, e):
    return lax.rem(plane + e, len(OFFSETS))


def in_hbm(x):
    return pltpu.with_memory_space_constraint(x, pltpu.HBM)


def lane_group(shape):
    lane = lax.broadcasted_iota(jnp.int32, shape, len(shape) - 1)
    return lane // 32


def turn(x, by):
    return pltpu.roll(x, by, x.ndim - 1)


def transpose_body(a_ref, b_ref, out_ref):
    half = a_ref.shape[0]
    out_ref[:, :half] = a_ref[...].T
    out_ref[:, half:] = b_ref[...].T


def pack_body(in_ref, out_w_ref, out_ref):
    width = out_w_ref.shape[1]
    row = lax.broadcasted_iota(jnp.int32, (width, 128), 0)
    lane = lax.broadcasted_iota(jnp.int32, (width, 128), 1)
    streams = [in_ref[0], in_ref[1], in_ref[2], out_w_ref[...]]
    for half in range(2):
        total = jnp.zeros(out_ref.shape[1:], F32)
        for s, w in enumerate(streams):
            chosen = (lane // 32 == s) & (row == half * 32 + lane % 32)
            total = total + jnp.dot(w, chosen.astype(F32).astype(BF16), preferred_element_type=F32)
        out_ref[half] = total.astype(BF16)


def conv_body(at_ref, own_ref, other_ref, out_ref):
    core = at_ref[0]
    row = lax.broadcasted_iota(jnp.int32, (own_ref.shape[1], 128), 0)
    lane = lax.broadcasted_iota(jnp.int32, (own_ref.shape[1], 128), 1)
    total = jnp.zeros(out_ref.shape, F32)
    for odd, ref in ((1, own_ref), (0, other_ref)):
        chosen = (lane // 32 % 2 == odd) & (row == core * 32 + lane % 32)
        total = total + jnp.dot(
            ref[...], chosen.astype(F32).astype(BF16), preferred_element_type=F32
        )
    out_ref[...] = total.astype(BF16)


def spread_body(piece_ref, out_ref):
    for k in range(out_ref.shape[0]):
        out_ref[k] = piece_ref[k % 2]


def total_body(part_ref, out_ref):
    for core in range(2):
        total = part_ref[core].astype(F32)
        for k in range(core + 2, part_ref.shape[0], 2):
            total = total + part_ref[k].astype(F32)
        out_ref[core] = total


def unpack_body(part_ref, in_ref, out_w_ref):
    low = part_ref[0]
    high = part_ref[1]
    for s, group in enumerate((0, 3, 2, 1)):
        left = low if group == 0 else turn(low, 128 - 32 * group)
        right = high if group == 1 else turn(high, (160 - 32 * group) % 128)
        both = jnp.where(lane_group(low.shape) == 0, left, right)[:, : out_w_ref.shape[1]]
        if s < 3:
            in_ref[s] = both
        else:
            out_w_ref[...] = both


def project_body(at_ref, own_t, other_t, own_g, other_g, w_ref, out_ref, own_ref):
    plane = at_ref[1]
    half = own_t.shape[0]

    def columns(e):
        return jnp.concatenate([w_ref[holder(plane, e, l)] for l in range(2)], axis=0)

    for e in range(0, out_ref.shape[0], 2):
        w = jnp.concatenate([columns(e), columns(e + 1)], axis=1)
        both = []
        for t_ref, g_ref in ((own_t, own_g), (other_t, other_g)):
            from_t = jnp.dot(t_ref[...], w, preferred_element_type=F32)
            from_g = jnp.dot(g_ref[...], w, preferred_element_type=F32)
            both.append(jnp.where(lane_group(from_t.shape) % GROUPS < 3, from_t, from_g))
        for k in range(2):
            own, other = (b[:, 128 * k : 128 * (k + 1)] for b in both)
            odd = lane_group(own.shape) % 2 == 1
            chunk = chunk_of(plane, e + k)
            early = jnp.where(odd, own, turn(other, 96))
            late = jnp.where(odd, turn(other, 32), own)
            high = early.astype(BF16)
            low = early - high.astype(F32)
            low = jnp.where(
                lane_group((half // 2, 128)) < 2, low[: half // 2], turn(low[half // 2 :], 64)
            )
            out_ref[chunk, :half] = high
            out_ref[chunk, half : 2 * half] = late.astype(BF16)
            out_ref[chunk, 2 * half :] = low.astype(BF16)
            if e + k == 0:
                own_ref[:half] = early
                own_ref[half:] = late


def store_signal(x, sig):
    half = x.shape[0]
    product = x * turn(x, 64)
    turned = turn(product, 32)
    odd = lane_group(x.shape) % 2 == 1
    sig[:half] = jnp.where(odd, product, turned)
    sig[half:] = jnp.where(odd, turned, product)


def chunk_rows(core, q_half, step, rows):
    half = rows // 2
    start = half * core if q_half == 0 else half * (1 - core)
    return pl.ds(start + step, half // STEPS, stride=STEPS)


def first_body(
    at_ref, part_ref, own_ref, decay_ref, far_ref, x_ref, late_ref, left_ref, state_ref, sig, st
):
    core = at_ref[0]
    rows = sig.shape[0]
    half = rows // 2
    total = own_ref[...]
    low = jnp.zeros((half // 2, 128), F32)
    for k in range(part_ref.shape[0]):
        mine = at_ref[1] == k
        total = total + jnp.where(mine, 0.0, part_ref[k, :rows].astype(F32))
        low = low + jnp.where(mine, 0.0, part_ref[k, rows:].astype(F32))
    low = jnp.concatenate([low, turn(low, 64)], axis=0)
    early = total[:half] + jnp.where(lane_group(low.shape) < 2, low, 0.0)
    x = jnp.where(lane_group(early.shape) < 2, early.astype(BF16).astype(F32), early)
    x_ref[...] = x
    late_ref[...] = total[half:].astype(BF16).astype(F32)
    store_signal(x, sig)
    decay = [decay_ref[m : m + 1, :] for m in range(MODE_ROWS)]
    chunks = rows // STEPS
    per = chunks // 2

    def step(i, held):
        t = STEPS - 1 - i
        g = [sig[chunk_rows(core, h, t, rows), :] for h in range(2)]
        return tuple(
            decay[m] * held[2 * m + h] + g[h] for m in range(MODE_ROWS) for h in range(2)
        )

    zero = jnp.zeros((per, 128), F32)
    held = lax.fori_loop(0, STEPS, step, (zero,) * (2 * MODE_ROWS), unroll=8)
    for m in range(MODE_ROWS):
        for h in range(2):
            st[m * chunks + h * per : m * chunks + (h + 1) * per, :] = held[2 * m + h]
    far = far_ref[...]
    acc = jnp.zeros((MODE_ROWS, 128), F32)
    for q in reversed(range(chunks)):
        where = pl.ds(q, MODE_ROWS, stride=chunks)
        left_ref[where, :] = acc
        acc = st[where, :] + far * acc
    state_ref[...] = jnp.broadcast_to(acc[None], state_ref.shape)


def second_body(
    at_ref, x_ref, late_ref, left_ref, states_ref, reach_ref, power_ref, decay_ref, weight_ref,
    conv_ref, out_ref, sig, ys,
):
    core = at_ref[0]
    rows = sig.shape[0]
    half = rows // 2
    chunks = rows // STEPS
    per = chunks // 2
    store_signal(x_ref[...], sig)
    carry = jnp.sum(states_ref[...] * reach_ref[...], axis=0)
    decay = [decay_ref[m : m + 1, :] for m in range(MODE_ROWS)]
    weight = [weight_ref[m : m + 1, :] for m in range(MODE_ROWS)]
    begin = []
    for m in range(MODE_ROWS):
        here = slice(m * chunks, (m + 1) * chunks)
        c = left_ref[here, :] + power_ref[here, :] * carry[m : m + 1, :]
        begin += [c[:per], c[per:]]

    def step(i, held):
        t = STEPS - 1 - i
        new = []
        for h in range(2):
            g = sig[chunk_rows(core, h, t, rows), :]
            states = [decay[m] * held[2 * m + h] + g for m in range(MODE_ROWS)]
            y = weight[0] * states[0]
            for m in range(1, MODE_ROWS):
                y = y + weight[m] * states[m]
            ys[chunk_rows(core, h, t, rows), :] = y
            new.append(states)
        return tuple(new[h][m] for m in range(MODE_ROWS) for h in range(2))

    lax.fori_loop(0, STEPS, step, tuple(begin), unroll=8)
    y = ys[...]
    y = y + turn(y, 64)
    y = y + turn(y, 32)
    odd = lane_group((half, 128)) % 2 == 1
    late = turn(late_ref[...], 64) * jnp.where(odd, y[half:], y[:half])
    early = x_ref[...] * conv_ref[...].astype(F32)
    own = jnp.where(odd, early, late)
    other = turn(jnp.where(odd, late, turn(early, 64)), 96)
    out = jnp.concatenate([own, other], axis=0).astype(BF16)
    for k in range(out_ref.shape[0]):
        out_ref[k] = out


def weigh_body(at_ref, tt_ref, gt_ref, grads_ref, out_ref):
    plane = at_ref[1]
    block = out_ref.shape[1]
    for l in range(2):
        r = l * block
        for c in range(0, grads_ref.shape[0], 2):
            g = jnp.concatenate([grads_ref[chunk_of(plane, c + k)] for k in range(2)], axis=1)
            from_t = jnp.dot(tt_ref[r : r + block, :], g, preferred_element_type=F32)
            from_g = jnp.dot(gt_ref[r : r + block, :], g, preferred_element_type=F32)
            both = jnp.where(lane_group(from_t.shape) % GROUPS != 1, from_t, from_g).astype(BF16)
            out_ref[holder(plane, c, l)] = both[:, :128]
            out_ref[holder(plane, c + 1, l)] = both[:, 128:]


def by_lanes(table):
    wide = jnp.repeat(table, 2, axis=1)
    channels = wide.shape[1]
    return wide.reshape(GROUPS, MODE_ROWS, channels).transpose(1, 0, 2).reshape(MODE_ROWS, -1)


def local(tokens, grad_out, in_weight, out_weight, conv_out, residues, decay_length):
    half = tokens.shape[0]
    depth = tokens.shape[1]
    rows = 2 * half
    owned = in_weight.shape[0]
    channels = out_weight.shape[1]
    size_z, size_y, size_x = (lax.axis_size(a) for a in ("seq_0", "seq_1", "chan"))
    chips = size_z * size_y
    core = lax.axis_index("seq_2")
    place = lax.axis_index(CHIPS)

    at = jnp.stack([core, lax.axis_index("chan")]).astype(jnp.int32)

    def transposed(value, to_owner):
        pairs = []
        for z in range(size_z):
            for x in range(size_x):
                j, l = z // 2, z % 2
                held = ((2 * j + OFFSETS[(x - j) % size_x][l]) % size_z) * size_x + j
                owner = z * size_x + x
                pairs.append((held, owner) if to_owner else (owner, held))
        return lax.ppermute(value, ("seq_0", "chan"), pairs)

    def swapped(value):
        return lax.ppermute(value, "seq_2", [(0, 1), (1, 0)])

    piece = call(pack_body, jax.ShapeDtypeStruct((2, owned, 128), BF16), 4)(
        in_hbm(in_weight.transpose(1, 0, 2)), in_hbm(out_weight)
    )
    piece = transposed(piece, False)
    spread = call(spread_body, jax.ShapeDtypeStruct((2 * chips, owned, 128), BF16), 4)(piece)
    weights = lax.all_to_all(spread, SEQ, 0, 0, tiled=True).reshape(size_z, -1, 128)

    tokens_too = swapped(tokens)
    grads_too = swapped(grad_out)
    conv = call(conv_body, jax.ShapeDtypeStruct((half, 128), BF16), 4, inputs=3)(
        at, conv_out, swapped(conv_out)
    )

    pick = residues.shape[1] // 2
    res = jnp.where(core == 0, residues[:, :pick], residues[:, pick:])
    length = jnp.where(core == 0, decay_length[:, :pick], decay_length[:, pick:])
    rate_raw = 1.0 / length
    weight = by_lanes(res * jnp.sqrt(-jnp.expm1(-2.0 * rate_raw)))
    rate = by_lanes(rate_raw)
    decay = jnp.exp(-rate)
    far = jnp.exp(-float(STEPS) * rate)
    chunks = rows // STEPS
    left_of = (chunks - 1 - jnp.arange(chunks)).astype(F32) * float(STEPS)
    power = jnp.exp(-left_of[None, :, None] * rate[:, None, :]).reshape(-1, 128)
    ahead = jnp.arange(chips) - place - 1
    reach = jnp.where(
        (ahead >= 0)[:, None, None],
        jnp.exp(-(jnp.maximum(ahead, 0) * rows).astype(F32)[:, None, None] * rate[None]),
        0.0,
    )

    weights, conv, weight, decay, far, power, reach = lax.optimization_barrier(
        (weights, conv, weight, decay, far, power, reach)
    )
    project = call(
        project_body,
        (jax.ShapeDtypeStruct((size_x, rows + half // 2, 128), BF16), jax.ShapeDtypeStruct((rows, 128), F32)),
        20,
        inputs=6,
        flops=4 * rows * depth * size_x * 128,
        moved=8 * rows * depth,
    )
    parts, own = project(
        at, in_hbm(tokens), in_hbm(tokens_too), in_hbm(grad_out), in_hbm(grads_too), weights
    )
    parts = lax.all_to_all(parts, "chan", 0, 0, tiled=True)

    first = call(
        first_body,
        (
            jax.ShapeDtypeStruct((half, 128), F32),
            jax.ShapeDtypeStruct((half, 128), F32),
            jax.ShapeDtypeStruct((MODE_ROWS * chunks, 128), F32),
            jax.ShapeDtypeStruct((chips, MODE_ROWS, 128), F32),
        ),
        10,
        scratch=[pltpu.VMEM((rows, 128), F32), pltpu.VMEM((MODE_ROWS * chunks, 128), F32)],
        inputs=5,
    )
    x, late, left, state = first(at, parts, own, decay, far)
    _, *turned = lax.optimization_barrier((left, tokens, tokens_too, grad_out, grads_too))
    turned = [in_hbm(t) for t in turned]
    flip = call(
        transpose_body, jax.ShapeDtypeStruct((depth, rows), BF16), 8, moved=4 * depth * rows
    )
    tokens_t = flip(*turned[:2])
    grads_t = flip(*turned[2:])
    states = lax.all_to_all(state, CHIPS, 0, 0, tiled=True)
    states, tokens_t, grads_t = lax.optimization_barrier((states, tokens_t, grads_t))
    second = call(
        second_body,
        jax.ShapeDtypeStruct((size_x, rows, 128), BF16),
        10,
        scratch=[pltpu.VMEM((rows, 128), F32), pltpu.VMEM((rows, 128), F32)],
        inputs=10,
    )
    grads = second(at, x, late, left, states, reach, power, decay, weight, conv)
    grads = lax.all_to_all(grads, "chan", 0, 0, tiled=True)

    weigh = call(
        weigh_body,
        jax.ShapeDtypeStruct((size_z, depth // 2, 128), BF16),
        16,
        inputs=4,
        flops=4 * rows * depth * size_x * 128,
        moved=8 * rows * depth,
    )
    partial = weigh(at, tokens_t, grads_t, grads).reshape(2 * chips, owned, 128)
    partial = lax.all_to_all(partial, SEQ, 0, 0, tiled=True)
    total = call(total_body, jax.ShapeDtypeStruct((2, owned, 128), F32), 6)(partial)
    total = transposed(total, True)
    grad_in, grad_proj = call(
        unpack_body,
        (
            jax.ShapeDtypeStruct((3, owned, channels), F32),
            jax.ShapeDtypeStruct((owned, channels), F32),
        ),
        4,
    )(total)
    return (grad_in.transpose(1, 0, 2), grad_proj)


def solution(mesh):
    finer = Mesh(
        mesh.devices.reshape(8, 8, 2, mesh.shape["chan"]), ("seq_0", "seq_1", "seq_2", "chan")
    )
    in_specs = (
        P(SEQ, "chan"),
        P(SEQ, "chan"),
        P(SEQ, None, "chan"),
        P(SEQ, "chan"),
        P(SEQ, "chan"),
        P(None, "chan"),
        P(None, "chan"),
    )
    out_specs = (P(SEQ, None, "chan"), P(SEQ, "chan"))
    return jax.shard_map(local, mesh=finer, in_specs=in_specs, out_specs=out_specs, check_vma=False)
```

```python
import jax
import jax.numpy as jnp
from jax import lax
from jax.experimental import pallas as pl
from jax.experimental.pallas import tpu as pltpu
from jax.sharding import Mesh
from jax.sharding import PartitionSpec as P

SEQ = ("seq_0", "seq_1", "seq_2")
CHIPS = ("seq_0", "seq_1")
STEPS = 64
MODE_ROWS = 4
GROUPS = 4
F32 = jnp.float32
BF16 = jnp.bfloat16
MIB = 1024 * 1024

OFFSETS = ((5, 4), (2, 3), (0, 1), (6, 7))


def call(body, out_shape, mib, scratch=(), flops=0, moved=0, inputs=None):
    specs = {}
    if inputs is not None:
        specs["in_specs"] = [pl.BlockSpec(memory_space=pltpu.SMEM)] + [
            pl.BlockSpec(memory_space=pltpu.VMEM)
        ] * (inputs - 1)
    return pl.pallas_call(
        body,
        out_shape=out_shape,
        scratch_shapes=list(scratch),
        compiler_params=pltpu.CompilerParams(vmem_limit_bytes=mib * MIB),
        cost_estimate=pl.CostEstimate(flops=flops, bytes_accessed=moved, transcendentals=0),
        **specs,
    )


def holder(plane, e, l):
    return lax.rem(2 * plane + OFFSETS[e][l], 2 * len(OFFSETS))


def chunk_of(plane, e):
    return lax.rem(plane + e, len(OFFSETS))


def in_hbm(x):
    return pltpu.with_memory_space_constraint(x, pltpu.HBM)


def lane_group(shape):
    lane = lax.broadcasted_iota(jnp.int32, shape, len(shape) - 1)
    return lane // 32


def turn(x, by):
    return pltpu.roll(x, by, x.ndim - 1)


def transpose_body(a_ref, b_ref, out_ref):
    half = a_ref.shape[0]
    out_ref[:, :half] = a_ref[...].T
    out_ref[:, half:] = b_ref[...].T


def pack_body(in_ref, out_w_ref, out_ref):
    width = out_w_ref.shape[1]
    row = lax.broadcasted_iota(jnp.int32, (width, 128), 0)
    lane = lax.broadcasted_iota(jnp.int32, (width, 128), 1)
    streams = [in_ref[0], in_ref[1], in_ref[2], out_w_ref[...]]
    for half in range(2):
        total = jnp.zeros(out_ref.shape[1:], F32)
        for s, w in enumerate(streams):
            chosen = (lane // 32 == s) & (row == half * 32 + lane % 32)
            total = total + jnp.dot(w, chosen.astype(F32).astype(BF16), preferred_element_type=F32)
        out_ref[half] = total.astype(BF16)


def conv_body(at_ref, own_ref, other_ref, out_ref):
    core = at_ref[0]
    row = lax.broadcasted_iota(jnp.int32, (own_ref.shape[1], 128), 0)
    lane = lax.broadcasted_iota(jnp.int32, (own_ref.shape[1], 128), 1)
    total = jnp.zeros(out_ref.shape, F32)
    for odd, ref in ((1, own_ref), (0, other_ref)):
        chosen = (lane // 32 % 2 == odd) & (row == core * 32 + lane % 32)
        total = total + jnp.dot(
            ref[...], chosen.astype(F32).astype(BF16), preferred_element_type=F32
        )
    out_ref[...] = total.astype(BF16)


def spread_body(piece_ref, out_ref):
    for k in range(out_ref.shape[0]):
        out_ref[k] = piece_ref[k % 2]


def total_body(part_ref, out_ref):
    for core in range(2):
        total = part_ref[core].astype(F32)
        for k in range(core + 2, part_ref.shape[0], 2):
            total = total + part_ref[k].astype(F32)
        out_ref[core] = total


def unpack_body(part_ref, in_ref, out_w_ref):
    low = part_ref[0]
    high = part_ref[1]
    for s, group in enumerate((0, 3, 2, 1)):
        left = low if group == 0 else turn(low, 128 - 32 * group)
        right = high if group == 1 else turn(high, (160 - 32 * group) % 128)
        both = jnp.where(lane_group(low.shape) == 0, left, right)[:, : out_w_ref.shape[1]]
        if s < 3:
            in_ref[s] = both
        else:
            out_w_ref[...] = both


def project_body(at_ref, own_t, other_t, own_g, other_g, w_ref, out_ref, own_ref):
    plane = at_ref[1]
    half = own_t.shape[0]

    def columns(e):
        return jnp.concatenate([w_ref[holder(plane, e, l)] for l in range(2)], axis=0)

    for e in range(0, out_ref.shape[0], 2):
        w = jnp.concatenate([columns(e), columns(e + 1)], axis=1)
        both = []
        for t_ref, g_ref in ((own_t, own_g), (other_t, other_g)):
            from_t = jnp.dot(t_ref[...], w, preferred_element_type=F32)
            from_g = jnp.dot(g_ref[...], w, preferred_element_type=F32)
            both.append(jnp.where(lane_group(from_t.shape) % GROUPS < 3, from_t, from_g))
        for k in range(2):
            own, other = (b[:, 128 * k : 128 * (k + 1)] for b in both)
            odd = lane_group(own.shape) % 2 == 1
            chunk = chunk_of(plane, e + k)
            early = jnp.where(odd, own, turn(other, 96))
            late = jnp.where(odd, turn(other, 32), own)
            high = early.astype(BF16)
            low = early - high.astype(F32)
            low = jnp.where(
                lane_group((half // 2, 128)) < 2, low[: half // 2], turn(low[half // 2 :], 64)
            )
            out_ref[chunk, :half] = high
            out_ref[chunk, half : 2 * half] = late.astype(BF16)
            out_ref[chunk, 2 * half :] = low.astype(BF16)
            if e + k == 0:
                own_ref[:half] = early
                own_ref[half:] = late


def store_signal(x, sig):
    half = x.shape[0]
    product = x * turn(x, 64)
    turned = turn(product, 32)
    odd = lane_group(x.shape) % 2 == 1
    sig[:half] = jnp.where(odd, product, turned)
    sig[half:] = jnp.where(odd, turned, product)


def chunk_rows(core, q_half, step, rows):
    half = rows // 2
    start = half * core if q_half == 0 else half * (1 - core)
    return pl.ds(start + step, half // STEPS, stride=STEPS)


def first_body(
    at_ref, part_ref, own_ref, decay_ref, far_ref, x_ref, late_ref, left_ref, state_ref, sig, st
):
    core = at_ref[0]
    rows = sig.shape[0]
    half = rows // 2
    total = own_ref[...]
    low = jnp.zeros((half // 2, 128), F32)
    for k in range(part_ref.shape[0]):
        mine = at_ref[1] == k
        total = total + jnp.where(mine, 0.0, part_ref[k, :rows].astype(F32))
        low = low + jnp.where(mine, 0.0, part_ref[k, rows:].astype(F32))
    low = jnp.concatenate([low, turn(low, 64)], axis=0)
    early = total[:half] + jnp.where(lane_group(low.shape) < 2, low, 0.0)
    x = jnp.where(lane_group(early.shape) < 2, early.astype(BF16).astype(F32), early)
    x_ref[...] = x
    late_ref[...] = total[half:].astype(BF16).astype(F32)
    store_signal(x, sig)
    decay = [decay_ref[m : m + 1, :] for m in range(MODE_ROWS)]
    chunks = rows // STEPS
    per = chunks // 2

    def step(i, held):
        t = STEPS - 1 - i
        g = [sig[chunk_rows(core, h, t, rows), :] for h in range(2)]
        return tuple(
            decay[m] * held[2 * m + h] + g[h] for m in range(MODE_ROWS) for h in range(2)
        )

    zero = jnp.zeros((per, 128), F32)
    held = lax.fori_loop(0, STEPS, step, (zero,) * (2 * MODE_ROWS), unroll=8)
    for m in range(MODE_ROWS):
        for h in range(2):
            st[m * chunks + h * per : m * chunks + (h + 1) * per, :] = held[2 * m + h]
    far = far_ref[...]
    acc = jnp.zeros((MODE_ROWS, 128), F32)
    for q in reversed(range(chunks)):
        where = pl.ds(q, MODE_ROWS, stride=chunks)
        left_ref[where, :] = acc
        acc = st[where, :] + far * acc
    state_ref[...] = jnp.broadcast_to(acc[None], state_ref.shape)


def second_body(
    at_ref, x_ref, late_ref, left_ref, states_ref, reach_ref, power_ref, decay_ref, weight_ref,
    conv_ref, out_ref, sig, ys,
):
    core = at_ref[0]
    rows = sig.shape[0]
    half = rows // 2
    chunks = rows // STEPS
    per = chunks // 2
    store_signal(x_ref[...], sig)
    carry = jnp.sum(states_ref[...] * reach_ref[...], axis=0)
    decay = [decay_ref[m : m + 1, :] for m in range(MODE_ROWS)]
    weight = [weight_ref[m : m + 1, :] for m in range(MODE_ROWS)]
    begin = []
    for m in range(MODE_ROWS):
        here = slice(m * chunks, (m + 1) * chunks)
        c = left_ref[here, :] + power_ref[here, :] * carry[m : m + 1, :]
        begin += [c[:per], c[per:]]

    def step(i, held):
        t = STEPS - 1 - i
        new = []
        for h in range(2):
            g = sig[chunk_rows(core, h, t, rows), :]
            states = [decay[m] * held[2 * m + h] + g for m in range(MODE_ROWS)]
            y = weight[0] * states[0]
            for m in range(1, MODE_ROWS):
                y = y + weight[m] * states[m]
            ys[chunk_rows(core, h, t, rows), :] = y
            new.append(states)
        return tuple(new[h][m] for m in range(MODE_ROWS) for h in range(2))

    lax.fori_loop(0, STEPS, step, tuple(begin), unroll=8)
    y = ys[...]
    y = y + turn(y, 64)
    y = y + turn(y, 32)
    odd = lane_group((half, 128)) % 2 == 1
    late = turn(late_ref[...], 64) * jnp.where(odd, y[half:], y[:half])
    early = x_ref[...] * conv_ref[...].astype(F32)
    own = jnp.where(odd, early, late)
    other = turn(jnp.where(odd, late, turn(early, 64)), 96)
    out = jnp.concatenate([own, other], axis=0).astype(BF16)
    for k in range(out_ref.shape[0]):
        out_ref[k] = out


def weigh_body(at_ref, tt_ref, gt_ref, grads_ref, out_ref):
    plane = at_ref[1]
    block = out_ref.shape[1]
    for l in range(2):
        r = l * block
        for c in range(0, grads_ref.shape[0], 2):
            g = jnp.concatenate([grads_ref[chunk_of(plane, c + k)] for k in range(2)], axis=1)
            from_t = jnp.dot(tt_ref[r : r + block, :], g, preferred_element_type=F32)
            from_g = jnp.dot(gt_ref[r : r + block, :], g, preferred_element_type=F32)
            both = jnp.where(lane_group(from_t.shape) % GROUPS != 1, from_t, from_g).astype(BF16)
            out_ref[holder(plane, c, l)] = both[:, :128]
            out_ref[holder(plane, c + 1, l)] = both[:, 128:]


def by_lanes(table):
    wide = jnp.repeat(table, 2, axis=1)
    channels = wide.shape[1]
    return wide.reshape(GROUPS, MODE_ROWS, channels).transpose(1, 0, 2).reshape(MODE_ROWS, -1)


def local(tokens, grad_out, in_weight, out_weight, conv_out, residues, decay_length):
    half = tokens.shape[0]
    depth = tokens.shape[1]
    rows = 2 * half
    owned = in_weight.shape[0]
    channels = out_weight.shape[1]
    size_z, size_y, size_x = (lax.axis_size(a) for a in ("seq_0", "seq_1", "chan"))
    chips = size_z * size_y
    core = lax.axis_index("seq_2")
    place = lax.axis_index(CHIPS)

    at = jnp.stack([core, lax.axis_index("chan")]).astype(jnp.int32)

    def transposed(value, to_owner):
        pairs = []
        for z in range(size_z):
            for x in range(size_x):
                j, l = z // 2, z % 2
                held = ((2 * j + OFFSETS[(x - j) % size_x][l]) % size_z) * size_x + j
                owner = z * size_x + x
                pairs.append((held, owner) if to_owner else (owner, held))
        return lax.ppermute(value, ("seq_0", "chan"), pairs)

    def swapped(value):
        return lax.ppermute(value, "seq_2", [(0, 1), (1, 0)])

    piece = call(pack_body, jax.ShapeDtypeStruct((2, owned, 128), BF16), 4)(
        in_hbm(in_weight.transpose(1, 0, 2)), in_hbm(out_weight)
    )
    piece = transposed(piece, False)
    spread = call(spread_body, jax.ShapeDtypeStruct((2 * chips, owned, 128), BF16), 4)(piece)
    weights = lax.all_to_all(spread, SEQ, 0, 0, tiled=True).reshape(size_z, -1, 128)

    tokens_too = swapped(tokens)
    grads_too = swapped(grad_out)
    conv = call(conv_body, jax.ShapeDtypeStruct((half, 128), BF16), 4, inputs=3)(
        at, conv_out, swapped(conv_out)
    )

    pick = residues.shape[1] // 2
    res = jnp.where(core == 0, residues[:, :pick], residues[:, pick:])
    length = jnp.where(core == 0, decay_length[:, :pick], decay_length[:, pick:])
    rate_raw = 1.0 / length
    weight = by_lanes(res * jnp.sqrt(-jnp.expm1(-2.0 * rate_raw)))
    rate = by_lanes(rate_raw)
    decay = jnp.exp(-rate)
    far = jnp.exp(-float(STEPS) * rate)
    chunks = rows // STEPS
    left_of = (chunks - 1 - jnp.arange(chunks)).astype(F32) * float(STEPS)
    power = jnp.exp(-left_of[None, :, None] * rate[:, None, :]).reshape(-1, 128)
    ahead = jnp.arange(chips) - place - 1
    reach = jnp.where(
        (ahead >= 0)[:, None, None],
        jnp.exp(-(jnp.maximum(ahead, 0) * rows).astype(F32)[:, None, None] * rate[None]),
        0.0,
    )

    weights, conv, weight, decay, far, power, reach = lax.optimization_barrier(
        (weights, conv, weight, decay, far, power, reach)
    )
    project = call(
        project_body,
        (jax.ShapeDtypeStruct((size_x, rows + half // 2, 128), BF16), jax.ShapeDtypeStruct((rows, 128), F32)),
        48,
        inputs=6,
        flops=4 * rows * depth * size_x * 128,
        moved=8 * rows * depth,
    )
    parts, own = project(
        at, in_hbm(tokens), in_hbm(tokens_too), in_hbm(grad_out), in_hbm(grads_too), weights
    )
    parts = lax.all_to_all(parts, "chan", 0, 0, tiled=True)

    first = call(
        first_body,
        (
            jax.ShapeDtypeStruct((half, 128), F32),
            jax.ShapeDtypeStruct((half, 128), F32),
            jax.ShapeDtypeStruct((MODE_ROWS * chunks, 128), F32),
            jax.ShapeDtypeStruct((chips, MODE_ROWS, 128), F32),
        ),
        10,
        scratch=[pltpu.VMEM((rows, 128), F32), pltpu.VMEM((MODE_ROWS * chunks, 128), F32)],
        inputs=5,
    )
    x, late, left, state = first(at, parts, own, decay, far)
    _, *turned = lax.optimization_barrier((left, tokens, tokens_too, grad_out, grads_too))
    turned = [in_hbm(t) for t in turned]
    flip = call(
        transpose_body, jax.ShapeDtypeStruct((depth, rows), BF16), 8, moved=4 * depth * rows
    )
    tokens_t = flip(*turned[:2])
    grads_t = flip(*turned[2:])
    states = lax.all_to_all(state, CHIPS, 0, 0, tiled=True)
    states, tokens_t, grads_t = lax.optimization_barrier((states, tokens_t, grads_t))
    second = call(
        second_body,
        jax.ShapeDtypeStruct((size_x, rows, 128), BF16),
        10,
        scratch=[pltpu.VMEM((rows, 128), F32), pltpu.VMEM((rows, 128), F32)],
        inputs=10,
    )
    grads = second(at, x, late, left, states, reach, power, decay, weight, conv)
    grads = lax.all_to_all(grads, "chan", 0, 0, tiled=True)

    weigh = call(
        weigh_body,
        jax.ShapeDtypeStruct((size_z, depth // 2, 128), BF16),
        48,
        inputs=4,
        flops=4 * rows * depth * size_x * 128,
        moved=8 * rows * depth,
    )
    partial = weigh(at, tokens_t, grads_t, grads).reshape(2 * chips, owned, 128)
    partial = lax.all_to_all(partial, SEQ, 0, 0, tiled=True)
    total = call(total_body, jax.ShapeDtypeStruct((2, owned, 128), F32), 48)(partial)
    total = transposed(total, True)
    grad_in, grad_proj = call(
        unpack_body,
        (
            jax.ShapeDtypeStruct((3, owned, channels), F32),
            jax.ShapeDtypeStruct((owned, channels), F32),
        ),
        4,
    )(total)
    return (grad_in.transpose(1, 0, 2), grad_proj)


def solution(mesh):
    finer = Mesh(
        mesh.devices.reshape(8, 8, 2, mesh.shape["chan"]), ("seq_0", "seq_1", "seq_2", "chan")
    )
    in_specs = (
        P(SEQ, "chan"),
        P(SEQ, "chan"),
        P(SEQ, None, "chan"),
        P(SEQ, "chan"),
        P(SEQ, "chan"),
        P(None, "chan"),
        P(None, "chan"),
    )
    out_specs = (P(SEQ, None, "chan"), P(SEQ, "chan"))
    return jax.shard_map(local, mesh=finer, in_specs=in_specs, out_specs=out_specs, check_vma=False)
```

```python
import jax
import jax.numpy as jnp
from jax import lax
from jax.experimental import pallas as pl
from jax.experimental.pallas import tpu as pltpu
from jax.sharding import Mesh
from jax.sharding import PartitionSpec as P

SEQ = ("seq_0", "seq_1", "seq_2")
CHIPS = ("seq_0", "seq_1")
STEPS = 64
MODE_ROWS = 4
GROUPS = 4
F32 = jnp.float32
BF16 = jnp.bfloat16
MIB = 1024 * 1024

OFFSETS = ((5, 4), (2, 3), (0, 1), (6, 7))


def call(body, out_shape, mib, scratch=(), flops=0, moved=0, inputs=None):
    specs = {}
    if inputs is not None:
        specs["in_specs"] = [pl.BlockSpec(memory_space=pltpu.SMEM)] + [
            pl.BlockSpec(memory_space=pltpu.VMEM)
        ] * (inputs - 1)
    return pl.pallas_call(
        body,
        out_shape=out_shape,
        scratch_shapes=list(scratch),
        compiler_params=pltpu.CompilerParams(vmem_limit_bytes=mib * MIB),
        cost_estimate=pl.CostEstimate(flops=flops, bytes_accessed=moved, transcendentals=0),
        **specs,
    )


def holder(plane, e, l):
    return lax.rem(2 * plane + OFFSETS[e][l], 2 * len(OFFSETS))


def chunk_of(plane, e):
    return lax.rem(plane + e, len(OFFSETS))


def in_hbm(x):
    return pltpu.with_memory_space_constraint(x, pltpu.HBM)


def lane_group(shape):
    lane = lax.broadcasted_iota(jnp.int32, shape, len(shape) - 1)
    return lane // 32


def turn(x, by):
    return pltpu.roll(x, by, x.ndim - 1)


def transpose_body(a_ref, b_ref, out_ref):
    half = a_ref.shape[0]
    out_ref[:, :half] = a_ref[...].T
    out_ref[:, half:] = b_ref[...].T


def pack_body(in_ref, out_w_ref, out_ref):
    width = out_w_ref.shape[1]
    row = lax.broadcasted_iota(jnp.int32, (width, 128), 0)
    lane = lax.broadcasted_iota(jnp.int32, (width, 128), 1)
    streams = [in_ref[0], in_ref[1], in_ref[2], out_w_ref[...]]
    for half in range(2):
        total = jnp.zeros(out_ref.shape[1:], F32)
        for s, w in enumerate(streams):
            chosen = (lane // 32 == s) & (row == half * 32 + lane % 32)
            total = total + jnp.dot(w, chosen.astype(F32).astype(BF16), preferred_element_type=F32)
        out_ref[half] = total.astype(BF16)


def conv_body(at_ref, own_ref, other_ref, out_ref):
    core = at_ref[0]
    row = lax.broadcasted_iota(jnp.int32, (own_ref.shape[1], 128), 0)
    lane = lax.broadcasted_iota(jnp.int32, (own_ref.shape[1], 128), 1)
    total = jnp.zeros(out_ref.shape, F32)
    for odd, ref in ((1, own_ref), (0, other_ref)):
        chosen = (lane // 32 % 2 == odd) & (row == core * 32 + lane % 32)
        total = total + jnp.dot(
            ref[...], chosen.astype(F32).astype(BF16), preferred_element_type=F32
        )
    out_ref[...] = total.astype(BF16)


def spread_body(piece_ref, out_ref):
    for k in range(out_ref.shape[0]):
        out_ref[k] = piece_ref[k % 2]


def total_body(part_ref, out_ref):
    for core in range(2):
        total = part_ref[core].astype(F32)
        for k in range(core + 2, part_ref.shape[0], 2):
            total = total + part_ref[k].astype(F32)
        out_ref[core] = total


def unpack_body(part_ref, in_ref, out_w_ref):
    low = part_ref[0]
    high = part_ref[1]
    for s, group in enumerate((0, 3, 2, 1)):
        left = low if group == 0 else turn(low, 128 - 32 * group)
        right = high if group == 1 else turn(high, (160 - 32 * group) % 128)
        both = jnp.where(lane_group(low.shape) == 0, left, right)[:, : out_w_ref.shape[1]]
        if s < 3:
            in_ref[s] = both
        else:
            out_w_ref[...] = both


def project_body(at_ref, own_t, other_t, own_g, other_g, w_ref, out_ref, own_ref):
    plane = at_ref[1]
    half = own_t.shape[0]

    def columns(e):
        return jnp.concatenate([w_ref[holder(plane, e, l)] for l in range(2)], axis=0)

    for e in range(0, out_ref.shape[0], 2):
        w = jnp.concatenate([columns(e), columns(e + 1)], axis=1)
        both = []
        for t_ref, g_ref in ((own_t, own_g), (other_t, other_g)):
            from_t = jnp.dot(t_ref[...], w, preferred_element_type=F32)
            from_g = jnp.dot(g_ref[...], w, preferred_element_type=F32)
            both.append(jnp.where(lane_group(from_t.shape) % GROUPS < 3, from_t, from_g))
        for k in range(2):
            own, other = (b[:, 128 * k : 128 * (k + 1)] for b in both)
            odd = lane_group(own.shape) % 2 == 1
            chunk = chunk_of(plane, e + k)
            early = jnp.where(odd, own, turn(other, 96))
            late = jnp.where(odd, turn(other, 32), own)
            high = early.astype(BF16)
            low = early - high.astype(F32)
            low = jnp.where(
                lane_group((half // 2, 128)) < 2, low[: half // 2], turn(low[half // 2 :], 64)
            )
            out_ref[chunk, :half] = high
            out_ref[chunk, half : 2 * half] = late.astype(BF16)
            out_ref[chunk, 2 * half :] = low.astype(BF16)
            if e + k == 0:
                own_ref[:half] = early
                own_ref[half:] = late


def store_signal(x, sig):
    half = x.shape[0]
    product = x * turn(x, 64)
    turned = turn(product, 32)
    odd = lane_group(x.shape) % 2 == 1
    sig[:half] = jnp.where(odd, product, turned)
    sig[half:] = jnp.where(odd, turned, product)


def chunk_rows(core, q_half, step, rows):
    half = rows // 2
    start = half * core if q_half == 0 else half * (1 - core)
    return pl.ds(start + step, half // STEPS, stride=STEPS)


def first_body(
    at_ref, part_ref, own_ref, decay_ref, far_ref, conv_ref, x_ref, late_ref, left_ref, state_ref,
    early_ref, sig, st,
):
    core = at_ref[0]
    rows = sig.shape[0]
    half = rows // 2
    total = own_ref[...]
    low = jnp.zeros((half // 2, 128), F32)
    for k in range(part_ref.shape[0]):
        mine = at_ref[1] == k
        total = total + jnp.where(mine, 0.0, part_ref[k, :rows].astype(F32))
        low = low + jnp.where(mine, 0.0, part_ref[k, rows:].astype(F32))
    low = jnp.concatenate([low, turn(low, 64)], axis=0)
    early = total[:half] + jnp.where(lane_group(low.shape) < 2, low, 0.0)
    x = jnp.where(lane_group(early.shape) < 2, early.astype(BF16).astype(F32), early)
    x_ref[...] = x
    late_ref[...] = total[half:].astype(BF16).astype(F32)
    grads = x * conv_ref[...].astype(F32)
    odd = lane_group(grads.shape) % 2 == 1
    early_ref[...] = jnp.where(odd, grads, turn(grads, 64))
    store_signal(x, sig)
    decay = [decay_ref[m : m + 1, :] for m in range(MODE_ROWS)]
    chunks = rows // STEPS
    per = chunks // 2

    def step(i, held):
        t = STEPS - 1 - i
        g = [sig[chunk_rows(core, h, t, rows), :] for h in range(2)]
        return tuple(
            decay[m] * held[2 * m + h] + g[h] for m in range(MODE_ROWS) for h in range(2)
        )

    zero = jnp.zeros((per, 128), F32)
    held = lax.fori_loop(0, STEPS, step, (zero,) * (2 * MODE_ROWS), unroll=8)
    for m in range(MODE_ROWS):
        for h in range(2):
            st[m * chunks + h * per : m * chunks + (h + 1) * per, :] = held[2 * m + h]
    far = far_ref[...]
    acc = jnp.zeros((MODE_ROWS, 128), F32)
    for q in reversed(range(chunks)):
        where = pl.ds(q, MODE_ROWS, stride=chunks)
        left_ref[where, :] = acc
        acc = st[where, :] + far * acc
    state_ref[...] = jnp.broadcast_to(acc[None], state_ref.shape)


def second_body(
    at_ref, x_ref, late_ref, left_ref, states_ref, reach_ref, power_ref, decay_ref, weight_ref,
    out_ref, sig, ys,
):
    core = at_ref[0]
    rows = sig.shape[0]
    half = rows // 2
    chunks = rows // STEPS
    per = chunks // 2
    store_signal(x_ref[...], sig)
    carry = jnp.sum(states_ref[...] * reach_ref[...], axis=0)
    decay = [decay_ref[m : m + 1, :] for m in range(MODE_ROWS)]
    weight = [weight_ref[m : m + 1, :] for m in range(MODE_ROWS)]
    begin = []
    for m in range(MODE_ROWS):
        here = slice(m * chunks, (m + 1) * chunks)
        c = left_ref[here, :] + power_ref[here, :] * carry[m : m + 1, :]
        begin += [c[:per], c[per:]]

    def step(i, held):
        t = STEPS - 1 - i
        new = []
        for h in range(2):
            g = sig[chunk_rows(core, h, t, rows), :]
            states = [decay[m] * held[2 * m + h] + g for m in range(MODE_ROWS)]
            y = weight[0] * states[0]
            for m in range(1, MODE_ROWS):
                y = y + weight[m] * states[m]
            ys[chunk_rows(core, h, t, rows), :] = y
            new.append(states)
        return tuple(new[h][m] for m in range(MODE_ROWS) for h in range(2))

    lax.fori_loop(0, STEPS, step, tuple(begin), unroll=8)
    y = ys[...]
    y = y + turn(y, 64)
    y = y + turn(y, 32)
    odd = lane_group((half, 128)) % 2 == 1
    out = (turn(late_ref[...], 64) * jnp.where(odd, y[half:], y[:half])).astype(BF16)
    for k in range(out_ref.shape[0]):
        out_ref[k] = out


def weigh_body(at_ref, tt_ref, gt_ref, early_ref, late_ref, out_ref):
    plane = at_ref[1]
    block = out_ref.shape[1]

    def columns(e):
        early = early_ref[chunk_of(plane, e)]
        late = late_ref[chunk_of(plane, e)].astype(F32)
        odd = lane_group(early.shape) % 2 == 1
        own = jnp.where(odd, early, late)
        other = turn(jnp.where(odd, late, early), 96)
        return jnp.concatenate([own, other], axis=0).astype(BF16)

    for e in range(0, early_ref.shape[0], 2):
        g = jnp.concatenate([columns(e), columns(e + 1)], axis=1)
        for l in range(2):
            here = slice(l * block, (l + 1) * block)
            from_t = jnp.dot(tt_ref[here, :], g, preferred_element_type=F32)
            from_g = jnp.dot(gt_ref[here, :], g, preferred_element_type=F32)
            both = jnp.where(lane_group(from_t.shape) % GROUPS != 1, from_t, from_g).astype(BF16)
            out_ref[holder(plane, e, l)] = both[:, :128]
            out_ref[holder(plane, e + 1, l)] = both[:, 128:]


def by_lanes(table):
    wide = jnp.repeat(table, 2, axis=1)
    channels = wide.shape[1]
    return wide.reshape(GROUPS, MODE_ROWS, channels).transpose(1, 0, 2).reshape(MODE_ROWS, -1)


def local(tokens, grad_out, in_weight, out_weight, conv_out, residues, decay_length):
    half = tokens.shape[0]
    depth = tokens.shape[1]
    rows = 2 * half
    owned = in_weight.shape[0]
    channels = out_weight.shape[1]
    size_z, size_y, size_x = (lax.axis_size(a) for a in ("seq_0", "seq_1", "chan"))
    chips = size_z * size_y
    core = lax.axis_index("seq_2")
    place = lax.axis_index(CHIPS)

    at = jnp.stack([core, lax.axis_index("chan")]).astype(jnp.int32)

    def transposed(value, to_owner):
        pairs = []
        for z in range(size_z):
            for x in range(size_x):
                j, l = z // 2, z % 2
                held = ((2 * j + OFFSETS[(x - j) % size_x][l]) % size_z) * size_x + j
                owner = z * size_x + x
                pairs.append((held, owner) if to_owner else (owner, held))
        return lax.ppermute(value, ("seq_0", "chan"), pairs)

    def swapped(value):
        return lax.ppermute(value, "seq_2", [(0, 1), (1, 0)])

    piece = call(pack_body, jax.ShapeDtypeStruct((2, owned, 128), BF16), 4)(
        in_hbm(in_weight.transpose(1, 0, 2)), in_hbm(out_weight)
    )
    piece = transposed(piece, False)
    spread = call(spread_body, jax.ShapeDtypeStruct((2 * chips, owned, 128), BF16), 4)(piece)
    weights = lax.all_to_all(spread, SEQ, 0, 0, tiled=True).reshape(size_z, -1, 128)

    tokens_too = swapped(tokens)
    grads_too = swapped(grad_out)
    conv = call(conv_body, jax.ShapeDtypeStruct((half, 128), BF16), 4, inputs=3)(
        at, conv_out, swapped(conv_out)
    )

    pick = residues.shape[1] // 2
    res = jnp.where(core == 0, residues[:, :pick], residues[:, pick:])
    length = jnp.where(core == 0, decay_length[:, :pick], decay_length[:, pick:])
    rate_raw = 1.0 / length
    weight = by_lanes(res * jnp.sqrt(-jnp.expm1(-2.0 * rate_raw)))
    rate = by_lanes(rate_raw)
    decay = jnp.exp(-rate)
    far = jnp.exp(-float(STEPS) * rate)
    chunks = rows // STEPS
    left_of = (chunks - 1 - jnp.arange(chunks)).astype(F32) * float(STEPS)
    power = jnp.exp(-left_of[None, :, None] * rate[:, None, :]).reshape(-1, 128)
    ahead = jnp.arange(chips) - place - 1
    reach = jnp.where(
        (ahead >= 0)[:, None, None],
        jnp.exp(-(jnp.maximum(ahead, 0) * rows).astype(F32)[:, None, None] * rate[None]),
        0.0,
    )

    weights, conv, weight, decay, far, power, reach = lax.optimization_barrier(
        (weights, conv, weight, decay, far, power, reach)
    )
    project = call(
        project_body,
        (jax.ShapeDtypeStruct((size_x, rows + half // 2, 128), BF16), jax.ShapeDtypeStruct((rows, 128), F32)),
        20,
        inputs=6,
        flops=4 * rows * depth * size_x * 128,
        moved=8 * rows * depth,
    )
    parts, own = project(
        at, in_hbm(tokens), in_hbm(tokens_too), in_hbm(grad_out), in_hbm(grads_too), weights
    )
    parts = lax.all_to_all(parts, "chan", 0, 0, tiled=True)

    first = call(
        first_body,
        (
            jax.ShapeDtypeStruct((half, 128), F32),
            jax.ShapeDtypeStruct((half, 128), F32),
            jax.ShapeDtypeStruct((MODE_ROWS * chunks, 128), F32),
            jax.ShapeDtypeStruct((chips, MODE_ROWS, 128), F32),
            pltpu.HBM((half, 128), F32),
        ),
        10,
        scratch=[pltpu.VMEM((rows, 128), F32), pltpu.VMEM((MODE_ROWS * chunks, 128), F32)],
        inputs=6,
    )
    x, late, left, state, early = first(at, parts, own, decay, far, conv)
    early = lax.all_gather(early, "chan", axis=0)
    _, *turned = lax.optimization_barrier((left, tokens, tokens_too, grad_out, grads_too))
    turned = [in_hbm(t) for t in turned]
    flip = call(
        transpose_body, jax.ShapeDtypeStruct((depth, rows), BF16), 8, moved=4 * depth * rows
    )
    tokens_t = flip(*turned[:2])
    grads_t = flip(*turned[2:])
    states = lax.all_to_all(state, CHIPS, 0, 0, tiled=True)
    states, tokens_t, grads_t = lax.optimization_barrier((states, tokens_t, grads_t))
    second = call(
        second_body,
        jax.ShapeDtypeStruct((size_x, half, 128), BF16),
        10,
        scratch=[pltpu.VMEM((rows, 128), F32), pltpu.VMEM((rows, 128), F32)],
        inputs=9,
    )
    grads = second(at, x, late, left, states, reach, power, decay, weight)
    grads = lax.all_to_all(grads, "chan", 0, 0, tiled=True)

    weigh = call(
        weigh_body,
        jax.ShapeDtypeStruct((size_z, depth // 2, 128), BF16),
        16,
        inputs=5,
        flops=4 * rows * depth * size_x * 128,
        moved=8 * rows * depth,
    )
    partial = weigh(at, tokens_t, grads_t, in_hbm(early), grads).reshape(2 * chips, owned, 128)
    partial = lax.all_to_all(partial, SEQ, 0, 0, tiled=True)
    total = call(total_body, jax.ShapeDtypeStruct((2, owned, 128), F32), 6)(partial)
    total = transposed(total, True)
    grad_in, grad_proj = call(
        unpack_body,
        (
            jax.ShapeDtypeStruct((3, owned, channels), F32),
            jax.ShapeDtypeStruct((owned, channels), F32),
        ),
        4,
    )(total)
    return (grad_in.transpose(1, 0, 2), grad_proj)


def solution(mesh):
    finer = Mesh(
        mesh.devices.reshape(8, 8, 2, mesh.shape["chan"]), ("seq_0", "seq_1", "seq_2", "chan")
    )
    in_specs = (
        P(SEQ, "chan"),
        P(SEQ, "chan"),
        P(SEQ, None, "chan"),
        P(SEQ, "chan"),
        P(SEQ, "chan"),
        P(None, "chan"),
        P(None, "chan"),
    )
    out_specs = (P(SEQ, None, "chan"), P(SEQ, "chan"))
    return jax.shard_map(local, mesh=finer, in_specs=in_specs, out_specs=out_specs, check_vma=False)
```

```python
import jax
import jax.numpy as jnp
from jax import lax
from jax.experimental import pallas as pl
from jax.experimental.pallas import tpu as pltpu
from jax.sharding import Mesh
from jax.sharding import PartitionSpec as P

SEQ = ("seq_0", "seq_1", "seq_2")
CHIPS = ("seq_0", "seq_1")
STEPS = 64
MODE_ROWS = 4
GROUPS = 4
F32 = jnp.float32
BF16 = jnp.bfloat16
MIB = 1024 * 1024

OFFSETS = ((5, 4), (2, 3), (0, 1), (6, 7))


def call(body, out_shape, mib, scratch=(), flops=0, moved=0, inputs=None):
    specs = {}
    if inputs is not None:
        specs["in_specs"] = [pl.BlockSpec(memory_space=pltpu.SMEM)] + [
            pl.BlockSpec(memory_space=pltpu.VMEM)
        ] * (inputs - 1)
    return pl.pallas_call(
        body,
        out_shape=out_shape,
        scratch_shapes=list(scratch),
        compiler_params=pltpu.CompilerParams(vmem_limit_bytes=mib * MIB),
        cost_estimate=pl.CostEstimate(flops=flops, bytes_accessed=moved, transcendentals=0),
        **specs,
    )


def holder(plane, e, l):
    return lax.rem(2 * plane + OFFSETS[e][l], 2 * len(OFFSETS))


def chunk_of(plane, e):
    return lax.rem(plane + e, len(OFFSETS))


def in_hbm(x):
    return pltpu.with_memory_space_constraint(x, pltpu.HBM)


def lane_group(shape):
    lane = lax.broadcasted_iota(jnp.int32, shape, len(shape) - 1)
    return lane // 32


def turn(x, by):
    return pltpu.roll(x, by, x.ndim - 1)


def transpose_body(a_ref, b_ref, out_ref):
    half = a_ref.shape[0]
    out_ref[:, :half] = a_ref[...].T
    out_ref[:, half:] = b_ref[...].T


def pack_body(in_ref, out_w_ref, out_ref):
    width = out_w_ref.shape[1]
    row = lax.broadcasted_iota(jnp.int32, (width, 128), 0)
    lane = lax.broadcasted_iota(jnp.int32, (width, 128), 1)
    streams = [in_ref[0], in_ref[1], in_ref[2], out_w_ref[...]]
    for half in range(2):
        total = jnp.zeros(out_ref.shape[1:], F32)
        for s, w in enumerate(streams):
            chosen = (lane // 32 == s) & (row == half * 32 + lane % 32)
            total = total + jnp.dot(w, chosen.astype(F32).astype(BF16), preferred_element_type=F32)
        out_ref[half] = total.astype(BF16)


def conv_body(at_ref, own_ref, other_ref, out_ref):
    core = at_ref[0]
    row = lax.broadcasted_iota(jnp.int32, (own_ref.shape[1], 128), 0)
    lane = lax.broadcasted_iota(jnp.int32, (own_ref.shape[1], 128), 1)
    total = jnp.zeros(out_ref.shape, F32)
    for odd, ref in ((1, own_ref), (0, other_ref)):
        chosen = (lane // 32 % 2 == odd) & (row == core * 32 + lane % 32)
        total = total + jnp.dot(
            ref[...], chosen.astype(F32).astype(BF16), preferred_element_type=F32
        )
    out_ref[...] = total.astype(BF16)


def spread_body(piece_ref, out_ref):
    for k in range(out_ref.shape[0]):
        out_ref[k] = piece_ref[k % 2]


def total_body(part_ref, out_ref):
    for core in range(2):
        total = part_ref[core].astype(F32)
        for k in range(core + 2, part_ref.shape[0], 2):
            total = total + part_ref[k].astype(F32)
        out_ref[core] = total


def unpack_body(part_ref, in_ref, out_w_ref):
    low = part_ref[0]
    high = part_ref[1]
    for s, group in enumerate((0, 3, 2, 1)):
        left = low if group == 0 else turn(low, 128 - 32 * group)
        right = high if group == 1 else turn(high, (160 - 32 * group) % 128)
        both = jnp.where(lane_group(low.shape) == 0, left, right)[:, : out_w_ref.shape[1]]
        if s < 3:
            in_ref[s] = both
        else:
            out_w_ref[...] = both


def project_body(at_ref, own_t, other_t, own_g, other_g, w_ref, out_ref, own_ref):
    plane = at_ref[1]
    half = own_t.shape[0]

    def columns(e):
        return jnp.concatenate([w_ref[holder(plane, e, l)] for l in range(2)], axis=0)

    for e in range(0, out_ref.shape[0], 2):
        w = jnp.concatenate([columns(e), columns(e + 1)], axis=1)
        both = []
        for t_ref, g_ref in ((own_t, own_g), (other_t, other_g)):
            from_t = jnp.dot(t_ref[...], w, preferred_element_type=F32)
            from_g = jnp.dot(g_ref[...], w, preferred_element_type=F32)
            both.append(jnp.where(lane_group(from_t.shape) % GROUPS < 3, from_t, from_g))
        for k in range(2):
            own, other = (b[:, 128 * k : 128 * (k + 1)] for b in both)
            odd = lane_group(own.shape) % 2 == 1
            chunk = chunk_of(plane, e + k)
            early = jnp.where(odd, own, turn(other, 96))
            late = jnp.where(odd, turn(other, 32), own)
            high = early.astype(BF16)
            low = early - high.astype(F32)
            low = jnp.where(
                lane_group((half // 2, 128)) < 2, low[: half // 2], turn(low[half // 2 :], 64)
            )
            out_ref[chunk, :half] = high
            out_ref[chunk, half : 2 * half] = late.astype(BF16)
            out_ref[chunk, 2 * half :] = low.astype(BF16)
            if e + k == 0:
                own_ref[:half] = early
                own_ref[half:] = late


def store_signal(x, sig):
    half = x.shape[0]
    product = x * turn(x, 64)
    turned = turn(product, 32)
    odd = lane_group(x.shape) % 2 == 1
    sig[:half] = jnp.where(odd, product, turned)
    sig[half:] = jnp.where(odd, turned, product)


def chunk_rows(core, q_half, step, rows):
    half = rows // 2
    start = half * core if q_half == 0 else half * (1 - core)
    return pl.ds(start + step, half // STEPS, stride=STEPS)


def first_body(
    at_ref, part_ref, own_ref, decay_ref, far_ref, conv_ref, x_ref, late_ref, left_ref, state_ref,
    early_ref, sig, st,
):
    core = at_ref[0]
    rows = sig.shape[0]
    half = rows // 2
    total = own_ref[...]
    low = jnp.zeros((half // 2, 128), F32)
    for k in range(part_ref.shape[0]):
        mine = at_ref[1] == k
        total = total + jnp.where(mine, 0.0, part_ref[k, :rows].astype(F32))
        low = low + jnp.where(mine, 0.0, part_ref[k, rows:].astype(F32))
    low = jnp.concatenate([low, turn(low, 64)], axis=0)
    early = total[:half] + jnp.where(lane_group(low.shape) < 2, low, 0.0)
    x = jnp.where(lane_group(early.shape) < 2, early.astype(BF16).astype(F32), early)
    x_ref[...] = x
    late_ref[...] = total[half:].astype(BF16).astype(F32)
    grads = x * conv_ref[...].astype(F32)
    odd = lane_group(grads.shape) % 2 == 1
    early_ref[...] = jnp.where(odd, grads, turn(grads, 64)).astype(BF16)
    store_signal(x, sig)
    decay = [decay_ref[m : m + 1, :] for m in range(MODE_ROWS)]
    chunks = rows // STEPS
    per = chunks // 2

    def step(i, held):
        t = STEPS - 1 - i
        g = [sig[chunk_rows(core, h, t, rows), :] for h in range(2)]
        return tuple(
            decay[m] * held[2 * m + h] + g[h] for m in range(MODE_ROWS) for h in range(2)
        )

    zero = jnp.zeros((per, 128), F32)
    held = lax.fori_loop(0, STEPS, step, (zero,) * (2 * MODE_ROWS), unroll=8)
    for m in range(MODE_ROWS):
        for h in range(2):
            st[m * chunks + h * per : m * chunks + (h + 1) * per, :] = held[2 * m + h]
    far = far_ref[...]
    acc = jnp.zeros((MODE_ROWS, 128), F32)
    for q in reversed(range(chunks)):
        where = pl.ds(q, MODE_ROWS, stride=chunks)
        left_ref[where, :] = acc
        acc = st[where, :] + far * acc
    state_ref[...] = jnp.broadcast_to(acc[None], state_ref.shape)


def second_body(
    at_ref, x_ref, late_ref, left_ref, states_ref, reach_ref, power_ref, decay_ref, weight_ref,
    out_ref, sig, ys,
):
    core = at_ref[0]
    rows = sig.shape[0]
    half = rows // 2
    chunks = rows // STEPS
    per = chunks // 2
    store_signal(x_ref[...], sig)
    carry = jnp.sum(states_ref[...] * reach_ref[...], axis=0)
    decay = [decay_ref[m : m + 1, :] for m in range(MODE_ROWS)]
    weight = [weight_ref[m : m + 1, :] for m in range(MODE_ROWS)]
    begin = []
    for m in range(MODE_ROWS):
        here = slice(m * chunks, (m + 1) * chunks)
        c = left_ref[here, :] + power_ref[here, :] * carry[m : m + 1, :]
        begin += [c[:per], c[per:]]

    def step(i, held):
        t = STEPS - 1 - i
        new = []
        for h in range(2):
            g = sig[chunk_rows(core, h, t, rows), :]
            states = [decay[m] * held[2 * m + h] + g for m in range(MODE_ROWS)]
            y = weight[0] * states[0]
            for m in range(1, MODE_ROWS):
                y = y + weight[m] * states[m]
            ys[chunk_rows(core, h, t, rows), :] = y
            new.append(states)
        return tuple(new[h][m] for m in range(MODE_ROWS) for h in range(2))

    lax.fori_loop(0, STEPS, step, tuple(begin), unroll=8)
    y = ys[...]
    y = y + turn(y, 64)
    y = y + turn(y, 32)
    odd = lane_group((half, 128)) % 2 == 1
    out = (turn(late_ref[...], 64) * jnp.where(odd, y[half:], y[:half])).astype(BF16)
    for k in range(out_ref.shape[0]):
        out_ref[k] = out


def weigh_body(at_ref, tt_ref, gt_ref, early_a, early_b, early_c, early_d, late_ref, out_ref):
    plane = at_ref[1]
    block = out_ref.shape[1]
    early_refs = (early_a, early_b, early_c, early_d)

    def columns(e):
        early = early_refs[e][...].astype(F32)
        late = late_ref[chunk_of(plane, e)].astype(F32)
        odd = lane_group(early.shape) % 2 == 1
        own = jnp.where(odd, early, late)
        other = turn(jnp.where(odd, late, early), 96)
        return jnp.concatenate([own, other], axis=0).astype(BF16)

    for e in range(0, len(early_refs), 2):
        g = jnp.concatenate([columns(e), columns(e + 1)], axis=1)
        for l in range(2):
            here = slice(l * block, (l + 1) * block)
            from_t = jnp.dot(tt_ref[here, :], g, preferred_element_type=F32)
            from_g = jnp.dot(gt_ref[here, :], g, preferred_element_type=F32)
            both = jnp.where(lane_group(from_t.shape) % GROUPS != 1, from_t, from_g).astype(BF16)
            out_ref[holder(plane, e, l)] = both[:, :128]
            out_ref[holder(plane, e + 1, l)] = both[:, 128:]


def by_lanes(table):
    wide = jnp.repeat(table, 2, axis=1)
    channels = wide.shape[1]
    return wide.reshape(GROUPS, MODE_ROWS, channels).transpose(1, 0, 2).reshape(MODE_ROWS, -1)


def local(tokens, grad_out, in_weight, out_weight, conv_out, residues, decay_length):
    half = tokens.shape[0]
    depth = tokens.shape[1]
    rows = 2 * half
    owned = in_weight.shape[0]
    channels = out_weight.shape[1]
    size_z, size_y, size_x = (lax.axis_size(a) for a in ("seq_0", "seq_1", "chan"))
    chips = size_z * size_y
    core = lax.axis_index("seq_2")
    place = lax.axis_index(CHIPS)

    at = jnp.stack([core, lax.axis_index("chan")]).astype(jnp.int32)

    def transposed(value, to_owner):
        pairs = []
        for z in range(size_z):
            for x in range(size_x):
                j, l = z // 2, z % 2
                held = ((2 * j + OFFSETS[(x - j) % size_x][l]) % size_z) * size_x + j
                owner = z * size_x + x
                pairs.append((held, owner) if to_owner else (owner, held))
        return lax.ppermute(value, ("seq_0", "chan"), pairs)

    def swapped(value):
        return lax.ppermute(value, "seq_2", [(0, 1), (1, 0)])

    piece = call(pack_body, jax.ShapeDtypeStruct((2, owned, 128), BF16), 4)(
        in_hbm(in_weight.transpose(1, 0, 2)), in_hbm(out_weight)
    )
    piece = transposed(piece, False)
    spread = call(spread_body, jax.ShapeDtypeStruct((2 * chips, owned, 128), BF16), 4)(piece)
    weights = lax.all_to_all(spread, SEQ, 0, 0, tiled=True).reshape(size_z, -1, 128)

    tokens_too = swapped(tokens)
    grads_too = swapped(grad_out)
    conv = call(conv_body, jax.ShapeDtypeStruct((half, 128), BF16), 4, inputs=3)(
        at, conv_out, swapped(conv_out)
    )

    pick = residues.shape[1] // 2
    res = jnp.where(core == 0, residues[:, :pick], residues[:, pick:])
    length = jnp.where(core == 0, decay_length[:, :pick], decay_length[:, pick:])
    rate_raw = 1.0 / length
    weight = by_lanes(res * jnp.sqrt(-jnp.expm1(-2.0 * rate_raw)))
    rate = by_lanes(rate_raw)
    decay = jnp.exp(-rate)
    far = jnp.exp(-float(STEPS) * rate)
    chunks = rows // STEPS
    left_of = (chunks - 1 - jnp.arange(chunks)).astype(F32) * float(STEPS)
    power = jnp.exp(-left_of[None, :, None] * rate[:, None, :]).reshape(-1, 128)
    ahead = jnp.arange(chips) - place - 1
    reach = jnp.where(
        (ahead >= 0)[:, None, None],
        jnp.exp(-(jnp.maximum(ahead, 0) * rows).astype(F32)[:, None, None] * rate[None]),
        0.0,
    )

    weights, conv, weight, decay, far, power, reach = lax.optimization_barrier(
        (weights, conv, weight, decay, far, power, reach)
    )
    project = call(
        project_body,
        (jax.ShapeDtypeStruct((size_x, rows + half // 2, 128), BF16), jax.ShapeDtypeStruct((rows, 128), F32)),
        20,
        inputs=6,
        flops=4 * rows * depth * size_x * 128,
        moved=8 * rows * depth,
    )
    parts, own = project(
        at, in_hbm(tokens), in_hbm(tokens_too), in_hbm(grad_out), in_hbm(grads_too), weights
    )
    parts = lax.all_to_all(parts, "chan", 0, 0, tiled=True)

    first = call(
        first_body,
        (
            jax.ShapeDtypeStruct((half, 128), F32),
            jax.ShapeDtypeStruct((half, 128), F32),
            jax.ShapeDtypeStruct((MODE_ROWS * chunks, 128), F32),
            jax.ShapeDtypeStruct((chips, MODE_ROWS, 128), F32),
            jax.ShapeDtypeStruct((half, 128), BF16),
        ),
        10,
        scratch=[pltpu.VMEM((rows, 128), F32), pltpu.VMEM((MODE_ROWS * chunks, 128), F32)],
        inputs=6,
    )
    x, late, left, state, early = first(at, parts, own, decay, far, conv)
    _, *turned = lax.optimization_barrier((left, tokens, tokens_too, grad_out, grads_too))
    turned = [in_hbm(t) for t in turned]
    flip = call(
        transpose_body, jax.ShapeDtypeStruct((depth, rows), BF16), 8, moved=4 * depth * rows
    )
    tokens_t = flip(*turned[:2])
    grads_t = flip(*turned[2:])
    early, tokens_t = lax.optimization_barrier((early, tokens_t))
    early = [early] + [
        lax.ppermute(early, "chan", [(k, (k - e) % size_x) for k in range(size_x)])
        for e in range(1, size_x)
    ]
    states = lax.all_to_all(state, CHIPS, 0, 0, tiled=True)
    states, tokens_t, grads_t, *early = lax.optimization_barrier(
        (states, tokens_t, grads_t, *early)
    )
    second = call(
        second_body,
        jax.ShapeDtypeStruct((size_x, half, 128), BF16),
        10,
        scratch=[pltpu.VMEM((rows, 128), F32), pltpu.VMEM((rows, 128), F32)],
        inputs=9,
    )
    grads = second(at, x, late, left, states, reach, power, decay, weight)
    grads = lax.all_to_all(grads, "chan", 0, 0, tiled=True)

    weigh = call(
        weigh_body,
        jax.ShapeDtypeStruct((size_z, depth // 2, 128), BF16),
        16,
        inputs=8,
        flops=4 * rows * depth * size_x * 128,
        moved=8 * rows * depth,
    )
    partial = weigh(at, tokens_t, grads_t, *early, grads).reshape(2 * chips, owned, 128)
    partial = lax.all_to_all(partial, SEQ, 0, 0, tiled=True)
    total = call(total_body, jax.ShapeDtypeStruct((2, owned, 128), F32), 6)(partial)
    total = transposed(total, True)
    grad_in, grad_proj = call(
        unpack_body,
        (
            jax.ShapeDtypeStruct((3, owned, channels), F32),
            jax.ShapeDtypeStruct((owned, channels), F32),
        ),
        4,
    )(total)
    return (grad_in.transpose(1, 0, 2), grad_proj)


def solution(mesh):
    finer = Mesh(
        mesh.devices.reshape(8, 8, 2, mesh.shape["chan"]), ("seq_0", "seq_1", "seq_2", "chan")
    )
    in_specs = (
        P(SEQ, "chan"),
        P(SEQ, "chan"),
        P(SEQ, None, "chan"),
        P(SEQ, "chan"),
        P(SEQ, "chan"),
        P(None, "chan"),
        P(None, "chan"),
    )
    out_specs = (P(SEQ, None, "chan"), P(SEQ, "chan"))
    return jax.shard_map(local, mesh=finer, in_specs=in_specs, out_specs=out_specs, check_vma=False)
```

```python
import jax
import jax.numpy as jnp
from jax import lax
from jax.experimental import pallas as pl
from jax.experimental.pallas import tpu as pltpu
from jax.sharding import Mesh
from jax.sharding import PartitionSpec as P

SEQ = ("seq_0", "seq_1", "seq_2")
CHIPS = ("seq_0", "seq_1")
STEPS = 64
MODE_ROWS = 4
GROUPS = 4
F32 = jnp.float32
BF16 = jnp.bfloat16
MIB = 1024 * 1024

OFFSETS = ((5, 4), (2, 3), (0, 1), (6, 7))


def call(body, out_shape, mib, scratch=(), flops=0, moved=0, inputs=None):
    specs = {}
    if inputs is not None:
        specs["in_specs"] = [pl.BlockSpec(memory_space=pltpu.SMEM)] + [
            pl.BlockSpec(memory_space=pltpu.VMEM)
        ] * (inputs - 1)
    return pl.pallas_call(
        body,
        out_shape=out_shape,
        scratch_shapes=list(scratch),
        compiler_params=pltpu.CompilerParams(vmem_limit_bytes=mib * MIB),
        cost_estimate=pl.CostEstimate(flops=flops, bytes_accessed=moved, transcendentals=0),
        **specs,
    )


def holder(plane, e, l):
    return lax.rem(2 * plane + OFFSETS[e][l], 2 * len(OFFSETS))


def chunk_of(plane, e):
    return lax.rem(plane + e, len(OFFSETS))


def in_hbm(x):
    return pltpu.with_memory_space_constraint(x, pltpu.HBM)


def lane_group(shape):
    lane = lax.broadcasted_iota(jnp.int32, shape, len(shape) - 1)
    return lane // 32


def turn(x, by):
    return pltpu.roll(x, by, x.ndim - 1)


def transpose_body(a_ref, b_ref, out_ref):
    half = a_ref.shape[0]
    out_ref[:, :half] = a_ref[...].T
    out_ref[:, half:] = b_ref[...].T


def pack_body(in_ref, out_w_ref, out_ref):
    width = out_w_ref.shape[1]
    row = lax.broadcasted_iota(jnp.int32, (width, 128), 0)
    lane = lax.broadcasted_iota(jnp.int32, (width, 128), 1)
    streams = [in_ref[0], in_ref[1], in_ref[2], out_w_ref[...]]
    for half in range(2):
        total = jnp.zeros(out_ref.shape[1:], F32)
        for s, w in enumerate(streams):
            chosen = (lane // 32 == s) & (row == half * 32 + lane % 32)
            total = total + jnp.dot(w, chosen.astype(F32).astype(BF16), preferred_element_type=F32)
        out_ref[half] = total.astype(BF16)


def conv_body(at_ref, own_ref, other_ref, out_ref):
    core = at_ref[0]
    row = lax.broadcasted_iota(jnp.int32, (own_ref.shape[1], 128), 0)
    lane = lax.broadcasted_iota(jnp.int32, (own_ref.shape[1], 128), 1)
    total = jnp.zeros(out_ref.shape, F32)
    for odd, ref in ((1, own_ref), (0, other_ref)):
        chosen = (lane // 32 % 2 == odd) & (row == core * 32 + lane % 32)
        total = total + jnp.dot(
            ref[...], chosen.astype(F32).astype(BF16), preferred_element_type=F32
        )
    out_ref[...] = total.astype(BF16)


def spread_body(piece_ref, out_ref):
    for k in range(out_ref.shape[0]):
        out_ref[k] = piece_ref[k % 2]


def total_body(part_ref, out_ref):
    owned = out_ref.shape[1]
    total = part_ref[0].astype(F32)
    for k in range(1, part_ref.shape[0]):
        total = total + part_ref[k].astype(F32)
    out_ref[0] = total[:owned]
    out_ref[1] = total[owned:]


def unpack_body(part_ref, in_ref, out_w_ref):
    low = part_ref[0]
    high = part_ref[1]
    for s, group in enumerate((0, 3, 2, 1)):
        left = low if group == 0 else turn(low, 128 - 32 * group)
        right = high if group == 1 else turn(high, (160 - 32 * group) % 128)
        both = jnp.where(lane_group(low.shape) == 0, left, right)[:, : out_w_ref.shape[1]]
        if s < 3:
            in_ref[s] = both
        else:
            out_w_ref[...] = both


def project_body(at_ref, own_t, other_t, own_g, other_g, w_ref, out_ref, own_ref):
    plane = at_ref[1]
    half = own_t.shape[0]

    def columns(e):
        return jnp.concatenate([w_ref[holder(plane, e, l)] for l in range(2)], axis=0)

    for e in range(0, out_ref.shape[0], 2):
        w = jnp.concatenate([columns(e), columns(e + 1)], axis=1)
        both = []
        for t_ref, g_ref in ((own_t, own_g), (other_t, other_g)):
            from_t = jnp.dot(t_ref[...], w, preferred_element_type=F32)
            from_g = jnp.dot(g_ref[...], w, preferred_element_type=F32)
            both.append(jnp.where(lane_group(from_t.shape) % GROUPS < 3, from_t, from_g))
        for k in range(2):
            own, other = (b[:, 128 * k : 128 * (k + 1)] for b in both)
            odd = lane_group(own.shape) % 2 == 1
            chunk = chunk_of(plane, e + k)
            early = jnp.where(odd, own, turn(other, 96))
            late = jnp.where(odd, turn(other, 32), own)
            high = early.astype(BF16)
            low = early - high.astype(F32)
            low = jnp.where(
                lane_group((half // 2, 128)) < 2, low[: half // 2], turn(low[half // 2 :], 64)
            )
            out_ref[chunk, :half] = high
            out_ref[chunk, half : 2 * half] = late.astype(BF16)
            out_ref[chunk, 2 * half :] = low.astype(BF16)
            if e + k == 0:
                own_ref[:half] = early
                own_ref[half:] = late


def store_signal(x, sig):
    half = x.shape[0]
    product = x * turn(x, 64)
    turned = turn(product, 32)
    odd = lane_group(x.shape) % 2 == 1
    sig[:half] = jnp.where(odd, product, turned)
    sig[half:] = jnp.where(odd, turned, product)


def chunk_rows(core, q_half, step, rows):
    half = rows // 2
    start = half * core if q_half == 0 else half * (1 - core)
    return pl.ds(start + step, half // STEPS, stride=STEPS)


def first_body(
    at_ref, part_ref, own_ref, decay_ref, far_ref, x_ref, late_ref, left_ref, state_ref, sig, st
):
    core = at_ref[0]
    rows = sig.shape[0]
    half = rows // 2
    total = own_ref[...]
    low = jnp.zeros((half // 2, 128), F32)
    for k in range(part_ref.shape[0]):
        mine = at_ref[1] == k
        total = total + jnp.where(mine, 0.0, part_ref[k, :rows].astype(F32))
        low = low + jnp.where(mine, 0.0, part_ref[k, rows:].astype(F32))
    low = jnp.concatenate([low, turn(low, 64)], axis=0)
    early = total[:half] + jnp.where(lane_group(low.shape) < 2, low, 0.0)
    x = jnp.where(lane_group(early.shape) < 2, early.astype(BF16).astype(F32), early)
    x_ref[...] = x
    late_ref[...] = total[half:].astype(BF16).astype(F32)
    store_signal(x, sig)
    decay = [decay_ref[m : m + 1, :] for m in range(MODE_ROWS)]
    chunks = rows // STEPS
    per = chunks // 2

    def step(i, held):
        t = STEPS - 1 - i
        g = [sig[chunk_rows(core, h, t, rows), :] for h in range(2)]
        return tuple(
            decay[m] * held[2 * m + h] + g[h] for m in range(MODE_ROWS) for h in range(2)
        )

    zero = jnp.zeros((per, 128), F32)
    held = lax.fori_loop(0, STEPS, step, (zero,) * (2 * MODE_ROWS), unroll=8)
    for m in range(MODE_ROWS):
        for h in range(2):
            st[m * chunks + h * per : m * chunks + (h + 1) * per, :] = held[2 * m + h]
    far = far_ref[...]
    acc = jnp.zeros((MODE_ROWS, 128), F32)
    for q in reversed(range(chunks)):
        where = pl.ds(q, MODE_ROWS, stride=chunks)
        left_ref[where, :] = acc
        acc = st[where, :] + far * acc
    state_ref[...] = jnp.broadcast_to(acc[None], state_ref.shape)


def second_body(
    at_ref, x_ref, late_ref, left_ref, states_ref, reach_ref, power_ref, decay_ref, weight_ref,
    conv_ref, out_ref, sig, ys,
):
    core = at_ref[0]
    rows = sig.shape[0]
    half = rows // 2
    chunks = rows // STEPS
    per = chunks // 2
    store_signal(x_ref[...], sig)
    carry = jnp.sum(states_ref[...] * reach_ref[...], axis=0)
    decay = [decay_ref[m : m + 1, :] for m in range(MODE_ROWS)]
    weight = [weight_ref[m : m + 1, :] for m in range(MODE_ROWS)]
    begin = []
    for m in range(MODE_ROWS):
        here = slice(m * chunks, (m + 1) * chunks)
        c = left_ref[here, :] + power_ref[here, :] * carry[m : m + 1, :]
        begin += [c[:per], c[per:]]

    def step(i, held):
        t = STEPS - 1 - i
        new = []
        for h in range(2):
            g = sig[chunk_rows(core, h, t, rows), :]
            states = [decay[m] * held[2 * m + h] + g for m in range(MODE_ROWS)]
            y = weight[0] * states[0]
            for m in range(1, MODE_ROWS):
                y = y + weight[m] * states[m]
            ys[chunk_rows(core, h, t, rows), :] = y
            new.append(states)
        return tuple(new[h][m] for m in range(MODE_ROWS) for h in range(2))

    lax.fori_loop(0, STEPS, step, tuple(begin), unroll=8)
    y = ys[...]
    y = y + turn(y, 64)
    y = y + turn(y, 32)
    odd = lane_group((half, 128)) % 2 == 1
    late = turn(late_ref[...], 64) * jnp.where(odd, y[half:], y[:half])
    early = x_ref[...] * conv_ref[...].astype(F32)
    own = jnp.where(odd, early, late)
    other = turn(jnp.where(odd, late, turn(early, 64)), 96)
    out = jnp.concatenate([own, other], axis=0).astype(BF16)
    for k in range(out_ref.shape[0]):
        out_ref[k] = out


def weigh_body(at_ref, tt_ref, gt_ref, grads_ref, out_ref):
    plane = at_ref[1]
    block = out_ref.shape[1]
    for l in range(2):
        r = l * block
        for c in range(0, grads_ref.shape[0], 2):
            g = jnp.concatenate([grads_ref[chunk_of(plane, c + k)] for k in range(2)], axis=1)
            from_t = jnp.dot(tt_ref[r : r + block, :], g, preferred_element_type=F32)
            from_g = jnp.dot(gt_ref[r : r + block, :], g, preferred_element_type=F32)
            both = jnp.where(lane_group(from_t.shape) % GROUPS != 1, from_t, from_g).astype(BF16)
            out_ref[holder(plane, c, l)] = both[:, :128]
            out_ref[holder(plane, c + 1, l)] = both[:, 128:]


def by_lanes(table):
    wide = jnp.repeat(table, 2, axis=1)
    channels = wide.shape[1]
    return wide.reshape(GROUPS, MODE_ROWS, channels).transpose(1, 0, 2).reshape(MODE_ROWS, -1)


def local(tokens, grad_out, in_weight, out_weight, conv_out, residues, decay_length):
    half = tokens.shape[0]
    depth = tokens.shape[1]
    rows = 2 * half
    owned = in_weight.shape[0]
    channels = out_weight.shape[1]
    size_z, size_y, size_x = (lax.axis_size(a) for a in ("seq_0", "seq_1", "chan"))
    chips = size_z * size_y
    core = lax.axis_index("seq_2")
    place = lax.axis_index(CHIPS)

    at = jnp.stack([core, lax.axis_index("chan")]).astype(jnp.int32)

    def transposed(value, to_owner):
        pairs = []
        for z in range(size_z):
            for x in range(size_x):
                j, l = z // 2, z % 2
                held = ((2 * j + OFFSETS[(x - j) % size_x][l]) % size_z) * size_x + j
                owner = z * size_x + x
                pairs.append((held, owner) if to_owner else (owner, held))
        return lax.ppermute(value, ("seq_0", "chan"), pairs)

    def swapped(value):
        return lax.ppermute(value, "seq_2", [(0, 1), (1, 0)])

    piece = call(pack_body, jax.ShapeDtypeStruct((2, owned, 128), BF16), 4)(
        in_hbm(in_weight.transpose(1, 0, 2)), in_hbm(out_weight)
    )
    piece = transposed(piece, False)
    spread = call(spread_body, jax.ShapeDtypeStruct((2 * chips, owned, 128), BF16), 4)(piece)
    weights = lax.all_to_all(spread, SEQ, 0, 0, tiled=True).reshape(size_z, -1, 128)

    tokens_too = swapped(tokens)
    grads_too = swapped(grad_out)
    conv = call(conv_body, jax.ShapeDtypeStruct((half, 128), BF16), 4, inputs=3)(
        at, conv_out, swapped(conv_out)
    )

    pick = residues.shape[1] // 2
    res = jnp.where(core == 0, residues[:, :pick], residues[:, pick:])
    length = jnp.where(core == 0, decay_length[:, :pick], decay_length[:, pick:])
    rate_raw = 1.0 / length
    weight = by_lanes(res * jnp.sqrt(-jnp.expm1(-2.0 * rate_raw)))
    rate = by_lanes(rate_raw)
    decay = jnp.exp(-rate)
    far = jnp.exp(-float(STEPS) * rate)
    chunks = rows // STEPS
    left_of = (chunks - 1 - jnp.arange(chunks)).astype(F32) * float(STEPS)
    power = jnp.exp(-left_of[None, :, None] * rate[:, None, :]).reshape(-1, 128)
    ahead = jnp.arange(chips) - place - 1
    reach = jnp.where(
        (ahead >= 0)[:, None, None],
        jnp.exp(-(jnp.maximum(ahead, 0) * rows).astype(F32)[:, None, None] * rate[None]),
        0.0,
    )

    weights, conv, weight, decay, far, power, reach = lax.optimization_barrier(
        (weights, conv, weight, decay, far, power, reach)
    )
    project = call(
        project_body,
        (jax.ShapeDtypeStruct((size_x, rows + half // 2, 128), BF16), jax.ShapeDtypeStruct((rows, 128), F32)),
        20,
        inputs=6,
        flops=4 * rows * depth * size_x * 128,
        moved=8 * rows * depth,
    )
    parts, own = project(
        at, tokens, in_hbm(tokens_too), grad_out, in_hbm(grads_too), weights
    )
    parts = lax.all_to_all(parts, "chan", 0, 0, tiled=True)

    first = call(
        first_body,
        (
            jax.ShapeDtypeStruct((half, 128), F32),
            jax.ShapeDtypeStruct((half, 128), F32),
            jax.ShapeDtypeStruct((MODE_ROWS * chunks, 128), F32),
            jax.ShapeDtypeStruct((chips, MODE_ROWS, 128), F32),
        ),
        10,
        scratch=[pltpu.VMEM((rows, 128), F32), pltpu.VMEM((MODE_ROWS * chunks, 128), F32)],
        inputs=5,
    )
    x, late, left, state = first(at, parts, own, decay, far)
    _, *turned = lax.optimization_barrier((left, tokens, tokens_too, grad_out, grads_too))
    turned = [in_hbm(t) for t in turned]
    flip = call(
        transpose_body, jax.ShapeDtypeStruct((depth, rows), BF16), 8, moved=4 * depth * rows
    )
    tokens_t = flip(*turned[:2])
    grads_t = flip(*turned[2:])
    states = lax.all_to_all(state, CHIPS, 0, 0, tiled=True)
    states, tokens_t, grads_t = lax.optimization_barrier((states, tokens_t, grads_t))
    second = call(
        second_body,
        jax.ShapeDtypeStruct((size_x, rows, 128), BF16),
        10,
        scratch=[pltpu.VMEM((rows, 128), F32), pltpu.VMEM((rows, 128), F32)],
        inputs=10,
    )
    grads = second(at, x, late, left, states, reach, power, decay, weight, conv)
    grads = lax.all_to_all(grads, "chan", 0, 0, tiled=True)

    weigh = call(
        weigh_body,
        pltpu.HBM((size_z, depth // 2, 128), BF16),
        16,
        inputs=4,
        flops=4 * rows * depth * size_x * 128,
        moved=8 * rows * depth,
    )
    partial = weigh(at, tokens_t, grads_t, grads).reshape(chips, 2 * owned, 128)
    partial = in_hbm(lax.all_to_all(partial, CHIPS, 0, 0, tiled=True))
    total = call(total_body, jax.ShapeDtypeStruct((2, owned, 128), F32), 6)(partial)
    total = lax.all_to_all(total, "seq_2", 0, 0, tiled=True)
    total = transposed(total, True)
    grad_in, grad_proj = call(
        unpack_body,
        (
            jax.ShapeDtypeStruct((3, owned, channels), F32),
            jax.ShapeDtypeStruct((owned, channels), F32),
        ),
        4,
    )(total)
    return (grad_in.transpose(1, 0, 2), grad_proj)


def solution(mesh):
    finer = Mesh(
        mesh.devices.reshape(8, 8, 2, mesh.shape["chan"]), ("seq_0", "seq_1", "seq_2", "chan")
    )
    in_specs = (
        P(SEQ, "chan"),
        P(SEQ, "chan"),
        P(SEQ, None, "chan"),
        P(SEQ, "chan"),
        P(SEQ, "chan"),
        P(None, "chan"),
        P(None, "chan"),
    )
    out_specs = (P(SEQ, None, "chan"), P(SEQ, "chan"))
    return jax.shard_map(local, mesh=finer, in_specs=in_specs, out_specs=out_specs, check_vma=False)
```

```python
import jax
import jax.numpy as jnp
from jax import lax
from jax.experimental import pallas as pl
from jax.experimental.pallas import tpu as pltpu
from jax.sharding import Mesh
from jax.sharding import PartitionSpec as P

SEQ = ("seq_0", "seq_1", "seq_2")
CHIPS = ("seq_0", "seq_1")
STEPS = 64
MODE_ROWS = 4
GROUPS = 4
F32 = jnp.float32
BF16 = jnp.bfloat16
MIB = 1024 * 1024

OFFSETS = ((5, 4), (2, 3), (0, 1), (6, 7))


def call(body, out_shape, mib, scratch=(), flops=0, moved=0, inputs=None):
    specs = {}
    if inputs is not None:
        specs["in_specs"] = [pl.BlockSpec(memory_space=pltpu.SMEM)] + [
            pl.BlockSpec(memory_space=pltpu.VMEM)
        ] * (inputs - 1)
    return pl.pallas_call(
        body,
        out_shape=out_shape,
        scratch_shapes=list(scratch),
        compiler_params=pltpu.CompilerParams(vmem_limit_bytes=mib * MIB),
        cost_estimate=pl.CostEstimate(flops=flops, bytes_accessed=moved, transcendentals=0),
        **specs,
    )


def holder(plane, e, l):
    return lax.rem(2 * plane + OFFSETS[e][l], 2 * len(OFFSETS))


def chunk_of(plane, e):
    return lax.rem(plane + e, len(OFFSETS))


def in_hbm(x):
    return pltpu.with_memory_space_constraint(x, pltpu.HBM)


def lane_group(shape):
    lane = lax.broadcasted_iota(jnp.int32, shape, len(shape) - 1)
    return lane // 32


def turn(x, by):
    return pltpu.roll(x, by, x.ndim - 1)


def transpose_body(a_ref, b_ref, out_ref):
    half = a_ref.shape[0]
    out_ref[:, :half] = a_ref[...].T
    out_ref[:, half:] = b_ref[...].T


def pack_body(in_ref, out_w_ref, out_ref):
    width = out_w_ref.shape[1]
    row = lax.broadcasted_iota(jnp.int32, (width, 128), 0)
    lane = lax.broadcasted_iota(jnp.int32, (width, 128), 1)
    streams = [in_ref[0], in_ref[1], in_ref[2], out_w_ref[...]]
    for half in range(2):
        total = jnp.zeros(out_ref.shape[1:], F32)
        for s, w in enumerate(streams):
            chosen = (lane // 32 == s) & (row == half * 32 + lane % 32)
            total = total + jnp.dot(w, chosen.astype(F32).astype(BF16), preferred_element_type=F32)
        out_ref[half] = total.astype(BF16)


def conv_body(at_ref, own_ref, other_ref, out_ref):
    core = at_ref[0]
    row = lax.broadcasted_iota(jnp.int32, (own_ref.shape[1], 128), 0)
    lane = lax.broadcasted_iota(jnp.int32, (own_ref.shape[1], 128), 1)
    total = jnp.zeros(out_ref.shape, F32)
    for odd, ref in ((1, own_ref), (0, other_ref)):
        chosen = (lane // 32 % 2 == odd) & (row == core * 32 + lane % 32)
        total = total + jnp.dot(
            ref[...], chosen.astype(F32).astype(BF16), preferred_element_type=F32
        )
    out_ref[...] = total.astype(BF16)


def spread_body(piece_ref, out_ref):
    for k in range(out_ref.shape[0]):
        out_ref[k] = piece_ref[k % 2]


def total_body(part_ref, out_ref):
    owned = out_ref.shape[1]
    total = part_ref[0].astype(F32)
    for k in range(1, part_ref.shape[0]):
        total = total + part_ref[k].astype(F32)
    out_ref[0] = total[:owned]
    out_ref[1] = total[owned:]


def unpack_body(part_ref, in_ref, out_w_ref):
    low = part_ref[0]
    high = part_ref[1]
    for s, group in enumerate((0, 3, 2, 1)):
        left = low if group == 0 else turn(low, 128 - 32 * group)
        right = high if group == 1 else turn(high, (160 - 32 * group) % 128)
        both = jnp.where(lane_group(low.shape) == 0, left, right)[:, : out_w_ref.shape[1]]
        if s < 3:
            in_ref[s] = both
        else:
            out_w_ref[...] = both


def project_body(at_ref, own_t, other_t, own_g, other_g, w_ref, out_ref, own_ref):
    plane = at_ref[1]
    half = own_t.shape[0]

    def columns(e):
        return jnp.concatenate([w_ref[holder(plane, e, l)] for l in range(2)], axis=0)

    for e in range(0, out_ref.shape[0], 2):
        w = jnp.concatenate([columns(e), columns(e + 1)], axis=1)
        both = []
        for t_ref, g_ref in ((own_t, own_g), (other_t, other_g)):
            from_t = jnp.dot(t_ref[...], w, preferred_element_type=F32)
            from_g = jnp.dot(g_ref[...], w, preferred_element_type=F32)
            both.append(jnp.where(lane_group(from_t.shape) % GROUPS < 3, from_t, from_g))
        for k in range(2):
            own, other = (b[:, 128 * k : 128 * (k + 1)] for b in both)
            odd = lane_group(own.shape) % 2 == 1
            chunk = chunk_of(plane, e + k)
            early = jnp.where(odd, own, turn(other, 96))
            late = jnp.where(odd, turn(other, 32), own)
            high = early.astype(BF16)
            low = early - high.astype(F32)
            low = jnp.where(
                lane_group((half // 2, 128)) < 2, low[: half // 2], turn(low[half // 2 :], 64)
            )
            out_ref[chunk, :half] = high
            out_ref[chunk, half : 2 * half] = late.astype(BF16)
            out_ref[chunk, 2 * half :] = low.astype(BF16)
            if e + k == 0:
                own_ref[:half] = early
                own_ref[half:] = late


def store_signal(x, sig):
    half = x.shape[0]
    product = x * turn(x, 64)
    turned = turn(product, 32)
    odd = lane_group(x.shape) % 2 == 1
    sig[:half] = jnp.where(odd, product, turned)
    sig[half:] = jnp.where(odd, turned, product)


def chunk_rows(core, q_half, step, rows):
    half = rows // 2
    start = half * core if q_half == 0 else half * (1 - core)
    return pl.ds(start + step, half // STEPS, stride=STEPS)


def first_body(
    at_ref, part_ref, own_ref, decay_ref, far_ref, x_ref, late_ref, left_ref, state_ref, sig, st
):
    core = at_ref[0]
    rows = sig.shape[0]
    half = rows // 2
    total = own_ref[...]
    low = jnp.zeros((half // 2, 128), F32)
    for k in range(part_ref.shape[0]):
        mine = at_ref[1] == k
        total = total + jnp.where(mine, 0.0, part_ref[k, :rows].astype(F32))
        low = low + jnp.where(mine, 0.0, part_ref[k, rows:].astype(F32))
    low = jnp.concatenate([low, turn(low, 64)], axis=0)
    early = total[:half] + jnp.where(lane_group(low.shape) < 2, low, 0.0)
    x = jnp.where(lane_group(early.shape) < 2, early.astype(BF16).astype(F32), early)
    x_ref[...] = x
    late_ref[...] = total[half:].astype(BF16).astype(F32)
    store_signal(x, sig)
    decay = [decay_ref[m : m + 1, :] for m in range(MODE_ROWS)]
    chunks = rows // STEPS
    per = chunks // 2

    def step(i, held):
        t = STEPS - 1 - i
        g = [sig[chunk_rows(core, h, t, rows), :] for h in range(2)]
        return tuple(
            decay[m] * held[2 * m + h] + g[h] for m in range(MODE_ROWS) for h in range(2)
        )

    zero = jnp.zeros((per, 128), F32)
    held = lax.fori_loop(0, STEPS, step, (zero,) * (2 * MODE_ROWS), unroll=8)
    for m in range(MODE_ROWS):
        for h in range(2):
            st[m * chunks + h * per : m * chunks + (h + 1) * per, :] = held[2 * m + h]
    far = far_ref[...]
    acc = jnp.zeros((MODE_ROWS, 128), F32)
    for q in reversed(range(chunks)):
        where = pl.ds(q, MODE_ROWS, stride=chunks)
        left_ref[where, :] = acc
        acc = st[where, :] + far * acc
    state_ref[...] = jnp.broadcast_to(acc[None], state_ref.shape)


def second_body(
    at_ref, x_ref, late_ref, left_ref, states_ref, reach_ref, power_ref, decay_ref, weight_ref,
    conv_ref, out_ref, sig, ys,
):
    core = at_ref[0]
    rows = sig.shape[0]
    half = rows // 2
    chunks = rows // STEPS
    per = chunks // 2
    store_signal(x_ref[...], sig)
    carry = jnp.sum(states_ref[...] * reach_ref[...], axis=0)
    decay = [decay_ref[m : m + 1, :] for m in range(MODE_ROWS)]
    weight = [weight_ref[m : m + 1, :] for m in range(MODE_ROWS)]
    begin = []
    for m in range(MODE_ROWS):
        here = slice(m * chunks, (m + 1) * chunks)
        c = left_ref[here, :] + power_ref[here, :] * carry[m : m + 1, :]
        begin += [c[:per], c[per:]]

    def step(i, held):
        t = STEPS - 1 - i
        new = []
        for h in range(2):
            g = sig[chunk_rows(core, h, t, rows), :]
            states = [decay[m] * held[2 * m + h] + g for m in range(MODE_ROWS)]
            y = weight[0] * states[0]
            for m in range(1, MODE_ROWS):
                y = y + weight[m] * states[m]
            ys[chunk_rows(core, h, t, rows), :] = y
            new.append(states)
        return tuple(new[h][m] for m in range(MODE_ROWS) for h in range(2))

    lax.fori_loop(0, STEPS, step, tuple(begin), unroll=8)
    y = ys[...]
    y = y + turn(y, 64)
    y = y + turn(y, 32)
    odd = lane_group((half, 128)) % 2 == 1
    late = turn(late_ref[...], 64) * jnp.where(odd, y[half:], y[:half])
    early = x_ref[...] * conv_ref[...].astype(F32)
    own = jnp.where(odd, early, late)
    other = turn(jnp.where(odd, late, turn(early, 64)), 96)
    out = jnp.concatenate([own, other], axis=0).astype(BF16)
    for k in range(out_ref.shape[0]):
        out_ref[k] = out


def weigh_body(at_ref, tt_ref, gt_ref, grads_ref, out_ref):
    plane = at_ref[1]
    block = out_ref.shape[1]
    for l in range(2):
        r = l * block
        for c in range(0, grads_ref.shape[0], 2):
            g = jnp.concatenate([grads_ref[chunk_of(plane, c + k)] for k in range(2)], axis=1)
            from_t = jnp.dot(tt_ref[r : r + block, :], g, preferred_element_type=F32)
            from_g = jnp.dot(gt_ref[r : r + block, :], g, preferred_element_type=F32)
            both = jnp.where(lane_group(from_t.shape) % GROUPS != 1, from_t, from_g).astype(BF16)
            out_ref[holder(plane, c, l)] = both[:, :128]
            out_ref[holder(plane, c + 1, l)] = both[:, 128:]


def by_lanes(table):
    wide = jnp.repeat(table, 2, axis=1)
    channels = wide.shape[1]
    return wide.reshape(GROUPS, MODE_ROWS, channels).transpose(1, 0, 2).reshape(MODE_ROWS, -1)


def local(tokens, grad_out, in_weight, out_weight, conv_out, residues, decay_length):
    half = tokens.shape[0]
    depth = tokens.shape[1]
    rows = 2 * half
    owned = in_weight.shape[0]
    channels = out_weight.shape[1]
    size_z, size_y, size_x = (lax.axis_size(a) for a in ("seq_0", "seq_1", "chan"))
    chips = size_z * size_y
    core = lax.axis_index("seq_2")
    place = lax.axis_index(CHIPS)

    at = jnp.stack([core, lax.axis_index("chan")]).astype(jnp.int32)

    def transposed(value, to_owner):
        pairs = []
        for z in range(size_z):
            for x in range(size_x):
                j, l = z // 2, z % 2
                held = ((2 * j + OFFSETS[(x - j) % size_x][l]) % size_z) * size_x + j
                owner = z * size_x + x
                pairs.append((held, owner) if to_owner else (owner, held))
        return lax.ppermute(value, ("seq_0", "chan"), pairs)

    def swapped(value):
        return lax.ppermute(value, "seq_2", [(0, 1), (1, 0)])

    piece = call(pack_body, jax.ShapeDtypeStruct((2, owned, 128), BF16), 4)(
        in_hbm(in_weight.transpose(1, 0, 2)), in_hbm(out_weight)
    )
    piece = transposed(piece, False)
    spread = call(spread_body, jax.ShapeDtypeStruct((2 * chips, owned, 128), BF16), 4)(piece)
    weights = lax.all_to_all(spread, SEQ, 0, 0, tiled=True).reshape(size_z, -1, 128)

    tokens_too = swapped(tokens)
    grads_too = swapped(grad_out)
    conv = call(conv_body, jax.ShapeDtypeStruct((half, 128), BF16), 4, inputs=3)(
        at, conv_out, swapped(conv_out)
    )

    pick = residues.shape[1] // 2
    res = jnp.where(core == 0, residues[:, :pick], residues[:, pick:])
    length = jnp.where(core == 0, decay_length[:, :pick], decay_length[:, pick:])
    rate_raw = 1.0 / length
    weight = by_lanes(res * jnp.sqrt(-jnp.expm1(-2.0 * rate_raw)))
    rate = by_lanes(rate_raw)
    decay = jnp.exp(-rate)
    far = jnp.exp(-float(STEPS) * rate)
    chunks = rows // STEPS
    left_of = (chunks - 1 - jnp.arange(chunks)).astype(F32) * float(STEPS)
    power = jnp.exp(-left_of[None, :, None] * rate[:, None, :]).reshape(-1, 128)
    ahead = jnp.arange(chips) - place - 1
    reach = jnp.where(
        (ahead >= 0)[:, None, None],
        jnp.exp(-(jnp.maximum(ahead, 0) * rows).astype(F32)[:, None, None] * rate[None]),
        0.0,
    )

    weights, conv, weight, decay, far, power, reach = lax.optimization_barrier(
        (weights, conv, weight, decay, far, power, reach)
    )
    project = call(
        project_body,
        (jax.ShapeDtypeStruct((size_x, rows + half // 2, 128), BF16), jax.ShapeDtypeStruct((rows, 128), F32)),
        20,
        inputs=6,
        flops=4 * rows * depth * size_x * 128,
        moved=8 * rows * depth,
    )
    parts, own = project(
        at, tokens, in_hbm(tokens_too), grad_out, in_hbm(grads_too), weights
    )
    parts = lax.all_to_all(parts, "chan", 0, 0, tiled=True)

    first = call(
        first_body,
        (
            jax.ShapeDtypeStruct((half, 128), F32),
            jax.ShapeDtypeStruct((half, 128), F32),
            jax.ShapeDtypeStruct((MODE_ROWS * chunks, 128), F32),
            jax.ShapeDtypeStruct((chips, MODE_ROWS, 128), F32),
        ),
        10,
        scratch=[pltpu.VMEM((rows, 128), F32), pltpu.VMEM((MODE_ROWS * chunks, 128), F32)],
        inputs=5,
    )
    x, late, left, state = first(at, parts, own, decay, far)
    _, *turned = lax.optimization_barrier((left, tokens, tokens_too, grad_out, grads_too))
    turned = [in_hbm(t) for t in turned]
    flip = call(
        transpose_body, jax.ShapeDtypeStruct((depth, rows), BF16), 8, moved=4 * depth * rows
    )
    tokens_t = flip(*turned[:2])
    grads_t = flip(*turned[2:])
    states = lax.all_to_all(state, CHIPS, 0, 0, tiled=True)
    states, tokens_t, grads_t = lax.optimization_barrier((states, tokens_t, grads_t))
    second = call(
        second_body,
        jax.ShapeDtypeStruct((size_x, rows, 128), BF16),
        10,
        scratch=[pltpu.VMEM((rows, 128), F32), pltpu.VMEM((rows, 128), F32)],
        inputs=10,
    )
    grads = second(at, x, late, left, states, reach, power, decay, weight, conv)
    grads = lax.all_to_all(grads, "chan", 0, 0, tiled=True)

    weigh = call(
        weigh_body,
        jax.ShapeDtypeStruct((size_z, depth // 2, 128), BF16),
        16,
        inputs=4,
        flops=4 * rows * depth * size_x * 128,
        moved=8 * rows * depth,
    )
    partial = weigh(at, tokens_t, grads_t, grads).reshape(chips, 2 * owned, 128)
    partial = lax.all_to_all(partial, CHIPS, 0, 0, tiled=True)
    total = call(total_body, jax.ShapeDtypeStruct((2, owned, 128), F32), 6)(partial)
    total = lax.all_to_all(total, "seq_2", 0, 0, tiled=True)
    total = transposed(total, True)
    grad_in, grad_proj = call(
        unpack_body,
        (
            jax.ShapeDtypeStruct((3, owned, channels), F32),
            jax.ShapeDtypeStruct((owned, channels), F32),
        ),
        4,
    )(total)
    return (grad_in.transpose(1, 0, 2), grad_proj)


def solution(mesh):
    finer = Mesh(
        mesh.devices.reshape(8, 8, 2, mesh.shape["chan"]), ("seq_0", "seq_1", "seq_2", "chan")
    )
    in_specs = (
        P(SEQ, "chan"),
        P(SEQ, "chan"),
        P(SEQ, None, "chan"),
        P(SEQ, "chan"),
        P(SEQ, "chan"),
        P(None, "chan"),
        P(None, "chan"),
    )
    out_specs = (P(SEQ, None, "chan"), P(SEQ, "chan"))
    return jax.shard_map(local, mesh=finer, in_specs=in_specs, out_specs=out_specs, check_vma=False)
```

```python
import jax
import jax.numpy as jnp
from jax import lax
from jax.experimental import pallas as pl
from jax.experimental.pallas import tpu as pltpu
from jax.sharding import Mesh
from jax.sharding import PartitionSpec as P

SEQ = ("seq_0", "seq_1", "seq_2")
CHIPS = ("seq_0", "seq_1")
STEPS = 64
MODE_ROWS = 4
GROUPS = 4
F32 = jnp.float32
BF16 = jnp.bfloat16
MIB = 1024 * 1024

OFFSETS = ((5, 4), (2, 3), (0, 1), (6, 7))


def call(body, out_shape, mib, scratch=(), flops=0, moved=0, inputs=None):
    specs = {}
    if inputs is not None:
        specs["in_specs"] = [pl.BlockSpec(memory_space=pltpu.SMEM)] + [
            pl.BlockSpec(memory_space=pltpu.VMEM)
        ] * (inputs - 1)
    return pl.pallas_call(
        body,
        out_shape=out_shape,
        scratch_shapes=list(scratch),
        compiler_params=pltpu.CompilerParams(vmem_limit_bytes=mib * MIB),
        cost_estimate=pl.CostEstimate(flops=flops, bytes_accessed=moved, transcendentals=0),
        **specs,
    )


def holder(plane, e, l):
    return lax.rem(2 * plane + OFFSETS[e][l], 2 * len(OFFSETS))


def chunk_of(plane, e):
    return lax.rem(plane + e, len(OFFSETS))


def in_hbm(x):
    return pltpu.with_memory_space_constraint(x, pltpu.HBM)


def lane_group(shape):
    lane = lax.broadcasted_iota(jnp.int32, shape, len(shape) - 1)
    return lane // 32


def turn(x, by):
    return pltpu.roll(x, by, x.ndim - 1)


def transpose_body(a_ref, b_ref, out_ref):
    half = a_ref.shape[0]
    out_ref[:, :half] = a_ref[...].T
    out_ref[:, half:] = b_ref[...].T


def pack_body(in_ref, out_w_ref, out_ref):
    width = out_w_ref.shape[1]
    row = lax.broadcasted_iota(jnp.int32, (width, 128), 0)
    lane = lax.broadcasted_iota(jnp.int32, (width, 128), 1)
    streams = [in_ref[0], in_ref[1], in_ref[2], out_w_ref[...]]
    for half in range(2):
        total = jnp.zeros(out_ref.shape[1:], F32)
        for s, w in enumerate(streams):
            chosen = (lane // 32 == s) & (row == half * 32 + lane % 32)
            total = total + jnp.dot(w, chosen.astype(F32).astype(BF16), preferred_element_type=F32)
        out_ref[half] = total.astype(BF16)


def conv_body(at_ref, own_ref, other_ref, out_ref):
    core = at_ref[0]
    row = lax.broadcasted_iota(jnp.int32, (own_ref.shape[1], 128), 0)
    lane = lax.broadcasted_iota(jnp.int32, (own_ref.shape[1], 128), 1)
    total = jnp.zeros(out_ref.shape, F32)
    for odd, ref in ((1, own_ref), (0, other_ref)):
        chosen = (lane // 32 % 2 == odd) & (row == core * 32 + lane % 32)
        total = total + jnp.dot(
            ref[...], chosen.astype(F32).astype(BF16), preferred_element_type=F32
        )
    out_ref[...] = total.astype(BF16)


def spread_body(piece_ref, out_ref):
    for k in range(out_ref.shape[0]):
        out_ref[k] = piece_ref[k % 2]


def total_body(part_ref, out_ref):
    owned = out_ref.shape[1]
    total = part_ref[0].astype(F32)
    for k in range(1, part_ref.shape[0]):
        total = total + part_ref[k].astype(F32)
    out_ref[0] = total[:owned]
    out_ref[1] = total[owned:]


def unpack_body(part_ref, in_ref, out_w_ref):
    low = part_ref[0]
    high = part_ref[1]
    for s, group in enumerate((0, 3, 2, 1)):
        left = low if group == 0 else turn(low, 128 - 32 * group)
        right = high if group == 1 else turn(high, (160 - 32 * group) % 128)
        both = jnp.where(lane_group(low.shape) == 0, left, right)[:, : out_w_ref.shape[1]]
        if s < 3:
            in_ref[s] = both
        else:
            out_w_ref[...] = both


def project_body(at_ref, own_t, other_t, own_g, other_g, w_ref, out_ref, own_ref):
    plane = at_ref[1]
    half = own_t.shape[0]

    def columns(e):
        return jnp.concatenate([w_ref[holder(plane, e, l)] for l in range(2)], axis=0)

    for e in range(0, out_ref.shape[0], 2):
        w = jnp.concatenate([columns(e), columns(e + 1)], axis=1)
        both = []
        for t_ref, g_ref in ((own_t, own_g), (other_t, other_g)):
            from_t = jnp.dot(t_ref[...], w, preferred_element_type=F32)
            from_g = jnp.dot(g_ref[...], w, preferred_element_type=F32)
            both.append(jnp.where(lane_group(from_t.shape) % GROUPS < 3, from_t, from_g))
        for k in range(2):
            own, other = (b[:, 128 * k : 128 * (k + 1)] for b in both)
            odd = lane_group(own.shape) % 2 == 1
            chunk = chunk_of(plane, e + k)
            early = jnp.where(odd, own, turn(other, 96))
            late = jnp.where(odd, turn(other, 32), own)
            high = early.astype(BF16)
            low = early - high.astype(F32)
            low = jnp.where(
                lane_group((half // 2, 128)) < 2, low[: half // 2], turn(low[half // 2 :], 64)
            )
            out_ref[chunk, :half] = high
            out_ref[chunk, half : 2 * half] = late.astype(BF16)
            out_ref[chunk, 2 * half :] = low.astype(BF16)
            if e + k == 0:
                own_ref[:half] = early
                own_ref[half:] = late


def store_signal(x, sig):
    half = x.shape[0]
    product = x * turn(x, 64)
    turned = turn(product, 32)
    odd = lane_group(x.shape) % 2 == 1
    sig[:half] = jnp.where(odd, product, turned)
    sig[half:] = jnp.where(odd, turned, product)


def chunk_rows(core, q_half, step, rows):
    half = rows // 2
    start = half * core if q_half == 0 else half * (1 - core)
    return pl.ds(start + step, half // STEPS, stride=STEPS)


def first_body(
    at_ref, part_ref, own_ref, decay_ref, far_ref, x_ref, late_ref, left_ref, state_ref, sig, st
):
    core = at_ref[0]
    rows = sig.shape[0]
    half = rows // 2
    total = own_ref[...]
    low = jnp.zeros((half // 2, 128), F32)
    for e in range(1, part_ref.shape[0]):
        k = chunk_of(at_ref[1], e)
        total = total + part_ref[k, :rows].astype(F32)
        low = low + part_ref[k, rows:].astype(F32)
    low = jnp.concatenate([low, turn(low, 64)], axis=0)
    early = total[:half] + jnp.where(lane_group(low.shape) < 2, low, 0.0)
    x = jnp.where(lane_group(early.shape) < 2, early.astype(BF16).astype(F32), early)
    x_ref[...] = x
    late_ref[...] = total[half:].astype(BF16).astype(F32)
    store_signal(x, sig)
    decay = [decay_ref[m : m + 1, :] for m in range(MODE_ROWS)]
    chunks = rows // STEPS
    per = chunks // 2

    def step(i, held):
        t = STEPS - 1 - i
        g = [sig[chunk_rows(core, h, t, rows), :] for h in range(2)]
        return tuple(
            decay[m] * held[2 * m + h] + g[h] for m in range(MODE_ROWS) for h in range(2)
        )

    zero = jnp.zeros((per, 128), F32)
    held = lax.fori_loop(0, STEPS, step, (zero,) * (2 * MODE_ROWS), unroll=16)
    for m in range(MODE_ROWS):
        for h in range(2):
            st[m * chunks + h * per : m * chunks + (h + 1) * per, :] = held[2 * m + h]
    far = far_ref[...]
    acc = jnp.zeros((MODE_ROWS, 128), F32)
    for q in reversed(range(chunks)):
        where = pl.ds(q, MODE_ROWS, stride=chunks)
        left_ref[where, :] = acc
        acc = st[where, :] + far * acc
    state_ref[...] = jnp.broadcast_to(acc[None], state_ref.shape)


def second_body(
    at_ref, x_ref, late_ref, left_ref, states_ref, reach_ref, power_ref, decay_ref, weight_ref,
    conv_ref, out_ref, sig, ys,
):
    core = at_ref[0]
    rows = sig.shape[0]
    half = rows // 2
    chunks = rows // STEPS
    per = chunks // 2
    store_signal(x_ref[...], sig)
    carry = jnp.sum(states_ref[...] * reach_ref[...], axis=0)
    decay = [decay_ref[m : m + 1, :] for m in range(MODE_ROWS)]
    weight = [weight_ref[m : m + 1, :] for m in range(MODE_ROWS)]
    begin = []
    for m in range(MODE_ROWS):
        here = slice(m * chunks, (m + 1) * chunks)
        c = left_ref[here, :] + power_ref[here, :] * carry[m : m + 1, :]
        begin += [c[:per], c[per:]]

    def step(i, held):
        t = STEPS - 1 - i
        new = []
        for h in range(2):
            g = sig[chunk_rows(core, h, t, rows), :]
            states = [decay[m] * held[2 * m + h] + g for m in range(MODE_ROWS)]
            y = weight[0] * states[0]
            for m in range(1, MODE_ROWS):
                y = y + weight[m] * states[m]
            ys[chunk_rows(core, h, t, rows), :] = y
            new.append(states)
        return tuple(new[h][m] for m in range(MODE_ROWS) for h in range(2))

    lax.fori_loop(0, STEPS, step, tuple(begin), unroll=16)
    y = ys[...]
    y = y + turn(y, 64)
    y = y + turn(y, 32)
    odd = lane_group((half, 128)) % 2 == 1
    late = turn(late_ref[...], 64) * jnp.where(odd, y[half:], y[:half])
    early = x_ref[...] * conv_ref[...].astype(F32)
    own = jnp.where(odd, early, late)
    other = turn(jnp.where(odd, late, turn(early, 64)), 96)
    out = jnp.concatenate([own, other], axis=0).astype(BF16)
    for k in range(out_ref.shape[0]):
        out_ref[k] = out


def weigh_body(at_ref, tt_ref, gt_ref, grads_ref, out_ref):
    plane = at_ref[1]
    block = out_ref.shape[1]
    for l in range(2):
        r = l * block
        for c in range(0, grads_ref.shape[0], 2):
            g = jnp.concatenate([grads_ref[chunk_of(plane, c + k)] for k in range(2)], axis=1)
            from_t = jnp.dot(tt_ref[r : r + block, :], g, preferred_element_type=F32)
            from_g = jnp.dot(gt_ref[r : r + block, :], g, preferred_element_type=F32)
            both = jnp.where(lane_group(from_t.shape) % GROUPS != 1, from_t, from_g).astype(BF16)
            out_ref[holder(plane, c, l)] = both[:, :128]
            out_ref[holder(plane, c + 1, l)] = both[:, 128:]


def by_lanes(table):
    wide = jnp.repeat(table, 2, axis=1)
    channels = wide.shape[1]
    return wide.reshape(GROUPS, MODE_ROWS, channels).transpose(1, 0, 2).reshape(MODE_ROWS, -1)


def local(tokens, grad_out, in_weight, out_weight, conv_out, residues, decay_length):
    half = tokens.shape[0]
    depth = tokens.shape[1]
    rows = 2 * half
    owned = in_weight.shape[0]
    channels = out_weight.shape[1]
    size_z, size_y, size_x = (lax.axis_size(a) for a in ("seq_0", "seq_1", "chan"))
    chips = size_z * size_y
    core = lax.axis_index("seq_2")
    place = lax.axis_index(CHIPS)

    at = jnp.stack([core, lax.axis_index("chan")]).astype(jnp.int32)

    def transposed(value, to_owner):
        pairs = []
        for z in range(size_z):
            for x in range(size_x):
                j, l = z // 2, z % 2
                held = ((2 * j + OFFSETS[(x - j) % size_x][l]) % size_z) * size_x + j
                owner = z * size_x + x
                pairs.append((held, owner) if to_owner else (owner, held))
        return lax.ppermute(value, ("seq_0", "chan"), pairs)

    def swapped(value):
        return lax.ppermute(value, "seq_2", [(0, 1), (1, 0)])

    piece = call(pack_body, jax.ShapeDtypeStruct((2, owned, 128), BF16), 4)(
        in_hbm(in_weight.transpose(1, 0, 2)), in_hbm(out_weight)
    )
    piece = transposed(piece, False)
    spread = call(spread_body, jax.ShapeDtypeStruct((2 * chips, owned, 128), BF16), 4)(piece)
    weights = lax.all_to_all(spread, SEQ, 0, 0, tiled=True).reshape(size_z, -1, 128)

    tokens_too = swapped(tokens)
    grads_too = swapped(grad_out)
    conv = call(conv_body, jax.ShapeDtypeStruct((half, 128), BF16), 4, inputs=3)(
        at, conv_out, swapped(conv_out)
    )

    pick = residues.shape[1] // 2
    res = jnp.where(core == 0, residues[:, :pick], residues[:, pick:])
    length = jnp.where(core == 0, decay_length[:, :pick], decay_length[:, pick:])
    rate_raw = 1.0 / length
    weight = by_lanes(res * jnp.sqrt(-jnp.expm1(-2.0 * rate_raw)))
    rate = by_lanes(rate_raw)
    decay = jnp.exp(-rate)
    far = jnp.exp(-float(STEPS) * rate)
    chunks = rows // STEPS
    left_of = (chunks - 1 - jnp.arange(chunks)).astype(F32) * float(STEPS)
    power = jnp.exp(-left_of[None, :, None] * rate[:, None, :]).reshape(-1, 128)
    ahead = jnp.arange(chips) - place - 1
    reach = jnp.where(
        (ahead >= 0)[:, None, None],
        jnp.exp(-(jnp.maximum(ahead, 0) * rows).astype(F32)[:, None, None] * rate[None]),
        0.0,
    )

    weights, conv, weight, decay, far, power, reach = lax.optimization_barrier(
        (weights, conv, weight, decay, far, power, reach)
    )
    project = call(
        project_body,
        (jax.ShapeDtypeStruct((size_x, rows + half // 2, 128), BF16), jax.ShapeDtypeStruct((rows, 128), F32)),
        20,
        inputs=6,
        flops=4 * rows * depth * size_x * 128,
        moved=8 * rows * depth,
    )
    parts, own = project(
        at, tokens, in_hbm(tokens_too), grad_out, in_hbm(grads_too), weights
    )
    parts = lax.all_to_all(parts, "chan", 0, 0, tiled=True)

    first = call(
        first_body,
        (
            jax.ShapeDtypeStruct((half, 128), F32),
            jax.ShapeDtypeStruct((half, 128), F32),
            jax.ShapeDtypeStruct((MODE_ROWS * chunks, 128), F32),
            jax.ShapeDtypeStruct((chips, MODE_ROWS, 128), F32),
        ),
        10,
        scratch=[pltpu.VMEM((rows, 128), F32), pltpu.VMEM((MODE_ROWS * chunks, 128), F32)],
        inputs=5,
    )
    x, late, left, state = first(at, parts, own, decay, far)
    _, *turned = lax.optimization_barrier((left, tokens, tokens_too, grad_out, grads_too))
    turned = [in_hbm(t) for t in turned]
    flip = call(
        transpose_body, jax.ShapeDtypeStruct((depth, rows), BF16), 8, moved=4 * depth * rows
    )
    tokens_t = flip(*turned[:2])
    grads_t = flip(*turned[2:])
    states = lax.all_to_all(state, CHIPS, 0, 0, tiled=True)
    states, tokens_t, grads_t = lax.optimization_barrier((states, tokens_t, grads_t))
    second = call(
        second_body,
        jax.ShapeDtypeStruct((size_x, rows, 128), BF16),
        10,
        scratch=[pltpu.VMEM((rows, 128), F32), pltpu.VMEM((rows, 128), F32)],
        inputs=10,
    )
    grads = second(at, x, late, left, states, reach, power, decay, weight, conv)
    grads = lax.all_to_all(grads, "chan", 0, 0, tiled=True)

    weigh = call(
        weigh_body,
        jax.ShapeDtypeStruct((size_z, depth // 2, 128), BF16),
        16,
        inputs=4,
        flops=4 * rows * depth * size_x * 128,
        moved=8 * rows * depth,
    )
    partial = weigh(at, tokens_t, grads_t, grads).reshape(chips, 2 * owned, 128)
    partial = lax.all_to_all(partial, CHIPS, 0, 0, tiled=True)
    total = call(total_body, jax.ShapeDtypeStruct((2, owned, 128), F32), 6)(partial)
    total = lax.all_to_all(total, "seq_2", 0, 0, tiled=True)
    total = transposed(total, True)
    grad_in, grad_proj = call(
        unpack_body,
        (
            jax.ShapeDtypeStruct((3, owned, channels), F32),
            jax.ShapeDtypeStruct((owned, channels), F32),
        ),
        4,
    )(total)
    return (grad_in.transpose(1, 0, 2), grad_proj)


def solution(mesh):
    finer = Mesh(
        mesh.devices.reshape(8, 8, 2, mesh.shape["chan"]), ("seq_0", "seq_1", "seq_2", "chan")
    )
    in_specs = (
        P(SEQ, "chan"),
        P(SEQ, "chan"),
        P(SEQ, None, "chan"),
        P(SEQ, "chan"),
        P(SEQ, "chan"),
        P(None, "chan"),
        P(None, "chan"),
    )
    out_specs = (P(SEQ, None, "chan"), P(SEQ, "chan"))
    return jax.shard_map(local, mesh=finer, in_specs=in_specs, out_specs=out_specs, check_vma=False)
```

```python
import jax
import jax.numpy as jnp
from jax import lax
from jax.experimental import pallas as pl
from jax.experimental.pallas import tpu as pltpu
from jax.sharding import Mesh
from jax.sharding import PartitionSpec as P

SEQ = ("seq_0", "seq_1", "seq_2")
CHIPS = ("seq_0", "seq_1")
STEPS = 64
MODE_ROWS = 4
GROUPS = 4
F32 = jnp.float32
BF16 = jnp.bfloat16
MIB = 1024 * 1024

OFFSETS = ((5, 4), (2, 3), (0, 1), (6, 7))


def call(body, out_shape, mib, scratch=(), flops=0, moved=0, inputs=None):
    specs = {}
    if inputs is not None:
        specs["in_specs"] = [pl.BlockSpec(memory_space=pltpu.SMEM)] + [
            pl.BlockSpec(memory_space=pltpu.VMEM)
        ] * (inputs - 1)
    return pl.pallas_call(
        body,
        out_shape=out_shape,
        scratch_shapes=list(scratch),
        compiler_params=pltpu.CompilerParams(vmem_limit_bytes=mib * MIB),
        cost_estimate=pl.CostEstimate(flops=flops, bytes_accessed=moved, transcendentals=0),
        **specs,
    )


def holder(plane, e, l):
    return lax.rem(2 * plane + OFFSETS[e][l], 2 * len(OFFSETS))


def chunk_of(plane, e):
    return lax.rem(plane + e, len(OFFSETS))


def in_hbm(x):
    return pltpu.with_memory_space_constraint(x, pltpu.HBM)


def lane_group(shape):
    lane = lax.broadcasted_iota(jnp.int32, shape, len(shape) - 1)
    return lane // 32


def turn(x, by):
    return pltpu.roll(x, by, x.ndim - 1)


def transpose_body(a_ref, b_ref, out_ref):
    half = a_ref.shape[0]
    out_ref[:, :half] = a_ref[...].T
    out_ref[:, half:] = b_ref[...].T


def pack_body(in_ref, out_w_ref, out_ref):
    width = out_w_ref.shape[1]
    row = lax.broadcasted_iota(jnp.int32, (width, 128), 0)
    lane = lax.broadcasted_iota(jnp.int32, (width, 128), 1)
    streams = [in_ref[0], in_ref[1], in_ref[2], out_w_ref[...]]
    for half in range(2):
        total = jnp.zeros(out_ref.shape[1:], F32)
        for s, w in enumerate(streams):
            chosen = (lane // 32 == s) & (row == half * 32 + lane % 32)
            total = total + jnp.dot(w, chosen.astype(F32).astype(BF16), preferred_element_type=F32)
        out_ref[half] = total.astype(BF16)


def conv_body(at_ref, own_ref, other_ref, out_ref):
    core = at_ref[0]
    row = lax.broadcasted_iota(jnp.int32, (own_ref.shape[1], 128), 0)
    lane = lax.broadcasted_iota(jnp.int32, (own_ref.shape[1], 128), 1)
    total = jnp.zeros(out_ref.shape, F32)
    for odd, ref in ((1, own_ref), (0, other_ref)):
        chosen = (lane // 32 % 2 == odd) & (row == core * 32 + lane % 32)
        total = total + jnp.dot(
            ref[...], chosen.astype(F32).astype(BF16), preferred_element_type=F32
        )
    out_ref[...] = total.astype(BF16)


def spread_body(piece_ref, out_ref):
    for k in range(out_ref.shape[0]):
        out_ref[k] = piece_ref[k % 2]


def total_body(part_ref, out_ref):
    owned = out_ref.shape[1]
    total = part_ref[0].astype(F32)
    for k in range(1, part_ref.shape[0]):
        total = total + part_ref[k].astype(F32)
    out_ref[0] = total[:owned]
    out_ref[1] = total[owned:]


def unpack_body(part_ref, in_ref, out_w_ref):
    low = part_ref[0]
    high = part_ref[1]
    for s, group in enumerate((0, 3, 2, 1)):
        left = low if group == 0 else turn(low, 128 - 32 * group)
        right = high if group == 1 else turn(high, (160 - 32 * group) % 128)
        both = jnp.where(lane_group(low.shape) == 0, left, right)[:, : out_w_ref.shape[1]]
        if s < 3:
            in_ref[s] = both
        else:
            out_w_ref[...] = both


def project_body(at_ref, own_t, other_t, own_g, other_g, w_ref, out_ref, own_ref):
    plane = at_ref[1]
    half = own_t.shape[0]

    def columns(e):
        return jnp.concatenate([w_ref[holder(plane, e, l)] for l in range(2)], axis=0)

    for e in range(0, out_ref.shape[0], 2):
        w = jnp.concatenate([columns(e), columns(e + 1)], axis=1)
        both = []
        for t_ref, g_ref in ((own_t, own_g), (other_t, other_g)):
            from_t = jnp.dot(t_ref[...], w, preferred_element_type=F32)
            from_g = jnp.dot(g_ref[...], w, preferred_element_type=F32)
            both.append(jnp.where(lane_group(from_t.shape) % GROUPS < 3, from_t, from_g))
        for k in range(2):
            own, other = (b[:, 128 * k : 128 * (k + 1)] for b in both)
            odd = lane_group(own.shape) % 2 == 1
            chunk = chunk_of(plane, e + k)
            early = jnp.where(odd, own, turn(other, 96))
            late = jnp.where(odd, turn(other, 32), own)
            high = early.astype(BF16)
            low = early - high.astype(F32)
            low = jnp.where(
                lane_group((half // 2, 128)) < 2, low[: half // 2], turn(low[half // 2 :], 64)
            )
            out_ref[chunk, :half] = high
            out_ref[chunk, half : 2 * half] = late.astype(BF16)
            out_ref[chunk, 2 * half :] = low.astype(BF16)
            if e + k == 0:
                own_ref[:half] = early
                own_ref[half:] = late


def store_signal(x, sig):
    half = x.shape[0]
    product = x * turn(x, 64)
    turned = turn(product, 32)
    odd = lane_group(x.shape) % 2 == 1
    sig[:half] = jnp.where(odd, product, turned)
    sig[half:] = jnp.where(odd, turned, product)


def chunk_rows(core, q_half, step, rows):
    half = rows // 2
    start = half * core if q_half == 0 else half * (1 - core)
    return pl.ds(start + step, half // STEPS, stride=STEPS)


def first_body(
    at_ref, part_ref, own_ref, decay_ref, far_ref, x_ref, late_ref, left_ref, state_ref, sig, st
):
    core = at_ref[0]
    rows = sig.shape[0]
    half = rows // 2
    total = own_ref[...]
    low = jnp.zeros((half // 2, 128), F32)
    for e in range(1, part_ref.shape[0]):
        k = chunk_of(at_ref[1], e)
        total = total + part_ref[k, :rows].astype(F32)
        low = low + part_ref[k, rows:].astype(F32)
    low = jnp.concatenate([low, turn(low, 64)], axis=0)
    early = total[:half] + jnp.where(lane_group(low.shape) < 2, low, 0.0)
    x = jnp.where(lane_group(early.shape) < 2, early.astype(BF16).astype(F32), early)
    x_ref[...] = x
    late_ref[...] = total[half:].astype(BF16).astype(F32)
    store_signal(x, sig)
    decay = [decay_ref[m : m + 1, :] for m in range(MODE_ROWS)]
    chunks = rows // STEPS
    per = chunks // 2

    def step(i, held):
        t = STEPS - 1 - i
        g = [sig[chunk_rows(core, h, t, rows), :] for h in range(2)]
        return tuple(
            decay[m] * held[2 * m + h] + g[h] for m in range(MODE_ROWS) for h in range(2)
        )

    zero = jnp.zeros((per, 128), F32)
    held = lax.fori_loop(0, STEPS, step, (zero,) * (2 * MODE_ROWS), unroll=16)
    for m in range(MODE_ROWS):
        for h in range(2):
            st[m * chunks + h * per : m * chunks + (h + 1) * per, :] = held[2 * m + h]
    far = far_ref[...]
    acc = jnp.zeros((MODE_ROWS, 128), F32)
    for q in reversed(range(chunks)):
        where = pl.ds(q, MODE_ROWS, stride=chunks)
        left_ref[where, :] = acc
        acc = st[where, :] + far * acc
    state_ref[...] = jnp.broadcast_to(acc[None], state_ref.shape)


def second_body(
    at_ref, x_ref, late_ref, left_ref, states_ref, reach_ref, power_ref, decay_ref, weight_ref,
    conv_ref, out_ref, sig, ys,
):
    core = at_ref[0]
    rows = sig.shape[0]
    half = rows // 2
    chunks = rows // STEPS
    per = chunks // 2
    store_signal(x_ref[...], sig)
    carry = jnp.sum(states_ref[...] * reach_ref[...], axis=0)
    decay = [decay_ref[m : m + 1, :] for m in range(MODE_ROWS)]
    weight = [weight_ref[m : m + 1, :] for m in range(MODE_ROWS)]
    begin = []
    for m in range(MODE_ROWS):
        here = slice(m * chunks, (m + 1) * chunks)
        c = left_ref[here, :] + power_ref[here, :] * carry[m : m + 1, :]
        begin += [c[:per], c[per:]]

    def step(i, held):
        t = STEPS - 1 - i
        new = []
        for h in range(2):
            g = sig[chunk_rows(core, h, t, rows), :]
            states = [decay[m] * held[2 * m + h] + g for m in range(MODE_ROWS)]
            y = weight[0] * states[0]
            for m in range(1, MODE_ROWS):
                y = y + weight[m] * states[m]
            ys[chunk_rows(core, h, t, rows), :] = y
            new.append(states)
        return tuple(new[h][m] for m in range(MODE_ROWS) for h in range(2))

    lax.fori_loop(0, STEPS, step, tuple(begin), unroll=16)
    y = ys[...]
    y = y + turn(y, 64)
    y = y + turn(y, 32)
    odd = lane_group((half, 128)) % 2 == 1
    late = turn(late_ref[...], 64) * jnp.where(odd, y[half:], y[:half])
    early = x_ref[...] * conv_ref[...].astype(F32)
    own = jnp.where(odd, early, late)
    other = turn(jnp.where(odd, late, turn(early, 64)), 96)
    out = jnp.concatenate([own, other], axis=0).astype(BF16)
    for k in range(out_ref.shape[0]):
        out_ref[k] = out


def weigh_body(at_ref, tt_ref, gt_ref, grads_ref, out_ref):
    plane = at_ref[1]
    block = out_ref.shape[1]
    for e in range(0, grads_ref.shape[0], 2):
        g = jnp.concatenate([grads_ref[chunk_of(plane, e + k)] for k in range(2)], axis=1)
        for l in range(2):
            here = slice(l * block, (l + 1) * block)
            from_t = jnp.dot(tt_ref[here, :], g, preferred_element_type=F32)
            from_g = jnp.dot(gt_ref[here, :], g, preferred_element_type=F32)
            both = jnp.where(lane_group(from_t.shape) % GROUPS != 1, from_t, from_g).astype(BF16)
            out_ref[holder(plane, e, l)] = both[:, :128]
            out_ref[holder(plane, e + 1, l)] = both[:, 128:]


def by_lanes(table):
    wide = jnp.repeat(table, 2, axis=1)
    channels = wide.shape[1]
    return wide.reshape(GROUPS, MODE_ROWS, channels).transpose(1, 0, 2).reshape(MODE_ROWS, -1)


def local(tokens, grad_out, in_weight, out_weight, conv_out, residues, decay_length):
    half = tokens.shape[0]
    depth = tokens.shape[1]
    rows = 2 * half
    owned = in_weight.shape[0]
    channels = out_weight.shape[1]
    size_z, size_y, size_x = (lax.axis_size(a) for a in ("seq_0", "seq_1", "chan"))
    chips = size_z * size_y
    core = lax.axis_index("seq_2")
    place = lax.axis_index(CHIPS)

    at = jnp.stack([core, lax.axis_index("chan")]).astype(jnp.int32)

    def transposed(value, to_owner):
        pairs = []
        for z in range(size_z):
            for x in range(size_x):
                j, l = z // 2, z % 2
                held = ((2 * j + OFFSETS[(x - j) % size_x][l]) % size_z) * size_x + j
                owner = z * size_x + x
                pairs.append((held, owner) if to_owner else (owner, held))
        return lax.ppermute(value, ("seq_0", "chan"), pairs)

    def swapped(value):
        return lax.ppermute(value, "seq_2", [(0, 1), (1, 0)])

    piece = call(pack_body, jax.ShapeDtypeStruct((2, owned, 128), BF16), 4)(
        in_hbm(in_weight.transpose(1, 0, 2)), in_hbm(out_weight)
    )
    piece = transposed(piece, False)
    spread = call(spread_body, jax.ShapeDtypeStruct((2 * chips, owned, 128), BF16), 4)(piece)
    weights = lax.all_to_all(spread, SEQ, 0, 0, tiled=True).reshape(size_z, -1, 128)

    tokens_too = swapped(tokens)
    grads_too = swapped(grad_out)
    conv = call(conv_body, jax.ShapeDtypeStruct((half, 128), BF16), 4, inputs=3)(
        at, conv_out, swapped(conv_out)
    )

    pick = residues.shape[1] // 2
    res = jnp.where(core == 0, residues[:, :pick], residues[:, pick:])
    length = jnp.where(core == 0, decay_length[:, :pick], decay_length[:, pick:])
    rate_raw = 1.0 / length
    weight = by_lanes(res * jnp.sqrt(-jnp.expm1(-2.0 * rate_raw)))
    rate = by_lanes(rate_raw)
    decay = jnp.exp(-rate)
    far = jnp.exp(-float(STEPS) * rate)
    chunks = rows // STEPS
    left_of = (chunks - 1 - jnp.arange(chunks)).astype(F32) * float(STEPS)
    power = jnp.exp(-left_of[None, :, None] * rate[:, None, :]).reshape(-1, 128)
    ahead = jnp.arange(chips) - place - 1
    reach = jnp.where(
        (ahead >= 0)[:, None, None],
        jnp.exp(-(jnp.maximum(ahead, 0) * rows).astype(F32)[:, None, None] * rate[None]),
        0.0,
    )

    weights, conv, weight, decay, far, power, reach = lax.optimization_barrier(
        (weights, conv, weight, decay, far, power, reach)
    )
    project = call(
        project_body,
        (jax.ShapeDtypeStruct((size_x, rows + half // 2, 128), BF16), jax.ShapeDtypeStruct((rows, 128), F32)),
        20,
        inputs=6,
        flops=4 * rows * depth * size_x * 128,
        moved=8 * rows * depth,
    )
    parts, own = project(
        at, tokens, in_hbm(tokens_too), grad_out, in_hbm(grads_too), weights
    )
    parts = lax.all_to_all(parts, "chan", 0, 0, tiled=True)

    first = call(
        first_body,
        (
            jax.ShapeDtypeStruct((half, 128), F32),
            jax.ShapeDtypeStruct((half, 128), F32),
            jax.ShapeDtypeStruct((MODE_ROWS * chunks, 128), F32),
            jax.ShapeDtypeStruct((chips, MODE_ROWS, 128), F32),
        ),
        10,
        scratch=[pltpu.VMEM((rows, 128), F32), pltpu.VMEM((MODE_ROWS * chunks, 128), F32)],
        inputs=5,
    )
    x, late, left, state = first(at, parts, own, decay, far)
    _, *turned = lax.optimization_barrier((left, tokens, tokens_too, grad_out, grads_too))
    turned = [in_hbm(t) for t in turned]
    flip = call(
        transpose_body, jax.ShapeDtypeStruct((depth, rows), BF16), 8, moved=4 * depth * rows
    )
    tokens_t = flip(*turned[:2])
    grads_t = flip(*turned[2:])
    states = lax.all_to_all(state, CHIPS, 0, 0, tiled=True)
    states, tokens_t, grads_t = lax.optimization_barrier((states, tokens_t, grads_t))
    second = call(
        second_body,
        jax.ShapeDtypeStruct((size_x, rows, 128), BF16),
        10,
        scratch=[pltpu.VMEM((rows, 128), F32), pltpu.VMEM((rows, 128), F32)],
        inputs=10,
    )
    grads = second(at, x, late, left, states, reach, power, decay, weight, conv)
    grads = lax.all_to_all(grads, "chan", 0, 0, tiled=True)

    weigh = call(
        weigh_body,
        jax.ShapeDtypeStruct((size_z, depth // 2, 128), BF16),
        16,
        inputs=4,
        flops=4 * rows * depth * size_x * 128,
        moved=8 * rows * depth,
    )
    partial = weigh(at, tokens_t, grads_t, grads).reshape(chips, 2 * owned, 128)
    partial = lax.all_to_all(partial, CHIPS, 0, 0, tiled=True)
    total = call(total_body, jax.ShapeDtypeStruct((2, owned, 128), F32), 6)(partial)
    total = lax.all_to_all(total, "seq_2", 0, 0, tiled=True)
    total = transposed(total, True)
    grad_in, grad_proj = call(
        unpack_body,
        (
            jax.ShapeDtypeStruct((3, owned, channels), F32),
            jax.ShapeDtypeStruct((owned, channels), F32),
        ),
        4,
    )(total)
    return (grad_in.transpose(1, 0, 2), grad_proj)


def solution(mesh):
    finer = Mesh(
        mesh.devices.reshape(8, 8, 2, mesh.shape["chan"]), ("seq_0", "seq_1", "seq_2", "chan")
    )
    in_specs = (
        P(SEQ, "chan"),
        P(SEQ, "chan"),
        P(SEQ, None, "chan"),
        P(SEQ, "chan"),
        P(SEQ, "chan"),
        P(None, "chan"),
        P(None, "chan"),
    )
    out_specs = (P(SEQ, None, "chan"), P(SEQ, "chan"))
    return jax.shard_map(local, mesh=finer, in_specs=in_specs, out_specs=out_specs, check_vma=False)
```

```python
import jax
import jax.numpy as jnp
from jax import lax
from jax.experimental import pallas as pl
from jax.experimental.pallas import tpu as pltpu
from jax.sharding import Mesh
from jax.sharding import PartitionSpec as P

SEQ = ("seq_0", "seq_1", "seq_2")
CHIPS = ("seq_0", "seq_1")
STEPS = 32
MODE_ROWS = 4
GROUPS = 4
F32 = jnp.float32
BF16 = jnp.bfloat16
MIB = 1024 * 1024

OFFSETS = ((5, 4), (2, 3), (0, 1), (6, 7))


def call(body, out_shape, mib, scratch=(), flops=0, moved=0, inputs=None):
    specs = {}
    if inputs is not None:
        specs["in_specs"] = [pl.BlockSpec(memory_space=pltpu.SMEM)] + [
            pl.BlockSpec(memory_space=pltpu.VMEM)
        ] * (inputs - 1)
    return pl.pallas_call(
        body,
        out_shape=out_shape,
        scratch_shapes=list(scratch),
        compiler_params=pltpu.CompilerParams(vmem_limit_bytes=mib * MIB),
        cost_estimate=pl.CostEstimate(flops=flops, bytes_accessed=moved, transcendentals=0),
        **specs,
    )


def holder(plane, e, l):
    return lax.rem(2 * plane + OFFSETS[e][l], 2 * len(OFFSETS))


def chunk_of(plane, e):
    return lax.rem(plane + e, len(OFFSETS))


def in_hbm(x):
    return pltpu.with_memory_space_constraint(x, pltpu.HBM)


def lane_group(shape):
    lane = lax.broadcasted_iota(jnp.int32, shape, len(shape) - 1)
    return lane // 32


def turn(x, by):
    return pltpu.roll(x, by, x.ndim - 1)


def transpose_body(a_ref, b_ref, out_ref):
    half = a_ref.shape[0]
    out_ref[:, :half] = a_ref[...].T
    out_ref[:, half:] = b_ref[...].T


def pack_body(in_ref, out_w_ref, out_ref):
    width = out_w_ref.shape[1]
    row = lax.broadcasted_iota(jnp.int32, (width, 128), 0)
    lane = lax.broadcasted_iota(jnp.int32, (width, 128), 1)
    streams = [in_ref[0], in_ref[1], in_ref[2], out_w_ref[...]]
    for half in range(2):
        total = jnp.zeros(out_ref.shape[1:], F32)
        for s, w in enumerate(streams):
            chosen = (lane // 32 == s) & (row == half * 32 + lane % 32)
            total = total + jnp.dot(w, chosen.astype(F32).astype(BF16), preferred_element_type=F32)
        out_ref[half] = total.astype(BF16)


def conv_body(at_ref, own_ref, other_ref, out_ref):
    core = at_ref[0]
    row = lax.broadcasted_iota(jnp.int32, (own_ref.shape[1], 128), 0)
    lane = lax.broadcasted_iota(jnp.int32, (own_ref.shape[1], 128), 1)
    total = jnp.zeros(out_ref.shape, F32)
    for odd, ref in ((1, own_ref), (0, other_ref)):
        chosen = (lane // 32 % 2 == odd) & (row == core * 32 + lane % 32)
        total = total + jnp.dot(
            ref[...], chosen.astype(F32).astype(BF16), preferred_element_type=F32
        )
    out_ref[...] = total.astype(BF16)


def spread_body(piece_ref, out_ref):
    for k in range(out_ref.shape[0]):
        out_ref[k] = piece_ref[k % 2]


def total_body(part_ref, out_ref):
    owned = out_ref.shape[1]
    total = part_ref[0].astype(F32)
    for k in range(1, part_ref.shape[0]):
        total = total + part_ref[k].astype(F32)
    out_ref[0] = total[:owned]
    out_ref[1] = total[owned:]


def unpack_body(part_ref, in_ref, out_w_ref):
    low = part_ref[0]
    high = part_ref[1]
    for s, group in enumerate((0, 3, 2, 1)):
        left = low if group == 0 else turn(low, 128 - 32 * group)
        right = high if group == 1 else turn(high, (160 - 32 * group) % 128)
        both = jnp.where(lane_group(low.shape) == 0, left, right)[:, : out_w_ref.shape[1]]
        if s < 3:
            in_ref[s] = both
        else:
            out_w_ref[...] = both


def project_body(at_ref, own_t, other_t, own_g, other_g, w_ref, out_ref, own_ref):
    plane = at_ref[1]
    half = own_t.shape[0]

    def columns(e):
        return jnp.concatenate([w_ref[holder(plane, e, l)] for l in range(2)], axis=0)

    for e in range(0, out_ref.shape[0], 2):
        w = jnp.concatenate([columns(e), columns(e + 1)], axis=1)
        both = []
        for t_ref, g_ref in ((own_t, own_g), (other_t, other_g)):
            from_t = jnp.dot(t_ref[...], w, preferred_element_type=F32)
            from_g = jnp.dot(g_ref[...], w, preferred_element_type=F32)
            both.append(jnp.where(lane_group(from_t.shape) % GROUPS < 3, from_t, from_g))
        for k in range(2):
            own, other = (b[:, 128 * k : 128 * (k + 1)] for b in both)
            odd = lane_group(own.shape) % 2 == 1
            chunk = chunk_of(plane, e + k)
            early = jnp.where(odd, own, turn(other, 96))
            late = jnp.where(odd, turn(other, 32), own)
            high = early.astype(BF16)
            low = early - high.astype(F32)
            low = jnp.where(
                lane_group((half // 2, 128)) < 2, low[: half // 2], turn(low[half // 2 :], 64)
            )
            out_ref[chunk, :half] = high
            out_ref[chunk, half : 2 * half] = late.astype(BF16)
            out_ref[chunk, 2 * half :] = low.astype(BF16)
            if e + k == 0:
                own_ref[:half] = early
                own_ref[half:] = late


def store_signal(x, sig):
    half = x.shape[0]
    product = x * turn(x, 64)
    turned = turn(product, 32)
    odd = lane_group(x.shape) % 2 == 1
    sig[:half] = jnp.where(odd, product, turned)
    sig[half:] = jnp.where(odd, turned, product)


def chunk_rows(core, q_half, step, rows):
    half = rows // 2
    start = half * core if q_half == 0 else half * (1 - core)
    return pl.ds(start + step, half // STEPS, stride=STEPS)


def first_body(
    at_ref, part_ref, own_ref, decay_ref, far_ref, x_ref, late_ref, left_ref, state_ref, sig, st
):
    core = at_ref[0]
    rows = sig.shape[0]
    half = rows // 2
    total = own_ref[...]
    low = jnp.zeros((half // 2, 128), F32)
    for e in range(1, part_ref.shape[0]):
        k = chunk_of(at_ref[1], e)
        total = total + part_ref[k, :rows].astype(F32)
        low = low + part_ref[k, rows:].astype(F32)
    low = jnp.concatenate([low, turn(low, 64)], axis=0)
    early = total[:half] + jnp.where(lane_group(low.shape) < 2, low, 0.0)
    x = jnp.where(lane_group(early.shape) < 2, early.astype(BF16).astype(F32), early)
    x_ref[...] = x
    late_ref[...] = total[half:].astype(BF16).astype(F32)
    store_signal(x, sig)
    decay = [decay_ref[m : m + 1, :] for m in range(MODE_ROWS)]
    chunks = rows // STEPS
    per = chunks // 2

    def step(i, held):
        t = STEPS - 1 - i
        g = [sig[chunk_rows(core, h, t, rows), :] for h in range(2)]
        return tuple(
            decay[m] * held[2 * m + h] + g[h] for m in range(MODE_ROWS) for h in range(2)
        )

    zero = jnp.zeros((per, 128), F32)
    held = lax.fori_loop(0, STEPS, step, (zero,) * (2 * MODE_ROWS), unroll=16)
    for m in range(MODE_ROWS):
        for h in range(2):
            st[m * chunks + h * per : m * chunks + (h + 1) * per, :] = held[2 * m + h]
    far = far_ref[...]
    acc = jnp.zeros((MODE_ROWS, 128), F32)
    for q in reversed(range(chunks)):
        where = pl.ds(q, MODE_ROWS, stride=chunks)
        left_ref[where, :] = acc
        acc = st[where, :] + far * acc
    state_ref[...] = jnp.broadcast_to(acc[None], state_ref.shape)


def second_body(
    at_ref, x_ref, late_ref, left_ref, states_ref, reach_ref, power_ref, decay_ref, weight_ref,
    conv_ref, out_ref, sig, ys,
):
    core = at_ref[0]
    rows = sig.shape[0]
    half = rows // 2
    chunks = rows // STEPS
    per = chunks // 2
    store_signal(x_ref[...], sig)
    carry = jnp.sum(states_ref[...] * reach_ref[...], axis=0)
    decay = [decay_ref[m : m + 1, :] for m in range(MODE_ROWS)]
    weight = [weight_ref[m : m + 1, :] for m in range(MODE_ROWS)]
    begin = []
    for m in range(MODE_ROWS):
        here = slice(m * chunks, (m + 1) * chunks)
        c = left_ref[here, :] + power_ref[here, :] * carry[m : m + 1, :]
        begin += [c[:per], c[per:]]

    def step(i, held):
        t = STEPS - 1 - i
        new = []
        for h in range(2):
            g = sig[chunk_rows(core, h, t, rows), :]
            states = [decay[m] * held[2 * m + h] + g for m in range(MODE_ROWS)]
            y = weight[0] * states[0]
            for m in range(1, MODE_ROWS):
                y = y + weight[m] * states[m]
            ys[chunk_rows(core, h, t, rows), :] = y
            new.append(states)
        return tuple(new[h][m] for m in range(MODE_ROWS) for h in range(2))

    lax.fori_loop(0, STEPS, step, tuple(begin), unroll=16)
    y = ys[...]
    y = y + turn(y, 64)
    y = y + turn(y, 32)
    odd = lane_group((half, 128)) % 2 == 1
    late = turn(late_ref[...], 64) * jnp.where(odd, y[half:], y[:half])
    early = x_ref[...] * conv_ref[...].astype(F32)
    own = jnp.where(odd, early, late)
    other = turn(jnp.where(odd, late, turn(early, 64)), 96)
    out = jnp.concatenate([own, other], axis=0).astype(BF16)
    for k in range(out_ref.shape[0]):
        out_ref[k] = out


def weigh_body(at_ref, tt_ref, gt_ref, grads_ref, out_ref):
    plane = at_ref[1]
    block = out_ref.shape[1]
    for e in range(0, grads_ref.shape[0], 2):
        g = jnp.concatenate([grads_ref[chunk_of(plane, e + k)] for k in range(2)], axis=1)
        for l in range(2):
            here = slice(l * block, (l + 1) * block)
            from_t = jnp.dot(tt_ref[here, :], g, preferred_element_type=F32)
            from_g = jnp.dot(gt_ref[here, :], g, preferred_element_type=F32)
            both = jnp.where(lane_group(from_t.shape) % GROUPS != 1, from_t, from_g).astype(BF16)
            out_ref[holder(plane, e, l)] = both[:, :128]
            out_ref[holder(plane, e + 1, l)] = both[:, 128:]


def by_lanes(table):
    wide = jnp.repeat(table, 2, axis=1)
    channels = wide.shape[1]
    return wide.reshape(GROUPS, MODE_ROWS, channels).transpose(1, 0, 2).reshape(MODE_ROWS, -1)


def local(tokens, grad_out, in_weight, out_weight, conv_out, residues, decay_length):
    half = tokens.shape[0]
    depth = tokens.shape[1]
    rows = 2 * half
    owned = in_weight.shape[0]
    channels = out_weight.shape[1]
    size_z, size_y, size_x = (lax.axis_size(a) for a in ("seq_0", "seq_1", "chan"))
    chips = size_z * size_y
    core = lax.axis_index("seq_2")
    place = lax.axis_index(CHIPS)

    at = jnp.stack([core, lax.axis_index("chan")]).astype(jnp.int32)

    def transposed(value, to_owner):
        pairs = []
        for z in range(size_z):
            for x in range(size_x):
                j, l = z // 2, z % 2
                held = ((2 * j + OFFSETS[(x - j) % size_x][l]) % size_z) * size_x + j
                owner = z * size_x + x
                pairs.append((held, owner) if to_owner else (owner, held))
        return lax.ppermute(value, ("seq_0", "chan"), pairs)

    def swapped(value):
        return lax.ppermute(value, "seq_2", [(0, 1), (1, 0)])

    piece = call(pack_body, jax.ShapeDtypeStruct((2, owned, 128), BF16), 4)(
        in_hbm(in_weight.transpose(1, 0, 2)), in_hbm(out_weight)
    )
    piece = transposed(piece, False)
    spread = call(spread_body, jax.ShapeDtypeStruct((2 * chips, owned, 128), BF16), 4)(piece)
    weights = lax.all_to_all(spread, SEQ, 0, 0, tiled=True).reshape(size_z, -1, 128)

    tokens_too = swapped(tokens)
    grads_too = swapped(grad_out)
    conv = call(conv_body, jax.ShapeDtypeStruct((half, 128), BF16), 4, inputs=3)(
        at, conv_out, swapped(conv_out)
    )

    pick = residues.shape[1] // 2
    res = jnp.where(core == 0, residues[:, :pick], residues[:, pick:])
    length = jnp.where(core == 0, decay_length[:, :pick], decay_length[:, pick:])
    rate_raw = 1.0 / length
    weight = by_lanes(res * jnp.sqrt(-jnp.expm1(-2.0 * rate_raw)))
    rate = by_lanes(rate_raw)
    decay = jnp.exp(-rate)
    far = jnp.exp(-float(STEPS) * rate)
    chunks = rows // STEPS
    left_of = (chunks - 1 - jnp.arange(chunks)).astype(F32) * float(STEPS)
    power = jnp.exp(-left_of[None, :, None] * rate[:, None, :]).reshape(-1, 128)
    ahead = jnp.arange(chips) - place - 1
    reach = jnp.where(
        (ahead >= 0)[:, None, None],
        jnp.exp(-(jnp.maximum(ahead, 0) * rows).astype(F32)[:, None, None] * rate[None]),
        0.0,
    )

    weights, conv, weight, decay, far, power, reach = lax.optimization_barrier(
        (weights, conv, weight, decay, far, power, reach)
    )
    project = call(
        project_body,
        (jax.ShapeDtypeStruct((size_x, rows + half // 2, 128), BF16), jax.ShapeDtypeStruct((rows, 128), F32)),
        20,
        inputs=6,
        flops=4 * rows * depth * size_x * 128,
        moved=8 * rows * depth,
    )
    parts, own = project(
        at, tokens, in_hbm(tokens_too), grad_out, in_hbm(grads_too), weights
    )
    parts = lax.all_to_all(parts, "chan", 0, 0, tiled=True)

    first = call(
        first_body,
        (
            jax.ShapeDtypeStruct((half, 128), F32),
            jax.ShapeDtypeStruct((half, 128), F32),
            jax.ShapeDtypeStruct((MODE_ROWS * chunks, 128), F32),
            jax.ShapeDtypeStruct((chips, MODE_ROWS, 128), F32),
        ),
        10,
        scratch=[pltpu.VMEM((rows, 128), F32), pltpu.VMEM((MODE_ROWS * chunks, 128), F32)],
        inputs=5,
    )
    x, late, left, state = first(at, parts, own, decay, far)
    _, *turned = lax.optimization_barrier((left, tokens, tokens_too, grad_out, grads_too))
    turned = [in_hbm(t) for t in turned]
    flip = call(
        transpose_body, jax.ShapeDtypeStruct((depth, rows), BF16), 8, moved=4 * depth * rows
    )
    tokens_t = flip(*turned[:2])
    grads_t = flip(*turned[2:])
    states = lax.all_to_all(state, CHIPS, 0, 0, tiled=True)
    states, tokens_t, grads_t = lax.optimization_barrier((states, tokens_t, grads_t))
    second = call(
        second_body,
        jax.ShapeDtypeStruct((size_x, rows, 128), BF16),
        10,
        scratch=[pltpu.VMEM((rows, 128), F32), pltpu.VMEM((rows, 128), F32)],
        inputs=10,
    )
    grads = second(at, x, late, left, states, reach, power, decay, weight, conv)
    grads = lax.all_to_all(grads, "chan", 0, 0, tiled=True)

    weigh = call(
        weigh_body,
        jax.ShapeDtypeStruct((size_z, depth // 2, 128), BF16),
        16,
        inputs=4,
        flops=4 * rows * depth * size_x * 128,
        moved=8 * rows * depth,
    )
    partial = weigh(at, tokens_t, grads_t, grads).reshape(chips, 2 * owned, 128)
    partial = lax.all_to_all(partial, CHIPS, 0, 0, tiled=True)
    total = call(total_body, jax.ShapeDtypeStruct((2, owned, 128), F32), 6)(partial)
    total = lax.all_to_all(total, "seq_2", 0, 0, tiled=True)
    total = transposed(total, True)
    grad_in, grad_proj = call(
        unpack_body,
        (
            jax.ShapeDtypeStruct((3, owned, channels), F32),
            jax.ShapeDtypeStruct((owned, channels), F32),
        ),
        4,
    )(total)
    return (grad_in.transpose(1, 0, 2), grad_proj)


def solution(mesh):
    finer = Mesh(
        mesh.devices.reshape(8, 8, 2, mesh.shape["chan"]), ("seq_0", "seq_1", "seq_2", "chan")
    )
    in_specs = (
        P(SEQ, "chan"),
        P(SEQ, "chan"),
        P(SEQ, None, "chan"),
        P(SEQ, "chan"),
        P(SEQ, "chan"),
        P(None, "chan"),
        P(None, "chan"),
    )
    out_specs = (P(SEQ, None, "chan"), P(SEQ, "chan"))
    return jax.shard_map(local, mesh=finer, in_specs=in_specs, out_specs=out_specs, check_vma=False)
```

```python
import jax
import jax.numpy as jnp
from jax import lax
from jax.experimental import pallas as pl
from jax.experimental.pallas import tpu as pltpu
from jax.sharding import Mesh
from jax.sharding import PartitionSpec as P

SEQ = ("seq_0", "seq_1", "seq_2")
CHIPS = ("seq_0", "seq_1")
STEPS = 32
MODE_ROWS = 4
GROUPS = 4
F32 = jnp.float32
BF16 = jnp.bfloat16
MIB = 1024 * 1024

OFFSETS = ((5, 4), (2, 3), (0, 1), (6, 7))


def call(body, out_shape, mib, scratch=(), flops=0, moved=0, inputs=None):
    specs = {}
    if inputs is not None:
        specs["in_specs"] = [pl.BlockSpec(memory_space=pltpu.SMEM)] + [
            pl.BlockSpec(memory_space=pltpu.VMEM)
        ] * (inputs - 1)
    return pl.pallas_call(
        body,
        out_shape=out_shape,
        scratch_shapes=list(scratch),
        compiler_params=pltpu.CompilerParams(vmem_limit_bytes=mib * MIB),
        cost_estimate=pl.CostEstimate(flops=flops, bytes_accessed=moved, transcendentals=0),
        **specs,
    )


def holder(plane, e, l):
    return lax.rem(2 * plane + OFFSETS[e][l], 2 * len(OFFSETS))


def chunk_of(plane, e):
    return lax.rem(plane + e, len(OFFSETS))


def in_hbm(x):
    return pltpu.with_memory_space_constraint(x, pltpu.HBM)


def lane_group(shape):
    lane = lax.broadcasted_iota(jnp.int32, shape, len(shape) - 1)
    return lane // 32


def turn(x, by):
    return pltpu.roll(x, by, x.ndim - 1)


def transpose_body(a_ref, b_ref, out_ref):
    half = a_ref.shape[0]
    out_ref[:, :half] = a_ref[...].T
    out_ref[:, half:] = b_ref[...].T


def pack_body(in_ref, out_w_ref, out_ref):
    width = out_w_ref.shape[1]
    row = lax.broadcasted_iota(jnp.int32, (width, 128), 0)
    lane = lax.broadcasted_iota(jnp.int32, (width, 128), 1)
    streams = [in_ref[0], in_ref[1], in_ref[2], out_w_ref[...]]
    for half in range(2):
        total = jnp.zeros(out_ref.shape[1:], F32)
        for s, w in enumerate(streams):
            chosen = (lane // 32 == s) & (row == half * 32 + lane % 32)
            total = total + jnp.dot(w, chosen.astype(F32).astype(BF16), preferred_element_type=F32)
        out_ref[half] = total.astype(BF16)


def conv_body(at_ref, own_ref, other_ref, out_ref):
    core = at_ref[0]
    row = lax.broadcasted_iota(jnp.int32, (own_ref.shape[1], 128), 0)
    lane = lax.broadcasted_iota(jnp.int32, (own_ref.shape[1], 128), 1)
    total = jnp.zeros(out_ref.shape, F32)
    for odd, ref in ((1, own_ref), (0, other_ref)):
        chosen = (lane // 32 % 2 == odd) & (row == core * 32 + lane % 32)
        total = total + jnp.dot(
            ref[...], chosen.astype(F32).astype(BF16), preferred_element_type=F32
        )
    out_ref[...] = total.astype(BF16)


def spread_body(piece_ref, out_ref):
    for k in range(out_ref.shape[0]):
        out_ref[k] = piece_ref[k % 2]


def total_body(part_ref, out_ref):
    owned = out_ref.shape[1]
    total = part_ref[0].astype(F32)
    for k in range(1, part_ref.shape[0]):
        total = total + part_ref[k].astype(F32)
    out_ref[0] = total[:owned]
    out_ref[1] = total[owned:]


def unpack_body(part_ref, in_ref, out_w_ref):
    low = part_ref[0]
    high = part_ref[1]
    for s, group in enumerate((0, 3, 2, 1)):
        left = low if group == 0 else turn(low, 128 - 32 * group)
        right = high if group == 1 else turn(high, (160 - 32 * group) % 128)
        both = jnp.where(lane_group(low.shape) == 0, left, right)[:, : out_w_ref.shape[1]]
        if s < 3:
            in_ref[s] = both
        else:
            out_w_ref[...] = both


def project_body(at_ref, own_t, other_t, own_g, other_g, w_ref, out_ref, own_ref):
    plane = at_ref[1]
    half = own_t.shape[0]

    def columns(e):
        return jnp.concatenate([w_ref[holder(plane, e, l)] for l in range(2)], axis=0)

    for e in range(0, out_ref.shape[0], 2):
        w = jnp.concatenate([columns(e), columns(e + 1)], axis=1)
        both = []
        for t_ref, g_ref in ((own_t, own_g), (other_t, other_g)):
            from_t = jnp.dot(t_ref[...], w, preferred_element_type=F32)
            from_g = jnp.dot(g_ref[...], w, preferred_element_type=F32)
            both.append(jnp.where(lane_group(from_t.shape) % GROUPS < 3, from_t, from_g))
        for k in range(2):
            own, other = (b[:, 128 * k : 128 * (k + 1)] for b in both)
            odd = lane_group(own.shape) % 2 == 1
            chunk = chunk_of(plane, e + k)
            early = jnp.where(odd, own, turn(other, 96))
            late = jnp.where(odd, turn(other, 32), own)
            high = early.astype(BF16)
            low = early - high.astype(F32)
            low = jnp.where(
                lane_group((half // 2, 128)) < 2, low[: half // 2], turn(low[half // 2 :], 64)
            )
            out_ref[chunk, :half] = high
            out_ref[chunk, half : 2 * half] = late.astype(BF16)
            out_ref[chunk, 2 * half :] = low.astype(BF16)
            if e + k == 0:
                own_ref[:half] = early
                own_ref[half:] = late


def store_signal(x, sig):
    half = x.shape[0]
    product = x * turn(x, 64)
    turned = turn(product, 32)
    odd = lane_group(x.shape) % 2 == 1
    sig[:half] = jnp.where(odd, product, turned)
    sig[half:] = jnp.where(odd, turned, product)


def chunk_rows(core, q_half, step, rows):
    half = rows // 2
    start = half * core if q_half == 0 else half * (1 - core)
    return pl.ds(start + step, half // STEPS, stride=STEPS)


def first_body(
    at_ref, part_ref, own_ref, decay_ref, far_ref, x_ref, late_ref, left_ref, state_ref, sig, st
):
    core = at_ref[0]
    rows = sig.shape[0]
    half = rows // 2
    total = own_ref[...]
    low = jnp.zeros((half // 2, 128), F32)
    for e in range(1, part_ref.shape[0]):
        k = chunk_of(at_ref[1], e)
        total = total + part_ref[k, :rows].astype(F32)
        low = low + part_ref[k, rows:].astype(F32)
    low = jnp.concatenate([low, turn(low, 64)], axis=0)
    early = total[:half] + jnp.where(lane_group(low.shape) < 2, low, 0.0)
    x = jnp.where(lane_group(early.shape) < 2, early.astype(BF16).astype(F32), early)
    x_ref[...] = x
    late_ref[...] = total[half:].astype(BF16).astype(F32)
    store_signal(x, sig)
    decay = [decay_ref[m : m + 1, :] for m in range(MODE_ROWS)]
    chunks = rows // STEPS
    per = chunks // 2

    def step(i, held):
        t = STEPS - 1 - i
        g = [sig[chunk_rows(core, h, t, rows), :] for h in range(2)]
        return tuple(
            decay[m] * held[2 * m + h] + g[h] for m in range(MODE_ROWS) for h in range(2)
        )

    zero = jnp.zeros((per, 128), F32)
    held = lax.fori_loop(0, STEPS, step, (zero,) * (2 * MODE_ROWS), unroll=8)
    for m in range(MODE_ROWS):
        for h in range(2):
            st[m * chunks + h * per : m * chunks + (h + 1) * per, :] = held[2 * m + h]
    far = far_ref[...]
    acc = jnp.zeros((MODE_ROWS, 128), F32)
    for q in reversed(range(chunks)):
        where = pl.ds(q, MODE_ROWS, stride=chunks)
        left_ref[where, :] = acc
        acc = st[where, :] + far * acc
    state_ref[...] = jnp.broadcast_to(acc[None], state_ref.shape)


def second_body(
    at_ref, x_ref, late_ref, left_ref, states_ref, reach_ref, power_ref, decay_ref, weight_ref,
    conv_ref, out_ref, sig, ys,
):
    core = at_ref[0]
    rows = sig.shape[0]
    half = rows // 2
    chunks = rows // STEPS
    per = chunks // 2
    store_signal(x_ref[...], sig)
    carry = jnp.sum(states_ref[...] * reach_ref[...], axis=0)
    decay = [decay_ref[m : m + 1, :] for m in range(MODE_ROWS)]
    weight = [weight_ref[m : m + 1, :] for m in range(MODE_ROWS)]
    begin = []
    for m in range(MODE_ROWS):
        here = slice(m * chunks, (m + 1) * chunks)
        c = left_ref[here, :] + power_ref[here, :] * carry[m : m + 1, :]
        begin += [c[:per], c[per:]]

    def step(i, held):
        t = STEPS - 1 - i
        new = []
        for h in range(2):
            g = sig[chunk_rows(core, h, t, rows), :]
            states = [decay[m] * held[2 * m + h] + g for m in range(MODE_ROWS)]
            y = weight[0] * states[0]
            for m in range(1, MODE_ROWS):
                y = y + weight[m] * states[m]
            ys[chunk_rows(core, h, t, rows), :] = y
            new.append(states)
        return tuple(new[h][m] for m in range(MODE_ROWS) for h in range(2))

    lax.fori_loop(0, STEPS, step, tuple(begin), unroll=8)
    y = ys[...]
    y = y + turn(y, 64)
    y = y + turn(y, 32)
    odd = lane_group((half, 128)) % 2 == 1
    late = turn(late_ref[...], 64) * jnp.where(odd, y[half:], y[:half])
    early = x_ref[...] * conv_ref[...].astype(F32)
    own = jnp.where(odd, early, late)
    other = turn(jnp.where(odd, late, turn(early, 64)), 96)
    out = jnp.concatenate([own, other], axis=0).astype(BF16)
    for k in range(out_ref.shape[0]):
        out_ref[k] = out


def weigh_body(at_ref, tt_ref, gt_ref, grads_ref, out_ref):
    plane = at_ref[1]
    block = out_ref.shape[1]
    for e in range(0, grads_ref.shape[0], 2):
        g = jnp.concatenate([grads_ref[chunk_of(plane, e + k)] for k in range(2)], axis=1)
        for l in range(2):
            here = slice(l * block, (l + 1) * block)
            from_t = jnp.dot(tt_ref[here, :], g, preferred_element_type=F32)
            from_g = jnp.dot(gt_ref[here, :], g, preferred_element_type=F32)
            both = jnp.where(lane_group(from_t.shape) % GROUPS != 1, from_t, from_g).astype(BF16)
            out_ref[holder(plane, e, l)] = both[:, :128]
            out_ref[holder(plane, e + 1, l)] = both[:, 128:]


def by_lanes(table):
    wide = jnp.repeat(table, 2, axis=1)
    channels = wide.shape[1]
    return wide.reshape(GROUPS, MODE_ROWS, channels).transpose(1, 0, 2).reshape(MODE_ROWS, -1)


def local(tokens, grad_out, in_weight, out_weight, conv_out, residues, decay_length):
    half = tokens.shape[0]
    depth = tokens.shape[1]
    rows = 2 * half
    owned = in_weight.shape[0]
    channels = out_weight.shape[1]
    size_z, size_y, size_x = (lax.axis_size(a) for a in ("seq_0", "seq_1", "chan"))
    chips = size_z * size_y
    core = lax.axis_index("seq_2")
    place = lax.axis_index(CHIPS)

    at = jnp.stack([core, lax.axis_index("chan")]).astype(jnp.int32)

    def transposed(value, to_owner):
        pairs = []
        for z in range(size_z):
            for x in range(size_x):
                j, l = z // 2, z % 2
                held = ((2 * j + OFFSETS[(x - j) % size_x][l]) % size_z) * size_x + j
                owner = z * size_x + x
                pairs.append((held, owner) if to_owner else (owner, held))
        return lax.ppermute(value, ("seq_0", "chan"), pairs)

    def swapped(value):
        return lax.ppermute(value, "seq_2", [(0, 1), (1, 0)])

    piece = call(pack_body, jax.ShapeDtypeStruct((2, owned, 128), BF16), 4)(
        in_hbm(in_weight.transpose(1, 0, 2)), in_hbm(out_weight)
    )
    piece = transposed(piece, False)
    spread = call(spread_body, jax.ShapeDtypeStruct((2 * chips, owned, 128), BF16), 4)(piece)
    weights = lax.all_to_all(spread, SEQ, 0, 0, tiled=True).reshape(size_z, -1, 128)

    tokens_too = swapped(tokens)
    grads_too = swapped(grad_out)
    conv = call(conv_body, jax.ShapeDtypeStruct((half, 128), BF16), 4, inputs=3)(
        at, conv_out, swapped(conv_out)
    )

    pick = residues.shape[1] // 2
    res = jnp.where(core == 0, residues[:, :pick], residues[:, pick:])
    length = jnp.where(core == 0, decay_length[:, :pick], decay_length[:, pick:])
    rate_raw = 1.0 / length
    weight = by_lanes(res * jnp.sqrt(-jnp.expm1(-2.0 * rate_raw)))
    rate = by_lanes(rate_raw)
    decay = jnp.exp(-rate)
    far = jnp.exp(-float(STEPS) * rate)
    chunks = rows // STEPS
    left_of = (chunks - 1 - jnp.arange(chunks)).astype(F32) * float(STEPS)
    power = jnp.exp(-left_of[None, :, None] * rate[:, None, :]).reshape(-1, 128)
    ahead = jnp.arange(chips) - place - 1
    reach = jnp.where(
        (ahead >= 0)[:, None, None],
        jnp.exp(-(jnp.maximum(ahead, 0) * rows).astype(F32)[:, None, None] * rate[None]),
        0.0,
    )

    weights, conv, weight, decay, far, power, reach = lax.optimization_barrier(
        (weights, conv, weight, decay, far, power, reach)
    )
    project = call(
        project_body,
        (jax.ShapeDtypeStruct((size_x, rows + half // 2, 128), BF16), jax.ShapeDtypeStruct((rows, 128), F32)),
        20,
        inputs=6,
        flops=4 * rows * depth * size_x * 128,
        moved=8 * rows * depth,
    )
    parts, own = project(
        at, tokens, in_hbm(tokens_too), grad_out, in_hbm(grads_too), weights
    )
    parts = lax.all_to_all(parts, "chan", 0, 0, tiled=True)

    first = call(
        first_body,
        (
            jax.ShapeDtypeStruct((half, 128), F32),
            jax.ShapeDtypeStruct((half, 128), F32),
            jax.ShapeDtypeStruct((MODE_ROWS * chunks, 128), F32),
            jax.ShapeDtypeStruct((chips, MODE_ROWS, 128), F32),
        ),
        10,
        scratch=[pltpu.VMEM((rows, 128), F32), pltpu.VMEM((MODE_ROWS * chunks, 128), F32)],
        inputs=5,
    )
    x, late, left, state = first(at, parts, own, decay, far)
    _, *turned = lax.optimization_barrier((left, tokens, tokens_too, grad_out, grads_too))
    turned = [in_hbm(t) for t in turned]
    flip = call(
        transpose_body, jax.ShapeDtypeStruct((depth, rows), BF16), 8, moved=4 * depth * rows
    )
    tokens_t = flip(*turned[:2])
    grads_t = flip(*turned[2:])
    states = lax.all_to_all(state, CHIPS, 0, 0, tiled=True)
    states, tokens_t, grads_t = lax.optimization_barrier((states, tokens_t, grads_t))
    second = call(
        second_body,
        jax.ShapeDtypeStruct((size_x, rows, 128), BF16),
        10,
        scratch=[pltpu.VMEM((rows, 128), F32), pltpu.VMEM((rows, 128), F32)],
        inputs=10,
    )
    grads = second(at, x, late, left, states, reach, power, decay, weight, conv)
    grads = lax.all_to_all(grads, "chan", 0, 0, tiled=True)

    weigh = call(
        weigh_body,
        jax.ShapeDtypeStruct((size_z, depth // 2, 128), BF16),
        16,
        inputs=4,
        flops=4 * rows * depth * size_x * 128,
        moved=8 * rows * depth,
    )
    partial = weigh(at, tokens_t, grads_t, grads).reshape(chips, 2 * owned, 128)
    partial = lax.all_to_all(partial, CHIPS, 0, 0, tiled=True)
    total = call(total_body, jax.ShapeDtypeStruct((2, owned, 128), F32), 6)(partial)
    total = lax.all_to_all(total, "seq_2", 0, 0, tiled=True)
    total = transposed(total, True)
    grad_in, grad_proj = call(
        unpack_body,
        (
            jax.ShapeDtypeStruct((3, owned, channels), F32),
            jax.ShapeDtypeStruct((owned, channels), F32),
        ),
        4,
    )(total)
    return (grad_in.transpose(1, 0, 2), grad_proj)


def solution(mesh):
    finer = Mesh(
        mesh.devices.reshape(8, 8, 2, mesh.shape["chan"]), ("seq_0", "seq_1", "seq_2", "chan")
    )
    in_specs = (
        P(SEQ, "chan"),
        P(SEQ, "chan"),
        P(SEQ, None, "chan"),
        P(SEQ, "chan"),
        P(SEQ, "chan"),
        P(None, "chan"),
        P(None, "chan"),
    )
    out_specs = (P(SEQ, None, "chan"), P(SEQ, "chan"))
    return jax.shard_map(local, mesh=finer, in_specs=in_specs, out_specs=out_specs, check_vma=False)
```
